128 devices in a mesh: nodes: 128 (over z, y, x, core).
Axes of the slice: x: 4, y: 4, z: 4, core: 2. Of those that a mesh axis runs over, the one named last changes fastest.
Arguments:
- ctrl_points: float32 [3, 4194304], P(None, 'nodes'), may hold values from 0 to 128, as said below
- ctrl_disp: float32 [3, 4194304], P(None, 'nodes'), may hold values from -16 to 16
- stiffness: float32 [4194304], P('nodes'), may hold values from 0.3 to 1
- pair_rows: int32 [98304], P('nodes'), may hold values from 0 to 255, as said below
- pair_cols: int32 [98304], P('nodes'), may hold values from 1 to 511, as said below
- pair_count: int32 [128], P('nodes'), may hold values from 256 to 768, as said below
- vol_points: float32 [3, 4194304], P(None, 'nodes'), may hold values from 0 to 128, as said below
- vol_rows: int32 [65536], P('nodes'), may hold values from 0 to 255, as said below
- vol_cols: int32 [65536], P('nodes'), may hold values from 0 to 1279, as said below
- vol_count: int32 [128], P('nodes'), may hold values from 170 to 512, as said below
Outputs:
- coefficients: float32 [3, 4194304], P(None, 'nodes')
- moved: float32 [3, 4194304], P(None, 'nodes')
The draws below stay inside these ranges and needn't reach their ends.
Inputs may be any that keep to these rules, and one draw needn't show every extreme that they name: `ctrl_points`: control block b of device d lies in the box [d, d + 1) x [2 (b // 16), 2 (b // 16) + 2) x [2 (b % 16), 2 (b % 16) + 2). `pair_rows`: A block of the device's own 256 control blocks. Below 256: an own block greater than the tile's row block; from 256 on: block pair_cols - 256 of the next device. The 768 listed pairs of one device are distinct. Only the first pair_count entries of a device's list are live; some device has all 768 live. `vol_points`: volume block b of device d lies in the box of control block b % 256 of device d. `vol_rows`: A block of the device's own 256 volume blocks. Names control block vol_cols % 256 of device d + vol_cols // 256 - 2. The 512 listed pairs of one device are distinct. Only the first vol_count entries of a device's list are live; some device has all 512 live.
All inputs are finite; a program needn't handle non-finite values.
Results may differ from the reference program's by a relative error of at most 0.0003.
Values sent between devices are 32-bit elements; how exact they have to be, the bound alone decides.
No kernel may reach another device: no remote copies, remote signals or barrier semaphores. Data moves between devices by JAX's collectives and lax.ppermute only.
A program may use at most 64 MiB of HBM per device.

```python
import math
import jax
import jax.numpy as jnp
from jax import lax

TILE = 128
SIDE = 16
CB = 256
VB = 256
ITERS = 3
MAXT = 768
MAXV = 512
NC = 4194304
NV = 4194304


def box_points(key, device_count, per_device, exponent):
    unit_cube = jax.random.uniform(key, (3, device_count * per_device), jnp.float32)
    unit_cube = unit_cube ** exponent
    node_ids = jnp.arange(device_count * per_device, dtype=jnp.int32)
    device_pos = (node_ids // per_device).astype(jnp.float32)
    cell_ids = node_ids % per_device // TILE % CB
    first_cell = (cell_ids // SIDE).astype(jnp.float32)
    second_cell = (cell_ids % SIDE).astype(jnp.float32)
    return jnp.stack([unit_cube[0] + device_pos, 2.0 * (unit_cube[1] + first_cell), 2.0 * (unit_cube[2] + second_cell)], axis=0)


def cell_reach(first_block, second_block):
    first_gap = jnp.abs(first_block // SIDE - second_block // SIDE)
    second_gap = jnp.abs(first_block % SIDE - second_block % SIDE)
    return jnp.maximum(first_gap, second_gap)


def draw_ctrl_points(key, part):
    key = jax.random.fold_in(key, 11)
    exponent = 1.0
    return box_points(key, NC // (CB * TILE), CB * TILE, exponent)


def draw_vol_points(key, part):
    key = jax.random.fold_in(key, 12)
    exponent = 1.0
    return box_points(key, NV // (VB * TILE), VB * TILE, exponent)


def draw_ctrl_disp(key, part):
    key = jax.random.fold_in(key, 13)
    device_count = NC // (CB * TILE)
    device_pos = (jnp.arange(NC) // (CB * TILE)).astype(jnp.float32)
    growth = jnp.exp(jnp.log(3.0) * device_pos / max(device_count - 1, 1))
    values = jax.random.truncated_normal(key, -4.0, 4.0, (3, NC), jnp.float32)
    return values * growth


def pair_lists(key):
    device_count = NC // (CB * TILE)
    candidate = jnp.arange(2 * CB * CB, dtype=jnp.int32)
    is_right = candidate < CB * CB
    local_pair = candidate - CB * CB
    row_block = jnp.where(is_right, candidate // CB, local_pair // CB)
    col_block = jnp.where(is_right, CB + candidate % CB, local_pair % CB)
    usable = (is_right | (row_block < col_block)) & (cell_reach(row_block, col_block % CB) <= 1)
    device_keys = jax.random.split(jax.random.fold_in(key, 1), device_count)

    def per_device(dev_key):
        shuffled = jax.random.permutation(dev_key, 2 * CB * CB).astype(jnp.int32)
        scores = jnp.where(usable, shuffled, -1)
        unused, chosen = lax.top_k(scores, MAXT)
        return (row_block[chosen], col_block[chosen])
    row_lists, col_lists = jax.vmap(per_device)(device_keys)
    live = jax.random.randint(jax.random.fold_in(key, 2), (device_count,), MAXT // 3, MAXT + 1)
    full_device = jax.random.randint(jax.random.fold_in(key, 3), (), 0, device_count)
    live = jnp.where(jnp.arange(device_count) == full_device, MAXT, live)
    return (row_lists.reshape(-1).astype(jnp.int32), col_lists.reshape(-1).astype(jnp.int32), live.astype(jnp.int32))


def vol_lists(key):
    device_count = NV // (VB * TILE)
    candidate = jnp.arange(VB * 5 * CB, dtype=jnp.int32)
    row_block = candidate // (5 * CB)
    col_code = candidate % (5 * CB)
    device_step = jnp.abs(col_code // CB - 2)
    reach = cell_reach(row_block % CB, col_code % CB) + jnp.maximum(device_step - 1, 0)
    usable = reach <= 1
    device_keys = jax.random.split(jax.random.fold_in(key, 4), device_count)

    def per_device(dev_key):
        shuffled = jax.random.permutation(dev_key, VB * 5 * CB).astype(jnp.int32)
        scores = jnp.where(usable, shuffled, -1)
        unused, chosen = lax.top_k(scores, MAXV)
        return (row_block[chosen], col_code[chosen])
    row_lists, col_lists = jax.vmap(per_device)(device_keys)
    live = jax.random.randint(jax.random.fold_in(key, 5), (device_count,), MAXV // 3, MAXV + 1)
    full_device = jax.random.randint(jax.random.fold_in(key, 6), (), 0, device_count)
    live = jnp.where(jnp.arange(device_count) == full_device, MAXV, live)
    return (row_lists.reshape(-1).astype(jnp.int32), col_lists.reshape(-1).astype(jnp.int32), live.astype(jnp.int32))


def draw_pair_rows(key, part):
    return pair_lists(key)[0]


def draw_pair_cols(key, part):
    return pair_lists(key)[1]


def draw_pair_count(key, part):
    return pair_lists(key)[2]


def draw_vol_rows(key, part):
    return vol_lists(key)[0]


def draw_vol_cols(key, part):
    return vol_lists(key)[1]


def draw_vol_count(key, part):
    return vol_lists(key)[2]


def block_levels(rng, extent, cuts, least, top_value):
    gain = 1.0
    for axis_at, parts in cuts:
        draws = jax.random.uniform(jax.random.fold_in(jax.random.fold_in(rng, 6), axis_at), (parts,), jnp.float32, least / len(cuts), top_value / len(cuts))
        gain = gain * jnp.repeat(jnp.exp(draws), extent[axis_at] // parts).reshape((-1,) + (1,) * (len(extent) - 1 - axis_at))
    return gain


def setup_inputs(seed: int = 0) -> dict:
    splits = jax.random.split(jax.random.key(seed), 11)
    return {
        "ctrl_points": draw_ctrl_points(jax.random.fold_in(splits[10], 71), 0),
        "ctrl_disp": draw_ctrl_disp(jax.random.fold_in(splits[10], 71), 0),
        "stiffness": jnp.clip(jnp.exp(math.log(1.0) - 1.2039728 * jax.random.uniform(splits[2], (NC,), jnp.float32) ** block_levels(splits[2], (NC,), ((0, 128),), -0.2, 0.2)), 0.3, 1.0),
        "pair_rows": draw_pair_rows(jax.random.fold_in(splits[10], 71), 0),
        "pair_cols": draw_pair_cols(jax.random.fold_in(splits[10], 71), 0),
        "pair_count": draw_pair_count(jax.random.fold_in(splits[10], 71), 0),
        "vol_points": draw_vol_points(jax.random.fold_in(splits[10], 71), 0),
        "vol_rows": draw_vol_rows(jax.random.fold_in(splits[10], 71), 0),
        "vol_cols": draw_vol_cols(jax.random.fold_in(splits[10], 71), 0),
        "vol_count": draw_vol_count(jax.random.fold_in(splits[10], 71), 0),
    }


support_radius = 2.0
exact_mode = lax.Precision.HIGHEST

def wendland(row_points, col_points):
    dist_sq = jnp.zeros((row_points.shape[0], row_points.shape[2], col_points.shape[2]), row_points.dtype)
    for component in range(3):
        coord_gap = row_points[:, component, :, None] - col_points[:, component, None, :]
        dist_sq = dist_sq + coord_gap * coord_gap
    scaled_r = jnp.sqrt(dist_sq) / support_radius
    falloff = jnp.maximum(1.0 - scaled_r, 0.0)
    squared = falloff * falloff
    return squared * squared * (4.0 * scaled_r + 1.0)

def to_blocks(field):
    return field.reshape(3, -1, TILE).transpose(1, 0, 2)

def from_blocks(blocks):
    return blocks.transpose(1, 0, 2).reshape(3, -1)

def operate(points, vector, stiff_blocks, pair_rows, pair_cols, pair_count):
    block_total = points.shape[0]
    device_count = block_total // CB
    result = stiff_blocks[:, None, :] * vector

    def diag_part(block_ids):
        kernel = wendland(points[block_ids], points[block_ids]) / TILE
        return jnp.einsum('gkj,gij->gki', vector[block_ids], kernel, precision=exact_mode)
    diag_out = lax.map(diag_part, jnp.arange(block_total, dtype=jnp.int32).reshape(device_count, CB))
    result = result + diag_out.reshape(vector.shape)

    def per_device(carried, device):
        row_ids = lax.dynamic_slice_in_dim(pair_rows, device * MAXT, MAXT)
        col_ids = lax.dynamic_slice_in_dim(pair_cols, device * MAXT, MAXT)
        live_count = lax.dynamic_slice_in_dim(pair_count, device, 1)[0]
        row_global = device * CB + row_ids
        col_global = device * CB + col_ids
        slot_ids = jnp.arange(MAXT, dtype=jnp.int32)
        valid_mask = ((slot_ids < live_count) & (col_global < block_total)).astype(vector.dtype)
        col_safe = jnp.minimum(col_global, block_total - 1)
        kernel = wendland(points[row_global], points[col_safe]) * (valid_mask / TILE)[:, None, None]
        row_vec = vector[row_global]
        col_vec = vector[col_safe]
        to_rows = jnp.einsum('gkj,gij->gki', col_vec, kernel, precision=exact_mode) + lax.optimization_barrier(jnp.sum(kernel, axis=2))[:, None, :] * row_vec
        to_cols = jnp.einsum('gki,gij->gkj', row_vec, kernel, precision=exact_mode) + lax.optimization_barrier(jnp.sum(kernel, axis=1))[:, None, :] * col_vec
        carried = carried.at[row_global].add(to_rows).at[col_safe].add(to_cols)
        return (carried, None)
    result, unused = lax.scan(per_device, result, jnp.arange(device_count, dtype=jnp.int32))
    return result

def reference(ctrl_points, ctrl_disp, stiffness, pair_rows, pair_cols, pair_count, vol_points, vol_rows, vol_cols, vol_count):
    points = to_blocks(ctrl_points)
    stiff_blocks = stiffness.reshape(-1, TILE)
    block_total = points.shape[0]
    device_count = block_total // CB
    residual = to_blocks(ctrl_disp)
    direction = residual
    solution = jnp.zeros_like(residual)
    norm_now = lax.optimization_barrier(jnp.sum(residual * residual, axis=(0, 2)))
    for step in range(ITERS):
        image = operate(points, direction, stiff_blocks, pair_rows, pair_cols, pair_count)
        step_len = norm_now / lax.optimization_barrier(jnp.sum(direction * image, axis=(0, 2)))
        solution = solution + step_len[None, :, None] * direction
        residual = residual - step_len[None, :, None] * image
        norm_next = lax.optimization_barrier(jnp.sum(residual * residual, axis=(0, 2)))
        direction = residual + (norm_next / norm_now)[None, :, None] * direction
        norm_now = norm_next
    volume = to_blocks(vol_points)
    moved = jnp.zeros_like(volume)

    def per_device(carried, device):
        row_ids = lax.dynamic_slice_in_dim(vol_rows, device * MAXV, MAXV)
        col_ids = lax.dynamic_slice_in_dim(vol_cols, device * MAXV, MAXV)
        live_count = lax.dynamic_slice_in_dim(vol_count, device, 1)[0]
        source_device = device + col_ids // CB - 2
        col_global = source_device * CB + col_ids % CB
        slot_ids = jnp.arange(MAXV, dtype=jnp.int32)
        valid_mask = ((slot_ids < live_count) & (source_device >= 0) & (source_device < device_count)).astype(volume.dtype)
        col_safe = jnp.clip(col_global, 0, block_total - 1)
        row_global = device * VB + row_ids
        kernel = wendland(volume[row_global], points[col_safe]) * valid_mask[:, None, None]
        contrib = jnp.einsum('gkj,gij->gki', solution[col_safe], kernel, precision=exact_mode)
        return (carried.at[row_global].add(contrib), None)
    moved, unused = lax.scan(per_device, moved, jnp.arange(device_count, dtype=jnp.int32))
    moved = moved * TILE ** (-0.5)
    return (from_blocks(solution), from_blocks(moved))
```

```python
import functools

import jax
import jax.numpy as jnp
from jax import lax
from jax.experimental import pallas as pl
from jax.experimental.pallas import tpu as pltpu
from jax.sharding import PartitionSpec as P

TILE = 128
SIDE = 16
CB = 256
VB = 256
MAXT = 768
MAXV = 512
GROUP = 16
SHIFT = 0.75
FAR = 64.0

f32 = jnp.float32
bf16 = jnp.bfloat16
i32 = jnp.int32


def from_behind(block, axis, distance):
    devices = range(lax.axis_size(axis))
    route = [(i - distance, i) for i in devices if i - distance in devices]
    return lax.ppermute(block, axis, route)


def blocks_of(field):
    return field.reshape(3, -1, TILE).transpose(1, 0, 2)


def from_blocks(blocks):
    return blocks.transpose(1, 0, 2).reshape(3, -1)


def head(value):
    return lax.reduce_precision(value, 8, 7)


def local_coords(points, device):
    blocks = blocks_of(points)
    block = lax.iota(i32, blocks.shape[0])
    centre = jnp.stack(
        [
            jnp.full(block.shape, 0.5, f32) + device.astype(f32),
            2.0 * (block // SIDE).astype(f32) + 1.0,
            2.0 * (block % SIDE).astype(f32) + 1.0,
        ],
        axis=1,
    )
    return (blocks - centre[:, :, None]) * 0.25


def column_side(local):
    one = jnp.ones_like(local[:, :1])
    return jnp.concatenate([local, local, one, jnp.zeros_like(one)], axis=1)


def row_side(local):
    one = jnp.ones_like(local[:, :1])
    norm = jnp.sum(local * local, axis=1, keepdims=True)
    full = jnp.concatenate([-2.0 * local, one, one, one, norm, jnp.zeros_like(one)], axis=1)
    high = head(full)
    mid = head(full - high)
    low = head(full - high - mid)
    last = jnp.concatenate([mid[:, :3], one, one, one, low[:, 6:7], jnp.zeros_like(one)], axis=1)
    packed = jnp.concatenate([high, high, mid, last], axis=1).astype(bf16)
    return packed.reshape(-1, TILE, TILE).transpose(0, 2, 1)


def offset_table():
    code = lax.iota(i32, 125)
    step_x = (code // 25 - 2).astype(f32) * 0.25
    step_y = (code // 5 % 5 - 2).astype(f32) * 0.5
    step_z = (code % 5 - 2).astype(f32) * 0.5
    zero = jnp.zeros_like(step_x)
    rows = jnp.stack([step_x, step_y, step_z, step_x, step_y, step_z, zero, zero], axis=1)
    return jnp.broadcast_to(rows[:, :, None], (125, 8, TILE))


def offset_code(step_x, row_cell, col_cell):
    step_y = jnp.clip(col_cell // SIDE - row_cell // SIDE, -2, 2)
    step_z = jnp.clip(col_cell % SIDE - row_cell % SIDE, -2, 2)
    return (step_x + 2) * 25 + (step_y + 2) * 5 + step_z + 2


def with_far(columns):
    return jnp.concatenate([columns, jnp.full((1, 8, TILE), FAR, f32)], axis=0)


def split_rows(vector):
    high = head(vector)
    one = jnp.ones_like(vector[:, :1])
    return jnp.concatenate([high, one, vector - high, jnp.zeros_like(one)], axis=1)


def tile_loop(groups, listed, rows_ref, cols_ref, table_ref, dist_ref, tile_ref, use):
    row = lax.broadcasted_iota(i32, (8, TILE), 0)
    coords = row < 3
    squares = (row >= 3) & (row < 6)
    unit = row == 6
    dist_ref[...] = jnp.full_like(dist_ref, FAR)
    tile_ref[...] = jnp.zeros_like(tile_ref)

    def distances(slot):
        packed = listed[slot]
        row_block = packed & 255
        moved = cols_ref[(packed >> 8) & 2047] + table_ref[packed >> 19]
        full = jnp.where(squares, moved * moved, moved)
        high = full.astype(bf16).astype(f32)
        rest = full - high
        mid = rest.astype(bf16).astype(f32)
        last = jnp.where(squares, rest - mid, jnp.where(unit, 1.0, mid))
        features = jnp.concatenate([high, mid, high, last], axis=0).astype(bf16)
        place = row_block & 3
        empty = jnp.zeros_like(features)
        spread = jnp.concatenate(
            [jnp.where(place == quarter, features, empty) for quarter in range(4)], axis=0
        )
        return jnp.dot(rows_ref[row_block >> 2], spread, preferred_element_type=f32)

    def phi(dist_sq):
        dist_sq = jnp.maximum(dist_sq, 1e-12)
        gap = jnp.maximum(0.5 - dist_sq * lax.rsqrt(dist_sq), 0.0)
        gap_sq = gap * gap
        return gap_sq * gap_sq * (0.625 - gap)

    def step(at, carry):
        use(jnp.maximum(at - 2, 0) * GROUP)
        for k in range(GROUP):
            tile_ref[k] = phi(dist_ref[k]).astype(tile_ref.dtype)
        first = jnp.minimum(at, groups - 1) * GROUP
        for k in range(GROUP):
            dist_ref[k] = distances(first + k)
        return carry

    lax.fori_loop(0, jnp.where(groups > 0, groups + 2, 0), step, 0)


def pair_body(full_image, groups, diag_list, pair_list, rows_ref, cols_ref, vec_ref, table_ref, row_out, col_out, dist_ref, tile_ref):
    row_out[...] = jnp.zeros_like(row_out)
    col_out[...] = jnp.zeros_like(col_out)
    row = lax.broadcasted_iota(i32, (8, TILE), 0)

    def two(first, second):
        return jnp.concatenate([first, second], axis=0).astype(bf16)

    def add(out, found):
        for block, value in found:
            out[block] += value

    def use_diag(first):
        found = []
        for k in range(0, GROUP, 2):
            a, b = diag_list[first + k] & 255, diag_list[first + k + 1] & 255
            left = two(jnp.where(row == 3, 0.0, vec_ref[a]), jnp.where(row == 3, 0.0, vec_ref[b]))
            image = jnp.dot(
                left, jnp.concatenate([tile_ref[k], tile_ref[k + 1]], axis=1), preferred_element_type=f32
            )
            found += [(a, image[:8, :TILE]), (b, image[8:, TILE:])]
        add(col_out, found)

    def use_pair(first):
        to_rows, to_cols = [], []
        for k in range(0, GROUP, 2):
            p, q = pair_list[first + k], pair_list[first + k + 1]
            row_a, col_a = p & 255, (p >> 8) & 2047
            row_b, col_b = q & 255, (q >> 8) & 2047
            one, other = tile_ref[k], tile_ref[k + 1]
            left = two(vec_ref[row_a], vec_ref[row_b])
            if not full_image:
                left = left * 2
            image = jnp.dot(left, jnp.concatenate([one, other], axis=1), preferred_element_type=f32)
            to_cols += [(col_a, image[:8, :TILE]), (col_b, image[8:, TILE:])]
            if full_image:
                image = lax.dot_general(
                    two(vec_ref[col_a], vec_ref[col_b]),
                    jnp.concatenate([one, other], axis=0),
                    (((1,), (1,)), ((), ())),
                    preferred_element_type=f32,
                )
                to_rows += [(row_a, image[:8, :TILE]), (row_b, image[8:, TILE:])]
        add(row_out, to_rows)
        add(col_out, to_cols)

    loop = functools.partial(
        tile_loop, rows_ref=rows_ref, cols_ref=cols_ref, table_ref=table_ref, dist_ref=dist_ref, tile_ref=tile_ref
    )
    loop(jnp.int32(CB // GROUP), diag_list, use=use_diag)
    loop(groups[0], pair_list, use=use_pair)


def pair_call(full_image, groups, diag_list, pair_list, rows, cols, vec, table):
    smem = pl.BlockSpec(memory_space=pltpu.SMEM)
    vmem = pl.BlockSpec(memory_space=pltpu.VMEM)
    return pl.pallas_call(
        functools.partial(pair_body, full_image),
        out_shape=(
            jax.ShapeDtypeStruct((CB, 8, TILE), f32),
            jax.ShapeDtypeStruct((2 * CB + 1, 8, TILE), f32),
        ),
        in_specs=[smem] * 3 + [vmem] * 4,
        out_specs=(vmem, vmem),
        scratch_shapes=[pltpu.VMEM((GROUP, TILE, TILE), f32), pltpu.VMEM((GROUP, TILE, TILE), bf16)],
        compiler_params=pltpu.CompilerParams(vmem_limit_bytes=48 * 2**20),
        name="pair_tiles",
    )(groups, diag_list, pair_list, rows, cols, vec, table)


def volume_body(groups, vol_list, rows_ref, cols_ref, coef_ref, table_ref, out, dist_ref, tile_ref):
    out[...] = jnp.zeros_like(out)

    def use(first):
        found = []
        for k in range(GROUP):
            p = vol_list[first + k]
            tile = tile_ref[k]
            high = tile.astype(bf16)
            low = (tile - high.astype(f32)).astype(bf16)
            left = coef_ref[(p >> 8) & 2047]
            left = jnp.concatenate([left, left], axis=0).astype(bf16)
            dims = (((1,), (1,)), ((), ()))
            by_high = lax.dot_general(left, high, dims, preferred_element_type=f32)
            by_low = lax.dot_general(left, low, dims, preferred_element_type=f32)
            found.append((p & 255, by_high[:8] + by_low[:8]))
        for block, value in found:
            out[block] += value

    tile_loop(groups[0], vol_list, rows_ref, cols_ref, table_ref, dist_ref, tile_ref, use)


def volume_call(groups, vol_list, rows, cols, coef, table):
    smem = pl.BlockSpec(memory_space=pltpu.SMEM)
    vmem = pl.BlockSpec(memory_space=pltpu.VMEM)
    return pl.pallas_call(
        volume_body,
        out_shape=jax.ShapeDtypeStruct((VB, 8, TILE), f32),
        in_specs=[smem] * 2 + [vmem] * 4,
        out_specs=vmem,
        scratch_shapes=[pltpu.VMEM((GROUP, TILE, TILE), f32), pltpu.VMEM((GROUP, TILE, TILE), f32)],
        compiler_params=pltpu.CompilerParams(vmem_limit_bytes=48 * 2**20),
        name="volume_tiles",
    )(groups, vol_list, rows, cols, coef, table)


def cg_weights(moment):
    def gram(first, second):
        return sum(a * b * moment[i + j] for i, a in enumerate(first) for j, b in enumerate(second))

    def image(vector):
        grown = [SHIFT * a for a in vector] + [0.0]
        return [a + (vector[k - 1] if k else 0.0) for k, a in enumerate(grown)]

    def axpy(scale, first, second):
        size = max(len(first), len(second))
        pad = lambda v: list(v) + [0.0] * (size - len(v))
        return [scale * a + b for a, b in zip(pad(first), pad(second))]

    one = jnp.ones_like(moment[0])
    residual, direction, total = [one], [one], [0.0 * one]
    norm = gram(residual, residual)
    for step in range(3):
        grown = image(direction)
        length = norm / gram(direction, grown)
        total = axpy(length, direction, total)
        if step < 2:
            residual = axpy(-length, grown, residual)
            norm_next = gram(residual, residual)
            direction = axpy(norm_next / norm, direction, residual)
            norm = norm_next
    return total


def comp_sum(first, second):
    return jnp.sum(first * second, axis=(0, 2))


def body(ctrl_points, ctrl_disp, stiffness, pair_rows, pair_cols, pair_count, vol_points, vol_rows, vol_cols, vol_count):
    me = lax.axis_index("nodes")
    devices = lax.axis_size("nodes")

    near = {0: ctrl_points}
    for offset in (-1, 1, 2, -2):
        near[offset] = from_behind(ctrl_points, "nodes", offset)
    columns = {k: column_side(local_coords(v, me - k)) for k, v in near.items()}
    rows = row_side(local_coords(ctrl_points, me))
    table = offset_table()

    slots = lax.iota(i32, MAXT)
    right = pair_cols >= CB
    live = (slots < pair_count[0]) & (~right | (me < devices - 1))
    code = offset_code(right.astype(i32), pair_rows, pair_cols % CB)
    pair_list = jnp.where(live, pair_rows | (pair_cols << 8) | (code << 19), (2 * CB) << 8)
    pair_groups = (pair_count + GROUP - 1) // GROUP
    own = lax.iota(i32, CB)
    diag_list = own | (own << 8) | (62 << 19)

    pair_columns = with_far(jnp.concatenate([columns[0], columns[-1]], axis=0))
    stiff = stiffness.reshape(CB, 1, TILE)
    no_rows = jnp.zeros((1, 8, TILE), f32)

    def product(vector, full_image):
        beside = from_behind(from_blocks(vector), "nodes", -1)
        vec = split_rows(jnp.concatenate([vector, blocks_of(beside)], axis=0))
        vec = jnp.concatenate([vec, no_rows], axis=0)
        return pair_call(full_image, pair_groups, diag_list, pair_list, rows, pair_columns, vec, table), blocks_of(beside)

    def folded(sums):
        return jnp.concatenate([sums[:, :3] + sums[:, 4:7], sums[:, 3:4]], axis=1)

    basis = [blocks_of(ctrl_disp)]
    diagonal = None
    for step in range(2):
        (to_rows, to_cols), _ = product(basis[-1], True)
        back = from_behind(folded(to_cols[CB : 2 * CB]), "nodes", 1)
        total = folded(to_rows + to_cols[:CB]) + back
        if diagonal is None:
            diagonal = stiff + total[:, 3:4]
        basis.append(total[:, :3] + (diagonal - SHIFT) * basis[-1])
    last = basis[-1]
    (_, to_cols), beside = product(last, False)
    folded_cols = folded(to_cols)[:, :3]
    quad = (
        comp_sum(folded_cols[:CB], last)
        + comp_sum(folded_cols[CB : 2 * CB], beside)
        + comp_sum((diagonal - SHIFT) * last, last)
    )
    moments = jnp.stack(
        [
            comp_sum(basis[0], basis[0]),
            comp_sum(basis[0], basis[1]),
            comp_sum(basis[1], basis[1]),
            comp_sum(basis[1], basis[2]),
            comp_sum(basis[2], basis[2]),
            quad,
        ]
    )
    moments = lax.psum(moments, "nodes")
    weights = cg_weights([moments[k] for k in range(6)])
    solution = sum(w[None, :, None] * u for w, u in zip(weights, basis))

    slots = lax.iota(i32, MAXV)
    step_x = vol_cols // CB - 2
    source = me + step_x
    live = (slots < vol_count[0]) & (source >= 0) & (source < devices)
    code = offset_code(step_x, vol_rows, vol_cols % CB)
    vol_list = jnp.where(live, vol_rows | (vol_cols << 8) | (code << 19), (5 * CB) << 8)
    vol_groups = (vol_count + GROUP - 1) // GROUP
    order = (2, 1, 0, -1, -2)
    flat = from_blocks(solution)
    near_coef = [flat if k == 0 else from_behind(flat, "nodes", k) for k in order]
    coef = jnp.concatenate([split_rows(blocks_of(c)) for c in near_coef] + [no_rows], axis=0)
    all_columns = with_far(jnp.concatenate([columns[k] for k in order], axis=0))
    vol_features = row_side(local_coords(vol_points, me))
    moved = volume_call(vol_groups, vol_list, vol_features, all_columns, coef, table)
    moved = (moved[:, :3] + moved[:, 4:7]) * (TILE**0.5)
    return (flat, from_blocks(moved))


def solution(mesh):
    split = P(None, "nodes")
    flat = P("nodes")
    return jax.shard_map(
        body,
        mesh=mesh,
        in_specs=(split, split, flat, flat, flat, flat, split, flat, flat, flat),
        out_specs=(split, split),
        check_vma=False,
    )
```

```python
import functools

import jax
import jax.numpy as jnp
from jax import lax
from jax.experimental import pallas as pl
from jax.experimental.pallas import tpu as pltpu
from jax.sharding import PartitionSpec as P

TILE = 128
SIDE = 16
CB = 256
VB = 256
MAXT = 768
MAXV = 512
GROUP = 16
PART = 32
SHIFT = 0.75
FAR = 64.0

f32 = jnp.float32
bf16 = jnp.bfloat16
i32 = jnp.int32


def from_behind(block, axis, distance):
    devices = range(lax.axis_size(axis))
    route = [(i - distance, i) for i in devices if i - distance in devices]
    return lax.ppermute(block, axis, route)


def blocks_of(field):
    return field.reshape(3, -1, TILE).transpose(1, 0, 2)


def from_blocks(blocks):
    return blocks.transpose(1, 0, 2).reshape(3, -1)


def local_coords(points, device):
    blocks = blocks_of(points)
    block = lax.iota(i32, blocks.shape[0])
    centre = jnp.stack(
        [
            jnp.full(block.shape, 0.5, f32) + device.astype(f32),
            2.0 * (block // SIDE).astype(f32) + 1.0,
            2.0 * (block % SIDE).astype(f32) + 1.0,
        ],
        axis=1,
    )
    return (blocks - centre[:, :, None]) * 0.25


def payload(local, vector):
    rest = jnp.zeros((local.shape[0], 2, TILE), f32)
    return jnp.concatenate([local, vector, rest], axis=1)


def offset_table():
    code = lax.iota(i32, 125)
    step_x = (code // 25 - 2).astype(f32) * 0.25
    step_y = (code // 5 % 5 - 2).astype(f32) * 0.5
    step_z = (code % 5 - 2).astype(f32) * 0.5
    zero = jnp.zeros_like(step_x)
    rows = jnp.stack([step_x, step_y, step_z, step_x, step_y, step_z, zero, zero], axis=1)
    return jnp.broadcast_to(rows[:, :, None], (125, 8, TILE))


def offset_code(step_x, row_cell, col_cell):
    step_y = jnp.clip(col_cell // SIDE - row_cell // SIDE, -2, 2)
    step_z = jnp.clip(col_cell % SIDE - row_cell % SIDE, -2, 2)
    return (step_x + 2) * 25 + (step_y + 2) * 5 + step_z + 2


def row_ids():
    return lax.broadcasted_iota(i32, (8, TILE), 0)


def split(value):
    high = value.astype(bf16).astype(f32)
    return high, value - high


def column_rows(geo_refs, cols_ref):
    row = row_ids()
    for at, ref in enumerate(geo_refs):

        def fill(b, carry):
            for k in range(4):
                block = ref[4 * b + k]
                both = jnp.where(row < 3, block, pltpu.roll(block, 3, 0))
                cols_ref[at * CB + 4 * b + k] = jnp.where(row < 6, both, jnp.where(row == 6, 1.0, 0.0))
            return carry

        lax.fori_loop(0, CB // 4, fill, 0)
    cols_ref[len(geo_refs) * CB] = jnp.full((8, TILE), FAR, f32)


def row_features(geo_ref, rows_ref):
    row = row_ids()

    def features(block):
        coords = jnp.where(row < 3, block, 0.0)
        norm = jnp.sum(coords * coords, axis=0, keepdims=True)
        full = jnp.where(row < 3, -2.0 * coords, jnp.where(row < 6, 1.0, jnp.where(row == 6, norm, 0.0)))
        high, rest = split(full)
        mid, low = split(rest)
        last = jnp.where(row < 3, mid, jnp.where(row < 6, 1.0, jnp.where(row == 6, low, 0.0)))
        return [high, high, mid, last]

    def fill(at, carry):
        parts = []
        for k in range(4):
            parts += features(geo_ref[4 * at + k])
        turned = jnp.transpose(jnp.concatenate(parts, axis=0).astype(bf16))
        for k in range(4):
            rows_ref[4 * at + k] = turned if k == 0 else pltpu.roll(turned, TILE - k * PART, 1)
        return carry

    lax.fori_loop(0, geo_ref.shape[0] // 4, fill, 0)


def tile_loop(groups, listed, rows_ref, cols_ref, table_ref, dist_ref, tile_ref, use):
    row = row_ids()
    squares = (row >= 3) & (row < 6)
    unit = row == 6
    dist_ref[...] = jnp.full_like(dist_ref, FAR)
    tile_ref[...] = jnp.zeros_like(tile_ref)

    def distances(slot):
        packed = listed[slot]
        moved = cols_ref[(packed >> 8) & 2047] + table_ref[packed >> 19]
        full = jnp.where(squares, moved * moved, moved)
        high, rest = split(full)
        mid, low = split(rest)
        last = jnp.where(squares, low, jnp.where(unit, 1.0, mid))
        features = jnp.concatenate([high, mid, high, last], axis=0).astype(bf16)
        return jnp.dot(rows_ref[packed & 255][:, :PART], features, preferred_element_type=f32)

    def phi(dist_sq):
        dist_sq = jnp.maximum(dist_sq, 1e-12)
        gap = jnp.maximum(0.5 - dist_sq * lax.rsqrt(dist_sq), 0.0)
        gap_sq = gap * gap
        return gap_sq * gap_sq * (0.625 - gap)

    def step(at, carry):
        used = jnp.maximum(at - 2, 0) * GROUP
        first = jnp.minimum(at, groups - 1) * GROUP
        found = []
        for k in range(0, GROUP, 2):
            found += use(used, k)
            for j in (k, k + 1):
                tile_ref[j] = phi(dist_ref[j]).astype(tile_ref.dtype)
            for j in (k, k + 1):
                dist_ref[j] = distances(first + j)
        for out, block, value in found:
            out[block] += value
        return carry

    lax.fori_loop(0, jnp.where(groups > 0, groups + 2, 0), step, 0)


def pair_body(step, *refs):
    if step == 0:
        groups, diag_list, pair_list, own_geo, right_geo, table_ref = refs[:6]
        refs = refs[6:]
    else:
        groups, diag_list, pair_list, own_geo, right_geo, own_vec, right_vec, table_ref = refs[:8]
        refs = refs[8:]
    if step < 2:
        own_out, right_out = refs[:2]
        refs = refs[2:]
    else:
        (quad_out,) = refs[:1]
        refs = refs[1:]
    rows_ref, cols_ref, vec_ref, row_sum, col_sum, dist_ref, tile_ref = refs
    row = row_ids()

    column_rows((own_geo, right_geo), cols_ref)
    row_features(own_geo, rows_ref)
    for at, source in enumerate((own_geo, right_geo) if step == 0 else (own_vec, right_vec)):

        def fill(b, carry):
            for k in range(4):
                block = 4 * b + k
                if step == 0:
                    value = pltpu.roll(source[block], 5, 0)
                else:
                    value = source[:, pl.ds(pl.multiple_of(block * TILE, TILE), TILE)]
                    value = jnp.concatenate([value, jnp.zeros((5, TILE), f32)], axis=0)
                high, low = split(value)
                low = pltpu.roll(low, 4, 0)
                rows = jnp.where(row < 3, high, jnp.where(row == 3, 1.0, jnp.where(row < 7, low, 0.0)))
                vec_ref[at * CB + block] = rows
            return carry

        lax.fori_loop(0, CB // 4, fill, 0)
    vec_ref[2 * CB] = jnp.zeros((8, TILE), f32)
    row_sum[...] = jnp.zeros_like(row_sum)
    col_sum[...] = jnp.zeros_like(col_sum)

    def two(first, second):
        return jnp.concatenate([first, second], axis=0).astype(bf16)

    def use_diag(first, k):
        a, b = diag_list[first + k] & 255, diag_list[first + k + 1] & 255
        left = two(jnp.where(row == 3, 0.0, vec_ref[a]), jnp.where(row == 3, 0.0, vec_ref[b]))
        image = jnp.dot(
            left, jnp.concatenate([tile_ref[k], tile_ref[k + 1]], axis=1), preferred_element_type=f32
        )
        return [(col_sum, a, image[:8, :TILE]), (col_sum, b, image[8:, TILE:])]

    def use_pair(first, k):
        p, q = pair_list[first + k], pair_list[first + k + 1]
        row_a, col_a = p & 255, (p >> 8) & 2047
        row_b, col_b = q & 255, (q >> 8) & 2047
        one, other = tile_ref[k], tile_ref[k + 1]
        left = two(vec_ref[row_a], vec_ref[row_b])
        if step == 2:
            left = left * 2
        image = jnp.dot(left, jnp.concatenate([one, other], axis=1), preferred_element_type=f32)
        found = [(col_sum, col_a, image[:8, :TILE]), (col_sum, col_b, image[8:, TILE:])]
        if step < 2:
            image = lax.dot_general(
                two(vec_ref[col_a], vec_ref[col_b]),
                jnp.concatenate([one, other], axis=0),
                (((1,), (1,)), ((), ())),
                preferred_element_type=f32,
            )
            found += [(row_sum, row_a, image[:8, :TILE]), (row_sum, row_b, image[8:, TILE:])]
        return found

    loop = functools.partial(
        tile_loop, rows_ref=rows_ref, cols_ref=cols_ref, table_ref=table_ref, dist_ref=dist_ref, tile_ref=tile_ref
    )
    loop(jnp.int32(CB // GROUP), diag_list, use=use_diag)
    loop(groups[0], pair_list, use=use_pair)

    def fold(value):
        return value + pltpu.roll(value, 4, 0)

    if step < 2:

        def finish(b, carry):
            for k in range(4):
                block = 4 * b + k
                place = pl.ds(pl.multiple_of(block * TILE, TILE), TILE)
                own_out[:, place] = fold(row_sum[block] + col_sum[block])[:4]
                right_out[:, place] = fold(col_sum[CB + block])[:4]
            return carry

        lax.fori_loop(0, CB // 4, finish, 0)
    else:

        def finish(b, sums):
            new = []
            for k, total in enumerate(sums):
                block = 4 * b + k
                new.append(total + fold(col_sum[block]) * fold(vec_ref[block]))
            return tuple(new)

        zero = jnp.zeros((8, TILE), f32)
        sums = lax.fori_loop(0, 2 * CB // 4, finish, (zero,) * 4)
        quad_out[...] = sums[0] + sums[1] + sums[2] + sums[3]


def pair_call(step, groups, diag_list, pair_list, *arrays):
    smem = pl.BlockSpec(memory_space=pltpu.SMEM)
    vmem = pl.BlockSpec(memory_space=pltpu.VMEM)
    if step < 2:
        out = (jax.ShapeDtypeStruct((4, CB * TILE), f32),) * 2
    else:
        out = (jax.ShapeDtypeStruct((8, TILE), f32),)
    return pl.pallas_call(
        functools.partial(pair_body, step),
        out_shape=out,
        in_specs=[smem] * 3 + [vmem] * len(arrays),
        out_specs=(vmem,) * len(out),
        scratch_shapes=[
            pltpu.VMEM((CB, TILE, TILE), bf16),
            pltpu.VMEM((2 * CB + 1, 8, TILE), f32),
            pltpu.VMEM((2 * CB + 1, 8, TILE), f32),
            pltpu.VMEM((CB, 8, TILE), f32),
            pltpu.VMEM((2 * CB + 1, 8, TILE), f32),
            pltpu.VMEM((GROUP, TILE, TILE), f32),
            pltpu.VMEM((GROUP, TILE, TILE), bf16),
        ],
        compiler_params=pltpu.CompilerParams(vmem_limit_bytes=48 * 2**20),
        name=f"pair_tiles_{step}",
    )(groups, diag_list, pair_list, *arrays)


def volume_body(groups, vol_list, vol_geo, *refs):
    geos, firsts, seconds = refs[:5], refs[5:10], refs[10:15]
    table_ref, out, rows_ref, cols_ref, coef_ref, dist_ref, tile_ref = refs[15:]
    row = row_ids()
    column_rows(geos, cols_ref)
    row_features(vol_geo, rows_ref)
    for at in range(5):

        def fill(b, carry):
            for k in range(4):
                block = 4 * b + k
                place = pl.ds(pl.multiple_of(block * TILE, TILE), TILE)
                rest = jnp.zeros((5, TILE), f32)
                one = jnp.concatenate([firsts[at][:, place], rest], axis=0)
                two = jnp.concatenate([seconds[at][:, place], rest], axis=0)
                coef_ref[at * CB + block, :8] = jnp.where(row < 3, one, geos[at][block])
                coef_ref[at * CB + block, 8:] = two
            return carry

        lax.fori_loop(0, CB // 4, fill, 0)
    coef_ref[5 * CB] = jnp.zeros((16, TILE), f32)
    out[...] = jnp.zeros_like(out)

    def use(first, start):
        found = []
        dims = (((1,), (1,)), ((), ()))
        for k in (start, start + 1):
            p = vol_list[first + k]
            tile = tile_ref[k]
            high = tile.astype(bf16)
            low = (tile - high.astype(f32)).astype(bf16)
            left = coef_ref[(p >> 8) & 2047]
            left_high, left_low = split(left)
            by_high = lax.dot_general(
                jnp.concatenate([left_high, left_low], axis=0).astype(bf16), high, dims, preferred_element_type=f32
            )
            by_low = lax.dot_general(left_high.astype(bf16), low, dims, preferred_element_type=f32)
            found.append((out, p & 255, by_high[:16] + by_high[16:] + by_low))
        return found

    tile_loop(groups[0], vol_list, rows_ref, cols_ref, table_ref, dist_ref, tile_ref, use)


def volume_call(groups, vol_list, *arrays):
    smem = pl.BlockSpec(memory_space=pltpu.SMEM)
    vmem = pl.BlockSpec(memory_space=pltpu.VMEM)
    return pl.pallas_call(
        volume_body,
        out_shape=jax.ShapeDtypeStruct((VB, 16, TILE), f32),
        in_specs=[smem] * 2 + [vmem] * len(arrays),
        out_specs=vmem,
        scratch_shapes=[
            pltpu.VMEM((VB, TILE, TILE), bf16),
            pltpu.VMEM((5 * CB + 1, 8, TILE), f32),
            pltpu.VMEM((5 * CB + 1, 16, TILE), f32),
            pltpu.VMEM((GROUP, TILE, TILE), f32),
            pltpu.VMEM((GROUP, TILE, TILE), f32),
        ],
        compiler_params=pltpu.CompilerParams(vmem_limit_bytes=56 * 2**20),
        name="volume_tiles",
    )(groups, vol_list, *arrays)


def cg_weights(moment):
    def gram(first, second):
        return sum(a * b * moment[i + j] for i, a in enumerate(first) for j, b in enumerate(second))

    def image(vector):
        grown = [SHIFT * a for a in vector] + [0.0]
        return [a + (vector[k - 1] if k else 0.0) for k, a in enumerate(grown)]

    def axpy(scale, first, second):
        size = max(len(first), len(second))
        pad = lambda v: list(v) + [0.0] * (size - len(v))
        return [scale * a + b for a, b in zip(pad(first), pad(second))]

    one = jnp.ones_like(moment[0])
    residual, direction, total = [one], [one], [0.0 * one]
    norm = gram(residual, residual)
    for step in range(3):
        grown = image(direction)
        length = norm / gram(direction, grown)
        total = axpy(length, direction, total)
        if step < 2:
            residual = axpy(-length, grown, residual)
            norm_next = gram(residual, residual)
            direction = axpy(norm_next / norm, direction, residual)
            norm = norm_next
    return total


def comp_sum(first, second):
    return jnp.sum(first * second, axis=1)


def body(ctrl_points, ctrl_disp, stiffness, pair_rows, pair_cols, pair_count, vol_points, vol_rows, vol_cols, vol_count):
    me = lax.axis_index("nodes")
    devices = lax.axis_size("nodes")
    order = (2, 1, 0, -1, -2)

    geo = {0: payload(local_coords(ctrl_points, me), blocks_of(ctrl_disp))}
    for offset in (-1, 1, 2, -2):
        geo[offset] = from_behind(geo[0], "nodes", offset)
    table = offset_table()

    slots = lax.iota(i32, MAXT)
    right = pair_cols >= CB
    live = (slots < pair_count[0]) & (~right | (me < devices - 1))
    code = offset_code(right.astype(i32), pair_rows, pair_cols % CB)
    pair_list = jnp.where(live, pair_rows | (pair_cols << 8) | (code << 19), (2 * CB) << 8)
    pair_groups = (pair_count + GROUP - 1) // GROUP
    own = lax.iota(i32, CB)
    diag_list = own | (own << 8) | (62 << 19)

    slots = lax.iota(i32, MAXV)
    step_x = vol_cols // CB - 2
    source = me + step_x
    live = (slots < vol_count[0]) & (source >= 0) & (source < devices)
    code = offset_code(step_x, vol_rows, vol_cols % CB)
    vol_list = jnp.where(live, vol_rows | (vol_cols << 8) | (code << 19), (5 * CB) << 8)
    vol_groups = (vol_count + GROUP - 1) // GROUP
    vol_local = local_coords(vol_points, me)
    vol_geo = payload(vol_local, jnp.zeros_like(vol_local))

    def images(step, *vectors):
        own_part, right_part = pair_call(step, pair_groups, diag_list, pair_list, geo[0], geo[-1], *vectors, table)
        return own_part + from_behind(right_part, "nodes", 1)

    total = images(0)
    diagonal = stiffness[None, :] + total[3:4] - SHIFT
    first = total[:3] + diagonal * ctrl_disp
    near_first = {k: first if k == 0 else from_behind(first, "nodes", k) for k in (-1, 0, 1, 2, -2)}
    total = images(1, first, near_first[-1])
    second = total[:3] + diagonal * first
    near_second = {k: second if k == 0 else from_behind(second, "nodes", k) for k in (-1, 0, 1, 2, -2)}
    (quad,) = pair_call(2, pair_groups, diag_list, pair_list, geo[0], geo[-1], second, near_second[-1], table)
    moments = jnp.concatenate(
        [
            comp_sum(ctrl_disp, ctrl_disp),
            comp_sum(ctrl_disp, first),
            comp_sum(first, first),
            comp_sum(first, second),
            comp_sum(second, second),
            jnp.sum(quad, axis=1)[:3] + comp_sum(diagonal * second, second),
            jnp.zeros((TILE - 18,), f32),
        ]
    )

    parts = volume_call(
        vol_groups,
        vol_list,
        vol_geo,
        *[geo[k] for k in order],
        *[near_first[k] for k in order],
        *[near_second[k] for k in order],
        table,
    )
    moments, parts = lax.optimization_barrier((moments, parts))
    sent = jnp.broadcast_to(moments[None, None, :], (devices, 1, TILE))
    moments = jnp.sum(lax.all_to_all(sent, "nodes", 0, 0, tiled=True), axis=(0, 1))
    weights = cg_weights([moments[3 * k : 3 * k + 3] for k in range(6)])
    solution = sum(w[:, None] * u for w, u in zip(weights, (ctrl_disp, first, second)))
    scale = TILE**0.5
    parts = (parts[:, 3:6], parts[:, :3], parts[:, 8:11])
    moved = sum((scale * w)[None, :, None] * u for w, u in zip(weights, parts))
    return (solution, from_blocks(moved))


def solution(mesh):
    across = P(None, "nodes")
    flat = P("nodes")
    return jax.shard_map(
        body,
        mesh=mesh,
        in_specs=(across, across, flat, flat, flat, flat, across, flat, flat, flat),
        out_specs=(across, across),
        check_vma=False,
    )
```

```python
import functools

import jax
import jax.numpy as jnp
from jax import lax
from jax.experimental import pallas as pl
from jax.experimental.pallas import tpu as pltpu
from jax.sharding import PartitionSpec as P

TILE = 128
SIDE = 16
CB = 256
VB = 256
MAXT = 768
MAXV = 512
GROUP = 16
PART = 32
SHIFT = 0.75
FAR = 64.0

f32 = jnp.float32
bf16 = jnp.bfloat16
i32 = jnp.int32


def from_behind(block, axis, distance):
    devices = range(lax.axis_size(axis))
    route = [(i - distance, i) for i in devices if i - distance in devices]
    return lax.ppermute(block, axis, route)


def local_coords(points, device):
    block = lax.iota(i32, points.shape[1]) // TILE
    centre = jnp.stack(
        [
            jnp.full(block.shape, 0.5, f32) + device.astype(f32),
            2.0 * (block // SIDE).astype(f32) + 1.0,
            2.0 * (block % SIDE).astype(f32) + 1.0,
        ]
    )
    return (points - centre) * 0.25


def offset_table():
    code = lax.iota(i32, 125)
    step_x = (code // 25 - 2).astype(f32) * 0.25
    step_y = (code // 5 % 5 - 2).astype(f32) * 0.5
    step_z = (code % 5 - 2).astype(f32) * 0.5
    zero = jnp.zeros_like(step_x)
    rows = jnp.stack([step_x, step_y, step_z, step_x, step_y, step_z, zero, zero], axis=1)
    return jnp.broadcast_to(rows[:, :, None], (125, 8, TILE))


def offset_code(step_x, row_cell, col_cell):
    step_y = jnp.clip(col_cell // SIDE - row_cell // SIDE, -2, 2)
    step_z = jnp.clip(col_cell % SIDE - row_cell % SIDE, -2, 2)
    return (step_x + 2) * 25 + (step_y + 2) * 5 + step_z + 2


def row_ids():
    return lax.broadcasted_iota(i32, (8, TILE), 0)


def split(value):
    high = value.astype(bf16).astype(f32)
    return high, value - high


def three_rows(ref, first, count):
    value = ref[:, pl.ds(pl.multiple_of(first * TILE, count * TILE), count * TILE)]
    rest = jnp.zeros((5, TILE), f32)
    return [jnp.concatenate([value[:, k * TILE : (k + 1) * TILE], rest], axis=0) for k in range(count)]


def each_chunk(count, todo):
    def step(at, carry):
        todo(8 * at)
        return carry

    lax.fori_loop(0, count // 8, step, 0)


def column_rows(geo_refs, cols_ref):
    unit = jnp.where(row_ids() == 6, 1.0, 0.0)
    for at, ref in enumerate(geo_refs):

        def fill(first):
            rows = [block + pltpu.roll(block, 3, 0) + unit for block in three_rows(ref, first, 8)]
            cols_ref[pl.ds(at * CB + first, 8)] = jnp.stack(rows)

        each_chunk(CB, fill)
    cols_ref[len(geo_refs) * CB] = jnp.full((8, TILE), FAR, f32)


def vector_rows(refs, vec_ref, unit):
    unit = jnp.where(row_ids() == 3, unit, 0.0)
    for at, ref in enumerate(refs):

        def fill(first):
            rows = []
            for block in three_rows(ref, first, 8):
                high, low = split(block)
                rows.append(high + pltpu.roll(low, 4, 0) + unit)
            vec_ref[pl.ds(at * CB + first, 8)] = jnp.stack(rows)

        each_chunk(CB, fill)
    vec_ref[len(refs) * CB] = jnp.zeros((8, TILE), f32)


def row_features(geo_ref, rows_ref, first, count):
    row = row_ids()
    middle = (row >= 3) & (row < 6)

    def features(coords):
        norm = jnp.sum(coords * coords, axis=0, keepdims=True)
        full = jnp.where(middle, 1.0, jnp.where(row == 6, norm, -2.0 * coords))
        high, rest = split(full)
        mid, low = split(rest)
        last = jnp.where(row < 3, mid, jnp.where(middle, 1.0, low))
        return [high, high, mid, last]

    blocks = three_rows(geo_ref, first, count)
    for k in range(0, count, 4):
        parts = []
        for j in range(4):
            parts += features(blocks[k + j])
        turned = jnp.transpose(jnp.concatenate(parts, axis=0).astype(bf16))
        for j in range(4):
            rows_ref[first + k + j] = turned if j == 0 else pltpu.roll(turned, TILE - j * PART, 1)


def tile_loop(groups, listed, rows_ref, cols_ref, table_ref, dist_ref, tile_ref, use, ahead=None):
    row = row_ids()
    squares = (row >= 3) & (row < 6)
    unit = row == 6
    dist_ref[...] = jnp.full_like(dist_ref, FAR)
    tile_ref[...] = jnp.zeros_like(tile_ref)

    def distances(slot):
        packed = listed[slot]
        moved = cols_ref[(packed >> 8) & 2047] + table_ref[packed >> 19]
        full = jnp.where(squares, moved * moved, moved)
        high, rest = split(full)
        mid, low = split(rest)
        last = jnp.where(squares, low, jnp.where(unit, 1.0, mid))
        features = jnp.concatenate([high, mid, high, last], axis=0).astype(bf16)
        return jnp.dot(rows_ref[packed & 255][:, :PART], features, preferred_element_type=f32)

    def phi(dist_sq):
        dist_sq = jnp.maximum(dist_sq, 1e-12)
        gap = jnp.maximum(0.5 - dist_sq * lax.rsqrt(dist_sq), 0.0)
        gap_sq = gap * gap
        return gap_sq * gap_sq * (0.625 - gap)

    def step(at, carry):
        used = jnp.maximum(at - 2, 0) * GROUP
        first = jnp.minimum(at, groups - 1) * GROUP
        found = []
        for k in range(0, GROUP, 2):
            found += use(used, k)
            for j in (k, k + 1):
                tile_ref[j] = phi(dist_ref[j]).astype(tile_ref.dtype)
            for j in (k, k + 1):
                dist_ref[j] = distances(first + j)
        for out, block, value in found:
            out[block] += value
        if ahead is not None:
            ahead(jnp.minimum(at + 1, groups - 1) * GROUP)
        return carry

    lax.fori_loop(0, jnp.where(groups > 0, groups + 2, 0), step, 0)


def pair_body(step, groups, diag_list, pair_list, own_geo, right_geo, own_vec, right_vec, table_ref, *refs):
    outs, refs = refs[: 2 if step < 2 else 1], refs[2 if step < 2 else 1 :]
    rows_ref, cols_ref, vec_ref, row_sum, col_sum, dist_ref, tile_ref = refs
    row = row_ids()

    column_rows((own_geo, right_geo), cols_ref)
    vector_rows((own_vec, right_vec), vec_ref, 1.0)
    row_sum[...] = jnp.zeros_like(row_sum)
    col_sum[...] = jnp.zeros_like(col_sum)

    def two(first, second):
        return jnp.concatenate([first, second], axis=0).astype(bf16)

    def use_diag(first, k):
        a, b = diag_list[first + k] & 255, diag_list[first + k + 1] & 255
        left = two(jnp.where(row == 3, 0.0, vec_ref[a]), jnp.where(row == 3, 0.0, vec_ref[b]))
        image = jnp.dot(
            left, jnp.concatenate([tile_ref[k], tile_ref[k + 1]], axis=1), preferred_element_type=f32
        )
        return [(col_sum, a, image[:8, :TILE]), (col_sum, b, image[8:, TILE:])]

    def use_pair(first, k):
        p, q = pair_list[first + k], pair_list[first + k + 1]
        row_a, col_a = p & 255, (p >> 8) & 2047
        row_b, col_b = q & 255, (q >> 8) & 2047
        one, other = tile_ref[k], tile_ref[k + 1]
        left = two(vec_ref[row_a], vec_ref[row_b])
        if step == 2:
            left = left * 2
        image = jnp.dot(left, jnp.concatenate([one, other], axis=1), preferred_element_type=f32)
        found = [(col_sum, col_a, image[:8, :TILE]), (col_sum, col_b, image[8:, TILE:])]
        if step < 2:
            image = lax.dot_general(
                two(vec_ref[col_a], vec_ref[col_b]),
                jnp.concatenate([one, other], axis=0),
                (((1,), (1,)), ((), ())),
                preferred_element_type=f32,
            )
            found += [(row_sum, row_a, image[:8, :TILE]), (row_sum, row_b, image[8:, TILE:])]
        return found

    loop = functools.partial(
        tile_loop, rows_ref=rows_ref, cols_ref=cols_ref, table_ref=table_ref, dist_ref=dist_ref, tile_ref=tile_ref
    )
    ahead = functools.partial(row_features, own_geo, rows_ref, count=GROUP)
    ahead(0)
    loop(jnp.int32(CB // GROUP), diag_list, use=use_diag, ahead=ahead)
    loop(groups[0], pair_list, use=use_pair)

    def fold(value):
        return value + pltpu.roll(value, 4, 0)

    if step < 2:
        own_out, right_out = outs

        def finish(first):
            place = pl.ds(pl.multiple_of(first * TILE, 8 * TILE), 8 * TILE)
            own, right = row_sum[pl.ds(first, 8)] + col_sum[pl.ds(first, 8)], col_sum[pl.ds(CB + first, 8)]
            own_out[:, place] = jnp.concatenate([fold(own[k])[:4] for k in range(8)], axis=1)
            right_out[:, place] = jnp.concatenate([fold(right[k])[:4] for k in range(8)], axis=1)

        each_chunk(CB, finish)
    else:
        (quad_out,) = outs

        def finish(at, sums):
            return tuple(
                total + fold(col_sum[8 * at + k]) * fold(vec_ref[8 * at + k]) for k, total in enumerate(sums)
            )

        zero = jnp.zeros((8, TILE), f32)
        sums = lax.fori_loop(0, 2 * CB // 8, finish, (zero,) * 8)
        quad_out[...] = sum(sums)


def pair_call(step, groups, diag_list, pair_list, *arrays):
    smem = pl.BlockSpec(memory_space=pltpu.SMEM)
    vmem = pl.BlockSpec(memory_space=pltpu.VMEM)
    if step < 2:
        out = (jax.ShapeDtypeStruct((4, CB * TILE), f32),) * 2
    else:
        out = (jax.ShapeDtypeStruct((8, TILE), f32),)
    return pl.pallas_call(
        functools.partial(pair_body, step),
        out_shape=out,
        in_specs=[smem] * 3 + [vmem] * len(arrays),
        out_specs=(vmem,) * len(out),
        scratch_shapes=[
            pltpu.VMEM((CB, TILE, TILE), bf16),
            pltpu.VMEM((2 * CB + 1, 8, TILE), f32),
            pltpu.VMEM((2 * CB + 1, 8, TILE), f32),
            pltpu.VMEM((CB, 8, TILE), f32),
            pltpu.VMEM((2 * CB + 1, 8, TILE), f32),
            pltpu.VMEM((GROUP, TILE, TILE), f32),
            pltpu.VMEM((GROUP, TILE, TILE), bf16),
        ],
        compiler_params=pltpu.CompilerParams(vmem_limit_bytes=48 * 2**20),
        name=f"pair_tiles_{step}",
    )(groups, diag_list, pair_list, *arrays)


def volume_body(groups, vol_list, vol_geo, *refs):
    geos, coefs = refs[:5], refs[5:10]
    table_ref, out, rows_ref, cols_ref, coef_ref, sums, dist_ref, tile_ref = refs[10:]
    column_rows(geos, cols_ref)
    vector_rows(coefs, coef_ref, 0.0)
    sums[...] = jnp.zeros_like(sums)

    def features(at, carry):
        row_features(vol_geo, rows_ref, at * 16, 16)
        return carry

    lax.fori_loop(0, VB // 16, features, 0)

    def use(first, k):
        dims = (((1,), (1,)), ((), ()))
        p, q = vol_list[first + k], vol_list[first + k + 1]
        left = jnp.concatenate([coef_ref[(p >> 8) & 2047], coef_ref[(q >> 8) & 2047]], axis=0).astype(bf16)
        highs, lows = [], []
        for j in (k, k + 1):
            tile = tile_ref[j]
            high = tile.astype(bf16)
            highs.append(high)
            lows.append((tile - high.astype(f32)).astype(bf16))
        image = lax.dot_general(left, jnp.concatenate(highs, axis=0), dims, preferred_element_type=f32)
        image += lax.dot_general(left, jnp.concatenate(lows, axis=0), dims, preferred_element_type=f32)
        return [(sums, p & 255, image[:8, :TILE]), (sums, q & 255, image[8:, TILE:])]

    tile_loop(groups[0], vol_list, rows_ref, cols_ref, table_ref, dist_ref, tile_ref, use)

    def finish(first):
        value = sums[pl.ds(first, 8)]
        rows = [(value[k] + pltpu.roll(value[k], 4, 0))[:3] for k in range(8)]
        out[:, pl.ds(pl.multiple_of(first * TILE, 8 * TILE), 8 * TILE)] = jnp.concatenate(rows, axis=1) * TILE**0.5

    each_chunk(VB, finish)


def volume_call(groups, vol_list, *arrays):
    smem = pl.BlockSpec(memory_space=pltpu.SMEM)
    vmem = pl.BlockSpec(memory_space=pltpu.VMEM)
    return pl.pallas_call(
        volume_body,
        out_shape=jax.ShapeDtypeStruct((3, VB * TILE), f32),
        in_specs=[smem] * 2 + [vmem] * len(arrays),
        out_specs=vmem,
        scratch_shapes=[
            pltpu.VMEM((VB, TILE, TILE), bf16),
            pltpu.VMEM((5 * CB + 1, 8, TILE), f32),
            pltpu.VMEM((5 * CB + 1, 8, TILE), f32),
            pltpu.VMEM((VB, 8, TILE), f32),
            pltpu.VMEM((GROUP, TILE, TILE), f32),
            pltpu.VMEM((GROUP, TILE, TILE), f32),
        ],
        compiler_params=pltpu.CompilerParams(vmem_limit_bytes=56 * 2**20),
        name="volume_tiles",
    )(groups, vol_list, *arrays)


def cg_weights(moment):
    def gram(first, second):
        return sum(a * b * moment[i + j] for i, a in enumerate(first) for j, b in enumerate(second))

    def image(vector):
        grown = [SHIFT * a for a in vector] + [0.0]
        return [a + (vector[k - 1] if k else 0.0) for k, a in enumerate(grown)]

    def axpy(scale, first, second):
        size = max(len(first), len(second))
        pad = lambda v: list(v) + [0.0] * (size - len(v))
        return [scale * a + b for a, b in zip(pad(first), pad(second))]

    one = jnp.ones_like(moment[0])
    residual, direction, total = [one], [one], [0.0 * one]
    norm = gram(residual, residual)
    for step in range(3):
        grown = image(direction)
        length = norm / gram(direction, grown)
        total = axpy(length, direction, total)
        if step < 2:
            residual = axpy(-length, grown, residual)
            norm_next = gram(residual, residual)
            direction = axpy(norm_next / norm, direction, residual)
            norm = norm_next
    return total


def comp_sum(first, second):
    return jnp.sum(first * second, axis=1)


def body(ctrl_points, ctrl_disp, stiffness, pair_rows, pair_cols, pair_count, vol_points, vol_rows, vol_cols, vol_count):
    me = lax.axis_index("nodes")
    devices = lax.axis_size("nodes")
    order = (2, 1, 0, -1, -2)

    geo = {0: local_coords(ctrl_points, me)}
    geo[-1] = from_behind(geo[0], "nodes", -1)
    beside = from_behind(ctrl_disp, "nodes", -1)
    for offset in (1, 2, -2):
        geo[offset] = from_behind(geo[0], "nodes", offset)
    table = offset_table()

    slots = lax.iota(i32, MAXT)
    right = pair_cols >= CB
    live = (slots < pair_count[0]) & (~right | (me < devices - 1))
    code = offset_code(right.astype(i32), pair_rows, pair_cols % CB)
    pair_list = jnp.where(live, pair_rows | (pair_cols << 8) | (code << 19), (2 * CB) << 8)
    pair_groups = (pair_count + GROUP - 1) // GROUP
    own = lax.iota(i32, CB)
    diag_list = own | (own << 8) | (62 << 19)

    slots = lax.iota(i32, MAXV)
    step_x = vol_cols // CB - 2
    source = me + step_x
    live = (slots < vol_count[0]) & (source >= 0) & (source < devices)
    code = offset_code(step_x, vol_rows, vol_cols % CB)
    vol_list = jnp.where(live, vol_rows | (vol_cols << 8) | (code << 19), (5 * CB) << 8)
    vol_groups = (vol_count + GROUP - 1) // GROUP
    vol_geo = local_coords(vol_points, me)

    def images(step, *vectors):
        return pair_call(step, pair_groups, diag_list, pair_list, geo[0], geo[-1], *vectors, table)

    own_part, right_part = images(0, ctrl_disp, beside)
    total = own_part + from_behind(right_part, "nodes", 1)
    diagonal = stiffness[None, :] + total[3:4] - SHIFT
    first = total[:3] + diagonal * ctrl_disp
    own_part, right_part = images(1, first, from_behind(first, "nodes", -1))
    total = own_part + from_behind(right_part, "nodes", 1)
    second = total[:3] + diagonal * first
    (quad,) = images(2, second, from_behind(second, "nodes", -1))
    moments = jnp.concatenate(
        [
            comp_sum(ctrl_disp, ctrl_disp),
            comp_sum(ctrl_disp, first),
            comp_sum(first, first),
            comp_sum(first, second),
            comp_sum(second, second),
            jnp.sum(quad, axis=1)[:3] + comp_sum(diagonal * second, second),
            jnp.zeros((TILE - 18,), f32),
        ]
    )

    sent = jnp.broadcast_to(moments[None, None, :], (devices, 1, TILE))
    moments = jnp.sum(lax.all_to_all(sent, "nodes", 0, 0, tiled=True), axis=(0, 1))
    weights = cg_weights([moments[3 * k : 3 * k + 3] for k in range(6)])
    coef = sum(w[:, None] * u for w, u in zip(weights, (ctrl_disp, first, second)))
    near = [coef if k == 0 else from_behind(coef, "nodes", k) for k in order]
    moved = volume_call(vol_groups, vol_list, vol_geo, *[geo[k] for k in order], *near, table)
    return (coef, moved)


def solution(mesh):
    across = P(None, "nodes")
    flat = P("nodes")
    return jax.shard_map(
        body,
        mesh=mesh,
        in_specs=(across, across, flat, flat, flat, flat, across, flat, flat, flat),
        out_specs=(across, across),
        check_vma=False,
    )
```

```python
import functools

import jax
import jax.numpy as jnp
from jax import lax
from jax.experimental import pallas as pl
from jax.experimental.pallas import tpu as pltpu
from jax.sharding import PartitionSpec as P

TILE = 128
SIDE = 16
CB = 256
VB = 256
MAXT = 768
MAXV = 512
GROUP = 16
PART = 32
RING = 8
DIAG_GROUPS = CB // GROUP
PAIR_GROUPS = MAXT // GROUP
SHIFT = 0.75
FAR = 64.0

f32 = jnp.float32
bf16 = jnp.bfloat16
i32 = jnp.int32


def from_behind(block, axis, distance):
    devices = range(lax.axis_size(axis))
    route = [(i - distance, i) for i in devices if i - distance in devices]
    return lax.ppermute(block, axis, route)


def local_coords(points, device):
    block = lax.iota(i32, points.shape[1]) // TILE
    centre = jnp.stack(
        [
            jnp.full(block.shape, 0.5, f32) + device.astype(f32),
            2.0 * (block // SIDE).astype(f32) + 1.0,
            2.0 * (block % SIDE).astype(f32) + 1.0,
        ]
    )
    return (points - centre) * 0.25


def offset_table():
    code = lax.iota(i32, 125)
    step_x = (code // 25 - 2).astype(f32) * 0.25
    step_y = (code // 5 % 5 - 2).astype(f32) * 0.5
    step_z = (code % 5 - 2).astype(f32) * 0.5
    zero = jnp.zeros_like(step_x)
    rows = jnp.stack([step_x, step_y, step_z, step_x, step_y, step_z, zero, zero], axis=1)
    return jnp.broadcast_to(rows[:, :, None], (125, 8, TILE))


def offset_code(step_x, row_cell, col_cell):
    step_y = jnp.clip(col_cell // SIDE - row_cell // SIDE, -2, 2)
    step_z = jnp.clip(col_cell % SIDE - row_cell % SIDE, -2, 2)
    return (step_x + 2) * 25 + (step_y + 2) * 5 + step_z + 2


def row_ids():
    return lax.broadcasted_iota(i32, (8, TILE), 0)


def split(value):
    high = value.astype(bf16).astype(f32)
    return high, value - high


def three_rows(ref, first, count):
    value = ref[:, pl.ds(pl.multiple_of(first * TILE, count * TILE), count * TILE)]
    rest = jnp.zeros((5, TILE), f32)
    return [jnp.concatenate([value[:, k * TILE : (k + 1) * TILE], rest], axis=0) for k in range(count)]


def each_chunk(count, todo):
    def step(at, carry):
        todo(8 * at)
        return carry

    lax.fori_loop(0, count // 8, step, 0)


def column_rows(geo_refs, cols_ref):
    unit = jnp.where(row_ids() == 6, 1.0, 0.0)
    for at, ref in enumerate(geo_refs):

        def fill(first):
            rows = [block + pltpu.roll(block, 3, 0) + unit for block in three_rows(ref, first, 8)]
            cols_ref[pl.ds(at * CB + first, 8)] = jnp.stack(rows)

        each_chunk(CB, fill)
    cols_ref[len(geo_refs) * CB] = jnp.full((8, TILE), FAR, f32)


def vector_rows(refs, vec_ref, unit):
    unit = jnp.where(row_ids() == 3, unit, 0.0)
    for at, ref in enumerate(refs):

        def fill(first):
            rows = []
            for block in three_rows(ref, first, 8):
                high, low = split(block)
                rows.append(high + pltpu.roll(low, 4, 0) + unit)
            vec_ref[pl.ds(at * CB + first, 8)] = jnp.stack(rows)

        each_chunk(CB, fill)
    vec_ref[len(refs) * CB] = jnp.zeros((8, TILE), f32)


def row_features(geo_ref, rows_ref, first, count):
    row = row_ids()
    middle = (row >= 3) & (row < 6)

    def features(coords):
        norm = jnp.sum(coords * coords, axis=0, keepdims=True)
        full = jnp.where(middle, 1.0, jnp.where(row == 6, norm, -2.0 * coords))
        high, rest = split(full)
        mid, low = split(rest)
        last = jnp.where(row < 3, mid, jnp.where(middle, 1.0, low))
        return [high, high, mid, last]

    blocks = three_rows(geo_ref, first, count)
    for k in range(0, count, 4):
        parts = []
        for j in range(4):
            parts += features(blocks[k + j])
        turned = jnp.transpose(jnp.concatenate(parts, axis=0).astype(bf16))
        for j in range(4):
            rows_ref[first + k + j] = turned if j == 0 else pltpu.roll(turned, TILE - j * PART, 1)


def tile_loop(groups, listed, rows_ref, cols_ref, table_ref, dist_ref, tile_ref, use, ahead=None, keep=None):
    row = row_ids()
    squares = (row >= 3) & (row < 6)
    unit = row == 6
    dist_ref[...] = jnp.full_like(dist_ref, FAR)
    tile_ref[...] = jnp.zeros_like(tile_ref)

    def distances(slot):
        packed = listed[slot]
        moved = cols_ref[(packed >> 8) & 2047] + table_ref[packed >> 19]
        full = jnp.where(squares, moved * moved, moved)
        high, rest = split(full)
        mid, low = split(rest)
        last = jnp.where(squares, low, jnp.where(unit, 1.0, mid))
        features = jnp.concatenate([high, mid, high, last], axis=0).astype(bf16)
        return jnp.dot(rows_ref[packed & 255][:, :PART], features, preferred_element_type=f32)

    def phi(dist_sq):
        dist_sq = jnp.maximum(dist_sq, 1e-12)
        gap = jnp.maximum(0.5 - dist_sq * lax.rsqrt(dist_sq), 0.0)
        gap_sq = gap * gap
        return gap_sq * gap_sq * (0.625 - gap)

    if keep is not None:
        stage_ref, sems, home = keep

    def copy_out(group):
        slot = lax.rem(group, RING)
        return pltpu.make_async_copy(stage_ref.at[pl.ds(slot, 1)], home(group), sems.at[slot])

    def step(at, carry):
        used = jnp.maximum(at - 2, 0) * GROUP
        first = jnp.minimum(at, groups - 1) * GROUP
        if keep is not None:
            stage = lax.rem(at + RING - 1, RING)
            before = at - 1 - RING

            @pl.when(before >= 0)
            def _():
                copy_out(before).wait()

        found = []
        for k in range(0, GROUP, 2):
            found += use(used, k, (tile_ref[k], tile_ref[k + 1]))
            for j in (k, k + 1):
                tile = phi(dist_ref[j]).astype(tile_ref.dtype)
                tile_ref[j] = tile
                if keep is not None:
                    stage_ref[stage, j] = tile
            for j in (k, k + 1):
                dist_ref[j] = distances(first + j)
        for out, block, value in found:
            out[block] += value
        if ahead is not None:
            ahead(jnp.minimum(at + 1, groups - 1) * GROUP)
        if keep is not None:

            @pl.when((at > 0) & (at <= groups))
            def _():
                copy_out(at - 1).start()

        return carry

    lax.fori_loop(0, jnp.where(groups > 0, groups + 2, 0), step, 0)
    if keep is not None:
        for back in range(1, RING):
            group = groups - back

            @pl.when(group >= 0)
            def _():
                copy_out(group).wait()


def stream_loop(pairs, home, stage_ref, sems, use):
    ring = stage_ref.shape[0]

    def copy_in(at):
        slot = lax.rem(at, ring)
        return pltpu.make_async_copy(home(2 * at, 2), stage_ref.at[slot], sems.at[slot])

    for at in range(ring - 1):

        @pl.when(at < pairs)
        def _():
            copy_in(at).start()

    def step(at, carry):
        @pl.when(at + ring - 1 < pairs)
        def _():
            copy_in(at + ring - 1).start()

        copy_in(at).wait()
        slot = lax.rem(at, ring)
        found = []
        for k in range(0, 2 * GROUP, 2):
            tile = k % GROUP
            found += use(2 * at * GROUP, k, (stage_ref[slot, k // GROUP, tile], stage_ref[slot, k // GROUP, tile + 1]))
        for out, block, value in found:
            out[block] += value
        return carry

    lax.fori_loop(0, pairs, step, 0)


def pair_body(step, groups, diag_list, pair_list, own_vec, right_vec, *refs):
    if step == 0:
        own_geo, right_geo, table_ref, stiff_ref, own_out, right_out, tiles = refs[:7]
        vec_ref, row_sum, col_sum, stage_ref, sems, rows_ref, cols_ref, dist_ref, tile_ref = refs[7:]
        column_rows((own_geo, right_geo), cols_ref)
    else:
        tiles, *outs, vec_ref, row_sum, col_sum, stage_ref, sems = refs
    row = row_ids()

    vector_rows((own_vec, right_vec), vec_ref, 1.0)
    row_sum[...] = jnp.zeros_like(row_sum)
    col_sum[...] = jnp.zeros_like(col_sum)

    def two(first, second):
        return jnp.concatenate([first, second], axis=0).astype(bf16)

    def use_diag(first, k, pair):
        a, b = diag_list[first + k] & 255, diag_list[first + k + 1] & 255
        left = two(jnp.where(row == 3, 0.0, vec_ref[a]), jnp.where(row == 3, 0.0, vec_ref[b]))
        image = jnp.dot(
            left, jnp.concatenate(pair, axis=1), preferred_element_type=f32
        )
        return [(col_sum, a, image[:8, :TILE]), (col_sum, b, image[8:, TILE:])]

    def use_pair(first, k, pair):
        p, q = pair_list[first + k], pair_list[first + k + 1]
        row_a, col_a = p & 255, (p >> 8) & 2047
        row_b, col_b = q & 255, (q >> 8) & 2047
        left = two(vec_ref[row_a], vec_ref[row_b])
        if step == 2:
            left = left * 2
        image = jnp.dot(left, jnp.concatenate(pair, axis=1), preferred_element_type=f32)
        found = [(col_sum, col_a, image[:8, :TILE]), (col_sum, col_b, image[8:, TILE:])]
        if step < 2:
            image = lax.dot_general(
                two(vec_ref[col_a], vec_ref[col_b]),
                jnp.concatenate(pair, axis=0),
                (((1,), (1,)), ((), ())),
                preferred_element_type=f32,
            )
            found += [(row_sum, row_a, image[:8, :TILE]), (row_sum, row_b, image[8:, TILE:])]
        return found

    def diag_home(group, count=1):
        return tiles.at[pl.ds(group, count)]

    def pair_home(group, count=1):
        return tiles.at[pl.ds(DIAG_GROUPS + group, count)]

    if step == 0:
        loop = functools.partial(
            tile_loop, rows_ref=rows_ref, cols_ref=cols_ref, table_ref=table_ref, dist_ref=dist_ref, tile_ref=tile_ref
        )
        ahead = functools.partial(row_features, own_geo, rows_ref, count=GROUP)
        ahead(0)
        loop(jnp.int32(DIAG_GROUPS), diag_list, use=use_diag, ahead=ahead, keep=(stage_ref, sems, diag_home))
        loop(groups[0], pair_list, use=use_pair, keep=(stage_ref, sems, pair_home))
    else:
        stream_loop(jnp.int32(DIAG_GROUPS // 2), diag_home, stage_ref, sems, use_diag)
        stream_loop(lax.div(groups[0], 2), pair_home, stage_ref, sems, use_pair)

    def fold(value):
        return value + pltpu.roll(value, 4, 0)

    if step < 2:
        images = (own_out, right_out) if step == 0 else outs

        def finish(first):
            place = pl.ds(pl.multiple_of(first * TILE, 8 * TILE), 8 * TILE)
            own, right = row_sum[pl.ds(first, 8)] + col_sum[pl.ds(first, 8)], col_sum[pl.ds(CB + first, 8)]
            own = jnp.concatenate([fold(own[k])[:4] for k in range(8)], axis=1)
            if step == 0:
                fourth = lax.broadcasted_iota(i32, own.shape, 0) == 3
                own = own + jnp.where(fourth, stiff_ref[:, place] - SHIFT, 0.0)
            images[0][:, place] = own
            images[1][:, place] = jnp.concatenate([fold(right[k])[:4] for k in range(8)], axis=1)

        each_chunk(CB, finish)
    else:
        quad_out = outs[0]

        def finish(at, sums):
            return tuple(
                total + fold(col_sum[8 * at + k]) * fold(vec_ref[8 * at + k]) for k, total in enumerate(sums)
            )

        zero = jnp.zeros((8, TILE), f32)
        sums = lax.fori_loop(0, 2 * CB // 8, finish, (zero,) * 8)
        quad_out[...] = sum(sums)


def pair_call(step, *arrays, groups, diag_list, pair_list):
    smem = pl.BlockSpec(memory_space=pltpu.SMEM)
    vmem = pl.BlockSpec(memory_space=pltpu.VMEM)
    some = pl.BlockSpec(memory_space=pl.ANY)
    image = jax.ShapeDtypeStruct((4, CB * TILE), f32)
    kept = jax.ShapeDtypeStruct((DIAG_GROUPS + PAIR_GROUPS, GROUP, TILE, TILE), bf16)
    scratch = [
        pltpu.VMEM((2 * CB + 1, 8, TILE), f32),
        pltpu.VMEM((CB, 8, TILE), f32),
        pltpu.VMEM((2 * CB + 1, 8, TILE), f32),
        pltpu.VMEM((RING, GROUP, TILE, TILE) if step == 0 else (RING // 2, 2, GROUP, TILE, TILE), bf16),
        pltpu.SemaphoreType.DMA((RING,)),
    ]
    if step == 0:
        scratch += [
            pltpu.VMEM((CB, TILE, TILE), bf16),
            pltpu.VMEM((2 * CB + 1, 8, TILE), f32),
            pltpu.VMEM((GROUP, TILE, TILE), f32),
            pltpu.VMEM((GROUP, TILE, TILE), bf16),
        ]
    return pl.pallas_call(
        functools.partial(pair_body, step),
        out_shape=((image, image, kept), (image, image), (jax.ShapeDtypeStruct((8, TILE), f32),))[step],
        in_specs=[smem] * 3 + [vmem] * (len(arrays) - 1) + [vmem if step == 0 else some],
        out_specs=((vmem, vmem, some), (vmem, vmem), (vmem,))[step],
        scratch_shapes=scratch,
        compiler_params=pltpu.CompilerParams(vmem_limit_bytes=48 * 2**20),
        cost_estimate=pl.CostEstimate(flops=2 * 10**9, bytes_accessed=10**8, transcendentals=0),
        name=f"pair_tiles_{step}",
    )(groups, diag_list, pair_list, *arrays)


def volume_body(groups, vol_list, vol_geo, *refs):
    geos, coefs = refs[:5], refs[5:10]
    table_ref, out, rows_ref, cols_ref, coef_ref, sums, dist_ref, tile_ref = refs[10:]
    column_rows(geos, cols_ref)
    vector_rows(coefs, coef_ref, 0.0)
    sums[...] = jnp.zeros_like(sums)

    def features(at, carry):
        row_features(vol_geo, rows_ref, at * 16, 16)
        return carry

    lax.fori_loop(0, VB // 16, features, 0)

    def use(first, k, pair):
        dims = (((1,), (1,)), ((), ()))
        p, q = vol_list[first + k], vol_list[first + k + 1]
        left = jnp.concatenate([coef_ref[(p >> 8) & 2047], coef_ref[(q >> 8) & 2047]], axis=0).astype(bf16)
        highs, lows = [], []
        for tile in pair:
            high = tile.astype(bf16)
            highs.append(high)
            lows.append((tile - high.astype(f32)).astype(bf16))
        image = lax.dot_general(left, jnp.concatenate(highs, axis=0), dims, preferred_element_type=f32)
        image += lax.dot_general(left, jnp.concatenate(lows, axis=0), dims, preferred_element_type=f32)
        return [(sums, p & 255, image[:8, :TILE]), (sums, q & 255, image[8:, TILE:])]

    tile_loop(groups[0], vol_list, rows_ref, cols_ref, table_ref, dist_ref, tile_ref, use)

    def finish(first):
        value = sums[pl.ds(first, 8)]
        rows = [(value[k] + pltpu.roll(value[k], 4, 0))[:3] for k in range(8)]
        out[:, pl.ds(pl.multiple_of(first * TILE, 8 * TILE), 8 * TILE)] = jnp.concatenate(rows, axis=1) * TILE**0.5

    each_chunk(VB, finish)


def volume_call(groups, vol_list, *arrays):
    smem = pl.BlockSpec(memory_space=pltpu.SMEM)
    vmem = pl.BlockSpec(memory_space=pltpu.VMEM)
    return pl.pallas_call(
        volume_body,
        out_shape=jax.ShapeDtypeStruct((3, VB * TILE), f32),
        in_specs=[smem] * 2 + [vmem] * len(arrays),
        out_specs=vmem,
        scratch_shapes=[
            pltpu.VMEM((VB, TILE, TILE), bf16),
            pltpu.VMEM((5 * CB + 1, 8, TILE), f32),
            pltpu.VMEM((5 * CB + 1, 8, TILE), f32),
            pltpu.VMEM((VB, 8, TILE), f32),
            pltpu.VMEM((GROUP, TILE, TILE), f32),
            pltpu.VMEM((GROUP, TILE, TILE), f32),
        ],
        compiler_params=pltpu.CompilerParams(vmem_limit_bytes=56 * 2**20),
        cost_estimate=pl.CostEstimate(flops=2 * 10**9, bytes_accessed=10**8, transcendentals=0),
        name="volume_tiles",
    )(groups, vol_list, *arrays)


def cg_weights(moment):
    def gram(first, second):
        return sum(a * b * moment[i + j] for i, a in enumerate(first) for j, b in enumerate(second))

    def image(vector):
        grown = [SHIFT * a for a in vector] + [0.0]
        return [a + (vector[k - 1] if k else 0.0) for k, a in enumerate(grown)]

    def axpy(scale, first, second):
        size = max(len(first), len(second))
        pad = lambda v: list(v) + [0.0] * (size - len(v))
        return [scale * a + b for a, b in zip(pad(first), pad(second))]

    one = jnp.ones_like(moment[0])
    residual, direction, total = [one], [one], [0.0 * one]
    norm = gram(residual, residual)
    for step in range(3):
        grown = image(direction)
        length = norm / gram(direction, grown)
        total = axpy(length, direction, total)
        if step < 2:
            residual = axpy(-length, grown, residual)
            norm_next = gram(residual, residual)
            direction = axpy(norm_next / norm, direction, residual)
            norm = norm_next
    return total


def comp_sum(first, second):
    return jnp.sum(first * second, axis=1)


def body(ctrl_points, ctrl_disp, stiffness, pair_rows, pair_cols, pair_count, vol_points, vol_rows, vol_cols, vol_count):
    me = lax.axis_index("nodes")
    devices = lax.axis_size("nodes")
    order = (2, 1, 0, -1, -2)

    geo = {0: local_coords(ctrl_points, me)}
    geo[-1] = from_behind(geo[0], "nodes", -1)
    beside = from_behind(ctrl_disp, "nodes", -1)
    for offset in (1, 2, -2):
        geo[offset] = from_behind(geo[0], "nodes", offset)
    table = offset_table()

    slots = lax.iota(i32, MAXT)
    right = pair_cols >= CB
    live = (slots < pair_count[0]) & (~right | (me < devices - 1))
    code = offset_code(right.astype(i32), pair_rows, pair_cols % CB)
    pair_list = jnp.where(live, pair_rows | (pair_cols << 8) | (code << 19), (2 * CB) << 8)
    pair_groups = (pair_count + 2 * GROUP - 1) // (2 * GROUP) * 2
    own = lax.iota(i32, CB)
    diag_list = own | (own << 8) | (62 << 19)

    slots = lax.iota(i32, MAXV)
    step_x = vol_cols // CB - 2
    source = me + step_x
    live = (slots < vol_count[0]) & (source >= 0) & (source < devices)
    code = offset_code(step_x, vol_rows, vol_cols % CB)
    vol_list = jnp.where(live, vol_rows | (vol_cols << 8) | (code << 19), (5 * CB) << 8)
    vol_groups = (vol_count + GROUP - 1) // GROUP
    vol_geo = local_coords(vol_points, me)

    images = functools.partial(pair_call, groups=pair_groups, diag_list=diag_list, pair_list=pair_list)

    def exchanged(own_part, right_part):
        back = from_behind(right_part, "nodes", 1)
        ahead = from_behind(own_part, "nodes", -1)
        return own_part + back, ahead + right_part

    own_part, right_part, tiles = images(0, ctrl_disp, beside, geo[0], geo[-1], table, stiffness[None, :])
    own_part, right_part, geo[1], geo[2], geo[-2] = lax.optimization_barrier(
        (own_part, right_part, geo[1], geo[2], geo[-2])
    )
    total, total_beside = exchanged(own_part, right_part)
    diagonal, diagonal_beside = total[3:4], total_beside[3:4]
    first = total[:3] + diagonal * ctrl_disp
    first_beside = total_beside[:3] + diagonal_beside * beside
    total, total_beside = exchanged(*images(1, first, first_beside, tiles))
    second = total[:3] + diagonal * first
    second_beside = total_beside[:3] + diagonal_beside * first_beside
    (quad,) = images(2, second, second_beside, tiles)
    moments = jnp.concatenate(
        [
            comp_sum(ctrl_disp, ctrl_disp),
            comp_sum(ctrl_disp, first),
            comp_sum(first, first),
            comp_sum(first, second),
            comp_sum(second, second),
            jnp.sum(quad, axis=1)[:3] + comp_sum(diagonal * second, second),
            jnp.zeros((TILE - 18,), f32),
        ]
    )

    sent = jnp.broadcast_to(moments[None, None, :], (devices, 1, TILE))
    moments = jnp.sum(lax.all_to_all(sent, "nodes", 0, 0, tiled=True), axis=(0, 1))
    weights = cg_weights([moments[3 * k : 3 * k + 3] for k in range(6)])
    coef = sum(w[:, None] * u for w, u in zip(weights, (ctrl_disp, first, second)))
    near = [coef if k == 0 else from_behind(coef, "nodes", k) for k in order]
    moved = volume_call(vol_groups, vol_list, vol_geo, *[geo[k] for k in order], *near, table)
    return (coef, moved)


def solution(mesh):
    across = P(None, "nodes")
    flat = P("nodes")
    return jax.shard_map(
        body,
        mesh=mesh,
        in_specs=(across, across, flat, flat, flat, flat, across, flat, flat, flat),
        out_specs=(across, across),
        check_vma=False,
    )
```

```python
import functools

import jax
import jax.numpy as jnp
from jax import lax
from jax.experimental import pallas as pl
from jax.experimental.pallas import tpu as pltpu
from jax.sharding import PartitionSpec as P

TILE = 128
SIDE = 16
CB = 256
VB = 256
MAXT = 768
MAXV = 512
GROUP = 16
PART = 32
RING = 8
DIAG_GROUPS = CB // GROUP
PAIR_GROUPS = MAXT // GROUP
SHIFT = 0.75
FAR = 64.0

f32 = jnp.float32
bf16 = jnp.bfloat16
i32 = jnp.int32


def from_behind(block, axis, distance):
    devices = range(lax.axis_size(axis))
    route = [(i - distance, i) for i in devices if i - distance in devices]
    return lax.ppermute(block, axis, route)


def around(block, axis):
    devices = range(lax.axis_size(axis))

    def send(value, target):
        return lax.ppermute(value, axis, [(i, target(i)) for i in devices if target(i) in devices])

    far = send(block, lambda i: i - 2 if i % 2 else i + 2)
    near = send(block, lambda i: i + 1 if i % 2 else i - 1)
    partner = send(block, lambda i: i ^ 1)
    shared = send(near, lambda i: i ^ 1)
    return [far, near, block, partner, shared]


def offset_table():
    code = lax.iota(i32, 125)
    step_x = (code // 25 - 2).astype(f32) * 0.25
    step_y = (code // 5 % 5 - 2).astype(f32) * 0.5
    step_z = (code % 5 - 2).astype(f32) * 0.5
    zero = jnp.zeros_like(step_x)
    rows = jnp.stack([step_x, step_y, step_z, step_x, step_y, step_z, zero, zero], axis=1)
    return jnp.broadcast_to(rows[:, :, None], (125, 8, TILE))


def offset_code(step_x, row_cell, col_cell):
    step_y = jnp.clip(col_cell // SIDE - row_cell // SIDE, -2, 2)
    step_z = jnp.clip(col_cell % SIDE - row_cell % SIDE, -2, 2)
    return (step_x + 2) * 25 + (step_y + 2) * 5 + step_z + 2


def row_ids():
    return lax.broadcasted_iota(i32, (8, TILE), 0)


def split(value):
    high = value.astype(bf16).astype(f32)
    return high, value - high


def three_rows(ref, first, count):
    value = ref[:, pl.ds(pl.multiple_of(first * TILE, count * TILE), count * TILE)]
    rest = jnp.zeros((5, TILE), f32)
    return [jnp.concatenate([value[:, k * TILE : (k + 1) * TILE], rest], axis=0) for k in range(count)]


def local_coords(blocks, first, device):
    row = row_ids()
    along_x = jnp.where(row == 0, 1.0, 0.0) * (device.astype(f32) + 0.5)
    along_y = jnp.where(row == 1, 2.0, 0.0) * ((first >> 4).astype(f32) + 0.5)
    along_z = jnp.where(row == 2, 2.0, 0.0)
    fixed = along_x + along_y
    cell = (first & 15).astype(f32) + 0.5
    return [(block - (fixed + along_z * (cell + k))) * 0.25 for k, block in enumerate(blocks)]


def each_chunk(count, todo):
    def step(at, carry):
        todo(8 * at)
        return carry

    lax.fori_loop(0, count // 8, step, 0)


def column_rows(geo_refs, devices, cols_ref):
    unit = jnp.where(row_ids() == 6, 1.0, 0.0)
    for at, ref in enumerate(geo_refs):

        def fill(first):
            local = local_coords(three_rows(ref, first, 8), first, devices[at])
            rows = [block + pltpu.roll(block, 3, 0) + unit for block in local]
            cols_ref[pl.ds(at * CB + first, 8)] = jnp.stack(rows)

        each_chunk(CB, fill)
    cols_ref[len(geo_refs) * CB] = jnp.full((8, TILE), FAR, f32)


def vector_rows(refs, vec_ref, unit, places=None):
    unit = jnp.where(row_ids() == 3, unit, 0.0)
    for at, ref in enumerate(refs):

        def fill(first):
            rows = []
            for block in three_rows(ref, first, 8):
                high, low = split(block)
                rows.append(high + pltpu.roll(low, 4, 0) + unit)
            vec_ref[pl.ds((at if places is None else places[at]) * CB + first, 8)] = jnp.stack(rows)

        each_chunk(CB, fill)
    vec_ref[len(refs) * CB] = jnp.zeros((8, TILE), f32)


def row_features(geo_ref, device, rows_ref, first, count):
    row = row_ids()
    middle = (row >= 3) & (row < 6)

    def features(coords):
        norm = jnp.sum(coords * coords, axis=0, keepdims=True)
        full = jnp.where(middle, 1.0, jnp.where(row == 6, norm, -2.0 * coords))
        high, rest = split(full)
        mid, low = split(rest)
        last = jnp.where(row < 3, mid, jnp.where(middle, 1.0, low))
        return [high, high, mid, last]

    blocks = local_coords(three_rows(geo_ref, first, count), first, device)
    for k in range(0, count, 4):
        parts = []
        for j in range(4):
            parts += features(blocks[k + j])
        turned = jnp.transpose(jnp.concatenate(parts, axis=0).astype(bf16))
        for j in range(4):
            rows_ref[first + k + j] = turned if j == 0 else pltpu.roll(turned, TILE - j * PART, 1)


def tile_loop(groups, listed, rows_ref, cols_ref, table_ref, dist_ref, tile_ref, use, ahead=None, keep=None):
    row = row_ids()
    squares = (row >= 3) & (row < 6)
    unit = row == 6
    dist_ref[...] = jnp.full_like(dist_ref, FAR)
    tile_ref[...] = jnp.zeros_like(tile_ref)

    def distances(slot):
        packed = listed[slot]
        moved = cols_ref[(packed >> 8) & 2047] + table_ref[packed >> 19]
        full = jnp.where(squares, moved * moved, moved)
        high, rest = split(full)
        mid, low = split(rest)
        last = jnp.where(squares, low, jnp.where(unit, 1.0, mid))
        features = jnp.concatenate([high, mid, high, last], axis=0).astype(bf16)
        return jnp.dot(rows_ref[packed & 255][:, :PART], features, preferred_element_type=f32)

    def phi(dist_sq):
        dist_sq = jnp.maximum(dist_sq, 1e-12)
        gap = jnp.maximum(0.5 - dist_sq * lax.rsqrt(dist_sq), 0.0)
        gap_sq = gap * gap
        return gap_sq * gap_sq * (0.625 - gap)

    if keep is not None:
        stage_ref, sems, home = keep

    def copy_out(group):
        slot = lax.rem(group, RING)
        return pltpu.make_async_copy(stage_ref.at[pl.ds(slot, 1)], home(group), sems.at[slot])

    def step(at, carry):
        used = jnp.maximum(at - 2, 0) * GROUP
        first = jnp.minimum(at, groups - 1) * GROUP
        if keep is not None:
            stage = lax.rem(at + RING - 1, RING)
            before = at - 1 - RING

            @pl.when(before >= 0)
            def _():
                copy_out(before).wait()

        found = []
        for k in range(0, GROUP, 2):
            found += use(used, k, (tile_ref[k], tile_ref[k + 1]))
            for j in (k, k + 1):
                tile = phi(dist_ref[j]).astype(tile_ref.dtype)
                tile_ref[j] = tile
                if keep is not None:
                    stage_ref[stage, j] = tile
            for j in (k, k + 1):
                dist_ref[j] = distances(first + j)
        for out, block, value in found:
            out[block] += value
        if ahead is not None:
            ahead(jnp.minimum(at + 1, groups - 1) * GROUP)
        if keep is not None:

            @pl.when((at > 0) & (at <= groups))
            def _():
                copy_out(at - 1).start()

        return carry

    lax.fori_loop(0, jnp.where(groups > 0, groups + 2, 0), step, 0)
    if keep is not None:
        for back in range(1, RING):
            group = groups - back

            @pl.when(group >= 0)
            def _():
                copy_out(group).wait()


def stream_loop(pairs, home, stage_ref, sems, use):
    ring = stage_ref.shape[0]

    def copy_in(at):
        slot = lax.rem(at, ring)
        return pltpu.make_async_copy(home(2 * at, 2), stage_ref.at[slot], sems.at[slot])

    for at in range(ring - 1):

        @pl.when(at < pairs)
        def _():
            copy_in(at).start()

    def step(at, carry):
        @pl.when(at + ring - 1 < pairs)
        def _():
            copy_in(at + ring - 1).start()

        copy_in(at).wait()
        slot = lax.rem(at, ring)
        found = []
        for k in range(0, 2 * GROUP, 2):
            tile = k % GROUP
            found += use(2 * at * GROUP, k, (stage_ref[slot, k // GROUP, tile], stage_ref[slot, k // GROUP, tile + 1]))
        for out, block, value in found:
            out[block] += value
        return carry

    lax.fori_loop(0, pairs, step, 0)


def pair_body(step, me, groups, diag_list, pair_list, own_vec, right_vec, *refs):
    if step == 0:
        own_geo, right_geo, table_ref, stiff_ref, own_out, right_out, tiles = refs[:7]
        vec_ref, row_sum, col_sum, stage_ref, sems, rows_ref, cols_ref, dist_ref, tile_ref = refs[7:]
        column_rows((own_geo, right_geo), (me[0], me[0] + 1), cols_ref)
    else:
        tiles, *outs, vec_ref, row_sum, col_sum, stage_ref, sems = refs
    row = row_ids()

    vector_rows((own_vec, right_vec), vec_ref, 1.0)
    row_sum[...] = jnp.zeros_like(row_sum)
    col_sum[...] = jnp.zeros_like(col_sum)

    def two(first, second):
        return jnp.concatenate([first, second], axis=0).astype(bf16)

    def use_diag(first, k, pair):
        a, b = diag_list[first + k] & 255, diag_list[first + k + 1] & 255
        left = two(jnp.where(row == 3, 0.0, vec_ref[a]), jnp.where(row == 3, 0.0, vec_ref[b]))
        image = jnp.dot(
            left, jnp.concatenate(pair, axis=1), preferred_element_type=f32
        )
        return [(col_sum, a, image[:8, :TILE]), (col_sum, b, image[8:, TILE:])]

    def use_pair(first, k, pair):
        p, q = pair_list[first + k], pair_list[first + k + 1]
        row_a, col_a = p & 255, (p >> 8) & 2047
        row_b, col_b = q & 255, (q >> 8) & 2047
        left = two(vec_ref[row_a], vec_ref[row_b])
        if step == 2:
            left = left * 2
        image = jnp.dot(left, jnp.concatenate(pair, axis=1), preferred_element_type=f32)
        found = [(col_sum, col_a, image[:8, :TILE]), (col_sum, col_b, image[8:, TILE:])]
        if step < 2:
            image = lax.dot_general(
                two(vec_ref[col_a], vec_ref[col_b]),
                jnp.concatenate(pair, axis=0),
                (((1,), (1,)), ((), ())),
                preferred_element_type=f32,
            )
            found += [(row_sum, row_a, image[:8, :TILE]), (row_sum, row_b, image[8:, TILE:])]
        return found

    def diag_home(group, count=1):
        return tiles.at[pl.ds(group, count)]

    def pair_home(group, count=1):
        return tiles.at[pl.ds(DIAG_GROUPS + group, count)]

    if step == 0:
        loop = functools.partial(
            tile_loop, rows_ref=rows_ref, cols_ref=cols_ref, table_ref=table_ref, dist_ref=dist_ref, tile_ref=tile_ref
        )
        ahead = functools.partial(row_features, own_geo, me[0], rows_ref, count=GROUP)
        ahead(jnp.int32(0))
        loop(jnp.int32(DIAG_GROUPS), diag_list, use=use_diag, ahead=ahead, keep=(stage_ref, sems, diag_home))
        loop(groups[0], pair_list, use=use_pair, keep=(stage_ref, sems, pair_home))
    else:
        stream_loop(jnp.int32(DIAG_GROUPS // 2), diag_home, stage_ref, sems, use_diag)
        stream_loop(lax.div(groups[0], 2), pair_home, stage_ref, sems, use_pair)

    def fold(value):
        return value + pltpu.roll(value, 4, 0)

    if step < 2:
        images = (own_out, right_out) if step == 0 else outs

        def finish(first):
            place = pl.ds(pl.multiple_of(first * TILE, 8 * TILE), 8 * TILE)
            own, right = row_sum[pl.ds(first, 8)] + col_sum[pl.ds(first, 8)], col_sum[pl.ds(CB + first, 8)]
            own = jnp.concatenate([fold(own[k])[:4] for k in range(8)], axis=1)
            if step == 0:
                fourth = lax.broadcasted_iota(i32, own.shape, 0) == 3
                own = own + jnp.where(fourth, stiff_ref[:, place] - SHIFT, 0.0)
            images[0][:, place] = own
            images[1][:, place] = jnp.concatenate([fold(right[k])[:4] for k in range(8)], axis=1)

        each_chunk(CB, finish)
    else:
        quad_out = outs[0]

        def finish(at, sums):
            return tuple(
                total + fold(col_sum[8 * at + k]) * fold(vec_ref[8 * at + k]) for k, total in enumerate(sums)
            )

        zero = jnp.zeros((8, TILE), f32)
        sums = lax.fori_loop(0, 2 * CB // 8, finish, (zero,) * 8)
        quad_out[...] = sum(sums)


def pair_call(step, *arrays, me, groups, diag_list, pair_list):
    smem = pl.BlockSpec(memory_space=pltpu.SMEM)
    vmem = pl.BlockSpec(memory_space=pltpu.VMEM)
    some = pl.BlockSpec(memory_space=pl.ANY)
    image = jax.ShapeDtypeStruct((4, CB * TILE), f32)
    kept = jax.ShapeDtypeStruct((DIAG_GROUPS + PAIR_GROUPS, GROUP, TILE, TILE), bf16)
    scratch = [
        pltpu.VMEM((2 * CB + 1, 8, TILE), f32),
        pltpu.VMEM((CB, 8, TILE), f32),
        pltpu.VMEM((2 * CB + 1, 8, TILE), f32),
        pltpu.VMEM((RING, GROUP, TILE, TILE) if step == 0 else (RING // 2, 2, GROUP, TILE, TILE), bf16),
        pltpu.SemaphoreType.DMA((RING,)),
    ]
    if step == 0:
        scratch += [
            pltpu.VMEM((CB, TILE, TILE), bf16),
            pltpu.VMEM((2 * CB + 1, 8, TILE), f32),
            pltpu.VMEM((GROUP, TILE, TILE), f32),
            pltpu.VMEM((GROUP, TILE, TILE), bf16),
        ]
    return pl.pallas_call(
        functools.partial(pair_body, step),
        out_shape=((image, image, kept), (image, image), (jax.ShapeDtypeStruct((8, TILE), f32),))[step],
        in_specs=[smem] * 4 + [vmem] * (len(arrays) - 1) + [vmem if step == 0 else some],
        out_specs=((vmem, vmem, some), (vmem, vmem), (vmem,))[step],
        scratch_shapes=scratch,
        compiler_params=pltpu.CompilerParams(vmem_limit_bytes=48 * 2**20),
        cost_estimate=pl.CostEstimate(flops=2 * 10**9, bytes_accessed=10**8, transcendentals=0),
        name=f"pair_tiles_{step}",
    )(me, groups, diag_list, pair_list, *arrays)


def volume_body(me, groups, vol_list, vol_geo, *refs):
    geos, coefs = refs[:5], refs[5:10]
    table_ref, out, rows_ref, cols_ref, coef_ref, sums, dist_ref, tile_ref = refs[10:]
    column_rows(geos, [me[0] + k for k in range(-2, 3)], cols_ref)
    odd = lax.rem(me[0], 2)
    vector_rows(coefs, coef_ref, 0.0, [jnp.where(odd == 1, 4 - k, k) for k in range(5)])
    sums[...] = jnp.zeros_like(sums)

    def features(at, carry):
        row_features(vol_geo, me[0], rows_ref, at * 16, 16)
        return carry

    lax.fori_loop(0, VB // 16, features, 0)

    def use(first, k, pair):
        dims = (((1,), (1,)), ((), ()))
        p, q = vol_list[first + k], vol_list[first + k + 1]
        left = jnp.concatenate([coef_ref[(p >> 8) & 2047], coef_ref[(q >> 8) & 2047]], axis=0).astype(bf16)
        highs, lows = [], []
        for tile in pair:
            high = tile.astype(bf16)
            highs.append(high)
            lows.append((tile - high.astype(f32)).astype(bf16))
        image = lax.dot_general(left, jnp.concatenate(highs, axis=0), dims, preferred_element_type=f32)
        image += lax.dot_general(left, jnp.concatenate(lows, axis=0), dims, preferred_element_type=f32)
        return [(sums, p & 255, image[:8, :TILE]), (sums, q & 255, image[8:, TILE:])]

    tile_loop(groups[0], vol_list, rows_ref, cols_ref, table_ref, dist_ref, tile_ref, use)

    def finish(first):
        value = sums[pl.ds(first, 8)]
        rows = [(value[k] + pltpu.roll(value[k], 4, 0))[:3] for k in range(8)]
        out[:, pl.ds(pl.multiple_of(first * TILE, 8 * TILE), 8 * TILE)] = jnp.concatenate(rows, axis=1) * TILE**0.5

    each_chunk(VB, finish)


def volume_call(me, groups, vol_list, *arrays):
    smem = pl.BlockSpec(memory_space=pltpu.SMEM)
    vmem = pl.BlockSpec(memory_space=pltpu.VMEM)
    return pl.pallas_call(
        volume_body,
        out_shape=jax.ShapeDtypeStruct((3, VB * TILE), f32),
        in_specs=[smem] * 3 + [vmem] * len(arrays),
        out_specs=vmem,
        scratch_shapes=[
            pltpu.VMEM((VB, TILE, TILE), bf16),
            pltpu.VMEM((5 * CB + 1, 8, TILE), f32),
            pltpu.VMEM((5 * CB + 1, 8, TILE), f32),
            pltpu.VMEM((VB, 8, TILE), f32),
            pltpu.VMEM((GROUP, TILE, TILE), f32),
            pltpu.VMEM((GROUP, TILE, TILE), f32),
        ],
        compiler_params=pltpu.CompilerParams(vmem_limit_bytes=56 * 2**20),
        cost_estimate=pl.CostEstimate(flops=2 * 10**9, bytes_accessed=10**8, transcendentals=0),
        name="volume_tiles",
    )(me, groups, vol_list, *arrays)


def cg_weights(moment):
    def gram(first, second):
        return sum(a * b * moment[i + j] for i, a in enumerate(first) for j, b in enumerate(second))

    def image(vector):
        grown = [SHIFT * a for a in vector] + [0.0]
        return [a + (vector[k - 1] if k else 0.0) for k, a in enumerate(grown)]

    def axpy(scale, first, second):
        size = max(len(first), len(second))
        pad = lambda v: list(v) + [0.0] * (size - len(v))
        return [scale * a + b for a, b in zip(pad(first), pad(second))]

    one = jnp.ones_like(moment[0])
    residual, direction, total = [one], [one], [0.0 * one]
    norm = gram(residual, residual)
    for step in range(3):
        grown = image(direction)
        length = norm / gram(direction, grown)
        total = axpy(length, direction, total)
        if step < 2:
            residual = axpy(-length, grown, residual)
            norm_next = gram(residual, residual)
            direction = axpy(norm_next / norm, direction, residual)
            norm = norm_next
    return total


def comp_sum(first, second):
    return jnp.sum(first * second, axis=1)


def body(ctrl_points, ctrl_disp, stiffness, pair_rows, pair_cols, pair_count, vol_points, vol_rows, vol_cols, vol_count):
    me = lax.axis_index("nodes")
    devices = lax.axis_size("nodes")
    order = (2, 1, 0, -1, -2)

    geo = {0: ctrl_points, -1: from_behind(ctrl_points, "nodes", -1)}
    beside = from_behind(ctrl_disp, "nodes", -1)
    later, beside = lax.optimization_barrier((ctrl_points, beside))
    for offset in (1, 2, -2):
        geo[offset] = from_behind(later, "nodes", offset)
    table = offset_table()

    slots = lax.iota(i32, MAXT)
    right = pair_cols >= CB
    live = (slots < pair_count[0]) & (~right | (me < devices - 1))
    code = offset_code(right.astype(i32), pair_rows, pair_cols % CB)
    pair_list = jnp.where(live, pair_rows | (pair_cols << 8) | (code << 19), (2 * CB) << 8)
    pair_groups = (pair_count + 2 * GROUP - 1) // (2 * GROUP) * 2
    own = lax.iota(i32, CB)
    diag_list = own | (own << 8) | (62 << 19)

    slots = lax.iota(i32, MAXV)
    step_x = vol_cols // CB - 2
    source = me + step_x
    live = (slots < vol_count[0]) & (source >= 0) & (source < devices)
    code = offset_code(step_x, vol_rows, vol_cols % CB)
    vol_list = jnp.where(live, vol_rows | (vol_cols << 8) | (code << 19), (5 * CB) << 8)
    vol_groups = (vol_count + GROUP - 1) // GROUP
    here = me.astype(i32)[None]

    images = functools.partial(pair_call, me=here, groups=pair_groups, diag_list=diag_list, pair_list=pair_list)

    def exchanged(own_part, right_part):
        back = from_behind(right_part, "nodes", 1)
        ahead = from_behind(own_part, "nodes", -1)
        return own_part + back, ahead + right_part

    own_part, right_part, tiles = images(0, ctrl_disp, beside, geo[0], geo[-1], table, stiffness[None, :])
    own_part, right_part, geo[1], geo[2], geo[-2] = lax.optimization_barrier(
        (own_part, right_part, geo[1], geo[2], geo[-2])
    )
    total, total_beside = exchanged(own_part, right_part)
    diagonal, diagonal_beside = total[3:4], total_beside[3:4]
    first = total[:3] + diagonal * ctrl_disp
    first_beside = total_beside[:3] + diagonal_beside * beside
    total, total_beside = exchanged(*images(1, first, first_beside, tiles))
    second = total[:3] + diagonal * first
    second_beside = total_beside[:3] + diagonal_beside * first_beside
    (quad,) = images(2, second, second_beside, tiles)
    moments = jnp.concatenate(
        [
            comp_sum(ctrl_disp, ctrl_disp),
            comp_sum(ctrl_disp, first),
            comp_sum(first, first),
            comp_sum(first, second),
            comp_sum(second, second),
            jnp.sum(quad, axis=1)[:3] + comp_sum(diagonal * second, second),
            jnp.zeros((TILE - 18,), f32),
        ]
    )

    sent = jnp.broadcast_to(moments[None, None, :], (devices, 1, TILE))
    moments = jnp.sum(lax.all_to_all(sent, "nodes", 0, 0, tiled=True), axis=(0, 1))
    weights = cg_weights([moments[3 * k : 3 * k + 3] for k in range(6)])
    coef = sum(w[:, None] * u for w, u in zip(weights, (ctrl_disp, first, second)))
    near = around(coef, "nodes")
    moved = volume_call(here, vol_groups, vol_list, vol_points, *[geo[k] for k in order], *near, table)
    return (coef, moved)


def solution(mesh):
    across = P(None, "nodes")
    flat = P("nodes")
    return jax.shard_map(
        body,
        mesh=mesh,
        in_specs=(across, across, flat, flat, flat, flat, across, flat, flat, flat),
        out_specs=(across, across),
        check_vma=False,
    )
```

```python
import functools

import jax
import jax.numpy as jnp
from jax import lax
from jax.experimental import pallas as pl
from jax.experimental.pallas import tpu as pltpu
from jax.sharding import PartitionSpec as P

TILE = 128
SIDE = 16
CB = 256
VB = 256
MAXT = 768
MAXV = 512
GROUP = 16
PART = 32
RING = 8
DIAG_GROUPS = CB // GROUP
PAIR_GROUPS = MAXT // GROUP
SHIFT = 0.75
FAR = 64.0

f32 = jnp.float32
bf16 = jnp.bfloat16
i32 = jnp.int32


def from_behind(block, axis, distance):
    devices = range(lax.axis_size(axis))
    route = [(i - distance, i) for i in devices if i - distance in devices]
    return lax.ppermute(block, axis, route)


def around(block, axis):
    devices = range(lax.axis_size(axis))

    def send(value, target):
        return lax.ppermute(value, axis, [(i, target(i)) for i in devices if target(i) in devices])

    far = send(block, lambda i: i - 2 if i % 2 else i + 2)
    near = send(block, lambda i: i + 1 if i % 2 else i - 1)
    partner = send(block, lambda i: i ^ 1)
    shared = send(near, lambda i: i ^ 1)
    return [far, near, block, partner, shared]


def offset_table():
    code = lax.iota(i32, 125)
    step_x = (code // 25 - 2).astype(f32) * 0.25
    step_y = (code // 5 % 5 - 2).astype(f32) * 0.5
    step_z = (code % 5 - 2).astype(f32) * 0.5
    zero = jnp.zeros_like(step_x)
    rows = jnp.stack([step_x, step_y, step_z, step_x, step_y, step_z, zero, zero], axis=1)
    return jnp.broadcast_to(rows[:, :, None], (125, 8, TILE))


def offset_code(step_x, row_cell, col_cell):
    step_y = jnp.clip(col_cell // SIDE - row_cell // SIDE, -2, 2)
    step_z = jnp.clip(col_cell % SIDE - row_cell % SIDE, -2, 2)
    return (step_x + 2) * 25 + (step_y + 2) * 5 + step_z + 2


def row_ids():
    return lax.broadcasted_iota(i32, (8, TILE), 0)


def split(value):
    high = value.astype(bf16).astype(f32)
    return high, value - high


def three_rows(ref, first, count):
    value = ref[:, pl.ds(pl.multiple_of(first * TILE, count * TILE), count * TILE)]
    rest = jnp.zeros((5, TILE), f32)
    return [jnp.concatenate([value[:, k * TILE : (k + 1) * TILE], rest], axis=0) for k in range(count)]


def local_coords(blocks, first, device):
    row = row_ids()
    along_x = jnp.where(row == 0, 1.0, 0.0) * (device.astype(f32) + 0.5)
    along_y = jnp.where(row == 1, 2.0, 0.0) * ((first >> 4).astype(f32) + 0.5)
    along_z = jnp.where(row == 2, 2.0, 0.0)
    fixed = along_x + along_y
    cell = (first & 15).astype(f32) + 0.5
    return [(block - (fixed + along_z * (cell + k))) * 0.25 for k, block in enumerate(blocks)]


def each_chunk(count, todo):
    def step(at, carry):
        todo(8 * at)
        return carry

    lax.fori_loop(0, count // 8, step, 0)


def column_rows(geo_refs, devices, cols_ref):
    unit = jnp.where(row_ids() == 6, 1.0, 0.0)
    for at, ref in enumerate(geo_refs):

        def fill(first):
            local = local_coords(three_rows(ref, first, 8), first, devices[at])
            rows = [block + pltpu.roll(block, 3, 0) + unit for block in local]
            cols_ref[pl.ds(at * CB + first, 8)] = jnp.stack(rows)

        each_chunk(CB, fill)
    cols_ref[len(geo_refs) * CB] = jnp.full((8, TILE), FAR, f32)


def vector_rows(refs, vec_ref, unit, places=None):
    unit = jnp.where(row_ids() == 3, unit, 0.0)
    for at, ref in enumerate(refs):

        def fill(first):
            rows = []
            for block in three_rows(ref, first, 8):
                high, low = split(block)
                rows.append(high + pltpu.roll(low, 4, 0) + unit)
            vec_ref[pl.ds((at if places is None else places[at]) * CB + first, 8)] = jnp.stack(rows)

        each_chunk(CB, fill)
    vec_ref[len(refs) * CB] = jnp.zeros((8, TILE), f32)


def row_features(geo_ref, device, rows_ref, first, count):
    row = row_ids()
    middle = (row >= 3) & (row < 6)

    def features(coords):
        norm = jnp.sum(coords * coords, axis=0, keepdims=True)
        full = jnp.where(middle, 1.0, jnp.where(row == 6, norm, -2.0 * coords))
        high, rest = split(full)
        mid, low = split(rest)
        last = jnp.where(row < 3, mid, jnp.where(middle, 1.0, low))
        return [high, high, mid, last]

    blocks = local_coords(three_rows(geo_ref, first, count), first, device)
    for k in range(0, count, 4):
        parts = []
        for j in range(4):
            parts += features(blocks[k + j])
        turned = jnp.transpose(jnp.concatenate(parts, axis=0).astype(bf16))
        for j in range(4):
            rows_ref[first + k + j] = turned if j == 0 else pltpu.roll(turned, TILE - j * PART, 1)


def tile_loop(groups, listed, rows_ref, cols_ref, table_ref, dist_ref, tile_ref, use, ahead=None, keep=None):
    row = row_ids()
    squares = (row >= 3) & (row < 6)
    unit = row == 6
    dist_ref[...] = jnp.full_like(dist_ref, FAR)
    tile_ref[...] = jnp.zeros_like(tile_ref)

    def distances(slot):
        packed = listed[slot]
        moved = cols_ref[(packed >> 8) & 2047] + table_ref[packed >> 19]
        full = jnp.where(squares, moved * moved, moved)
        high, rest = split(full)
        mid, low = split(rest)
        last = jnp.where(squares, low, jnp.where(unit, 1.0, mid))
        features = jnp.concatenate([high, mid, high, last], axis=0).astype(bf16)
        return jnp.dot(rows_ref[packed & 255][:, :PART], features, preferred_element_type=f32)

    def phi(dist_sq):
        dist_sq = jnp.maximum(dist_sq, 1e-12)
        gap = jnp.maximum(0.5 - dist_sq * lax.rsqrt(dist_sq), 0.0)
        gap_sq = gap * gap
        return gap_sq * gap_sq * (0.625 - gap)

    if keep is not None:
        stage_ref, sems, home = keep

    def copy_out(group):
        slot = lax.rem(group, RING)
        return pltpu.make_async_copy(stage_ref.at[pl.ds(slot, 1)], home(group), sems.at[slot])

    def step(at, carry):
        used = jnp.maximum(at - 2, 0) * GROUP
        first = jnp.minimum(at, groups - 1) * GROUP
        if keep is not None:
            stage = lax.rem(at + RING - 1, RING)
            before = at - 1 - RING

            @pl.when(before >= 0)
            def _():
                copy_out(before).wait()

        found = []
        for k in range(0, GROUP, 2):
            found += use(used, k, (tile_ref[k], tile_ref[k + 1]))
            for j in (k, k + 1):
                tile = phi(dist_ref[j]).astype(tile_ref.dtype)
                tile_ref[j] = tile
                if keep is not None:
                    stage_ref[stage, j] = tile
            for j in (k, k + 1):
                dist_ref[j] = distances(first + j)
        for out, block, value in found:
            out[block] += value
        if ahead is not None:
            ahead(jnp.minimum(at + 1, groups - 1) * GROUP)
        if keep is not None:

            @pl.when((at > 0) & (at <= groups))
            def _():
                copy_out(at - 1).start()

        return carry

    lax.fori_loop(0, jnp.where(groups > 0, groups + 2, 0), step, 0)
    if keep is not None:
        for back in range(1, RING):
            group = groups - back

            @pl.when(group >= 0)
            def _():
                copy_out(group).wait()


def stream_loop(pairs, home, stage_ref, sems, use):
    ring = stage_ref.shape[0]

    def copy_in(at):
        slot = lax.rem(at, ring)
        return pltpu.make_async_copy(home(2 * at, 2), stage_ref.at[slot], sems.at[slot])

    for at in range(ring - 1):

        @pl.when(at < pairs)
        def _():
            copy_in(at).start()

    def step(at, carry):
        @pl.when(at + ring - 1 < pairs)
        def _():
            copy_in(at + ring - 1).start()

        copy_in(at).wait()
        slot = lax.rem(at, ring)
        found = []
        for k in range(0, 2 * GROUP, 2):
            tile = k % GROUP
            found += use(2 * at * GROUP, k, (stage_ref[slot, k // GROUP, tile], stage_ref[slot, k // GROUP, tile + 1]))
        for out, block, value in found:
            out[block] += value
        return carry

    lax.fori_loop(0, pairs, step, 0)


def pair_body(step, me, groups, diag_list, pair_list, *refs):
    row = row_ids()
    own = functools.partial(row_features, device=me[0], count=GROUP)
    if step == "diag":
        own_vec, own_geo, table_ref, stiff_ref, own_out, diag_tiles = refs[:6]
        vec_ref, row_sum, col_sum, stage_ref, sems, rows_ref, cols_ref, dist_ref, tile_ref = refs[6:]
        column_rows((own_geo,), (me[0],), cols_ref)
        vector_rows((own_vec,), vec_ref, 1.0)
    elif step == "pairs":
        own_vec, right_vec, own_geo, right_geo, table_ref, diag_ref, own_out, right_out, pair_tiles = refs[:9]
        vec_ref, row_sum, col_sum, stage_ref, sems, rows_ref, cols_ref, dist_ref, tile_ref = refs[9:]
        column_rows((own_geo, right_geo), (me[0], me[0] + 1), cols_ref)
        vector_rows((own_vec, right_vec), vec_ref, 1.0)
    else:
        own_vec, right_vec, diag_tiles, pair_tiles, *outs, vec_ref, row_sum, col_sum, stage_ref, sems = refs
        vector_rows((own_vec, right_vec), vec_ref, 1.0)
    row_sum[...] = jnp.zeros_like(row_sum)
    col_sum[...] = jnp.zeros_like(col_sum)

    def two(first, second):
        return jnp.concatenate([first, second], axis=0).astype(bf16)

    def use_diag(first, k, pair):
        a, b = diag_list[first + k] & 255, diag_list[first + k + 1] & 255
        left = two(jnp.where(row == 3, 0.0, vec_ref[a]), jnp.where(row == 3, 0.0, vec_ref[b]))
        image = jnp.dot(
            left, jnp.concatenate(pair, axis=1), preferred_element_type=f32
        )
        return [(col_sum, a, image[:8, :TILE]), (col_sum, b, image[8:, TILE:])]

    def use_pair(first, k, pair):
        p, q = pair_list[first + k], pair_list[first + k + 1]
        row_a, col_a = p & 255, (p >> 8) & 2047
        row_b, col_b = q & 255, (q >> 8) & 2047
        left = two(vec_ref[row_a], vec_ref[row_b])
        if step == 2:
            left = left * 2
        image = jnp.dot(left, jnp.concatenate(pair, axis=1), preferred_element_type=f32)
        found = [(col_sum, col_a, image[:8, :TILE]), (col_sum, col_b, image[8:, TILE:])]
        if step != 2:
            image = lax.dot_general(
                two(vec_ref[col_a], vec_ref[col_b]),
                jnp.concatenate(pair, axis=0),
                (((1,), (1,)), ((), ())),
                preferred_element_type=f32,
            )
            found += [(row_sum, row_a, image[:8, :TILE]), (row_sum, row_b, image[8:, TILE:])]
        return found

    def diag_home(group, count=1):
        return diag_tiles.at[pl.ds(group, count)]

    def pair_home(group, count=1):
        return pair_tiles.at[pl.ds(group, count)]

    if step in ("diag", "pairs"):
        loop = functools.partial(
            tile_loop, rows_ref=rows_ref, cols_ref=cols_ref, table_ref=table_ref, dist_ref=dist_ref, tile_ref=tile_ref
        )

        def features(at, carry):
            own(own_geo, rows_ref=rows_ref, first=at * GROUP)
            return carry

        if step == "diag":
            features(jnp.int32(0), 0)
            loop(
                jnp.int32(DIAG_GROUPS),
                diag_list,
                use=use_diag,
                ahead=lambda first: own(own_geo, rows_ref=rows_ref, first=first),
                keep=(stage_ref, sems, diag_home),
            )
        else:
            lax.fori_loop(0, DIAG_GROUPS, features, 0)
            loop(groups[0], pair_list, use=use_pair, keep=(stage_ref, sems, pair_home))
    else:
        stream_loop(jnp.int32(DIAG_GROUPS // 2), diag_home, stage_ref, sems, use_diag)
        stream_loop(lax.div(groups[0], 2), pair_home, stage_ref, sems, use_pair)

    def fold(value):
        return value + pltpu.roll(value, 4, 0)

    if step != 2:
        if step == "diag":
            images = (own_out,)
        else:
            images = (own_out, right_out) if step == "pairs" else outs

        def finish(first):
            place = pl.ds(pl.multiple_of(first * TILE, 8 * TILE), 8 * TILE)
            sums = row_sum[pl.ds(first, 8)] + col_sum[pl.ds(first, 8)]
            image = jnp.concatenate([fold(sums[k])[:4] for k in range(8)], axis=1)
            if step == "diag":
                fourth = lax.broadcasted_iota(i32, image.shape, 0) == 3
                image = image + jnp.where(fourth, stiff_ref[:, place] - SHIFT, 0.0)
            elif step == "pairs":
                image = image + diag_ref[:, place]
            images[0][:, place] = image
            if step != "diag":
                sums = col_sum[pl.ds(CB + first, 8)]
                images[1][:, place] = jnp.concatenate([fold(sums[k])[:4] for k in range(8)], axis=1)

        each_chunk(CB, finish)
    else:
        quad_out = outs[0]

        def finish(at, sums):
            return tuple(
                total + fold(col_sum[8 * at + k]) * fold(vec_ref[8 * at + k]) for k, total in enumerate(sums)
            )

        zero = jnp.zeros((8, TILE), f32)
        sums = lax.fori_loop(0, 2 * CB // 8, finish, (zero,) * 8)
        quad_out[...] = sum(sums)


def pair_call(step, *arrays, me, groups, diag_list, pair_list):
    smem = pl.BlockSpec(memory_space=pltpu.SMEM)
    vmem = pl.BlockSpec(memory_space=pltpu.VMEM)
    some = pl.BlockSpec(memory_space=pl.ANY)
    image = (jax.ShapeDtypeStruct((4, CB * TILE), f32), vmem)
    out = {
        "diag": (image, (jax.ShapeDtypeStruct((DIAG_GROUPS, GROUP, TILE, TILE), bf16), some)),
        "pairs": (image, image, (jax.ShapeDtypeStruct((PAIR_GROUPS, GROUP, TILE, TILE), bf16), some)),
        1: (image, image),
        2: ((jax.ShapeDtypeStruct((8, TILE), f32), vmem),),
    }[step]
    first = step in ("diag", "pairs")
    blocks = (1 if step == "diag" else 2) * CB + 1
    scratch = [
        pltpu.VMEM((blocks, 8, TILE), f32),
        pltpu.VMEM((CB, 8, TILE), f32),
        pltpu.VMEM((blocks, 8, TILE), f32),
        pltpu.VMEM((RING, GROUP, TILE, TILE) if first else (RING // 2, 2, GROUP, TILE, TILE), bf16),
        pltpu.SemaphoreType.DMA((RING,)),
    ]
    if first:
        scratch += [
            pltpu.VMEM((CB, TILE, TILE), bf16),
            pltpu.VMEM((blocks, 8, TILE), f32),
            pltpu.VMEM((GROUP, TILE, TILE), f32),
            pltpu.VMEM((GROUP, TILE, TILE), bf16),
        ]
    return pl.pallas_call(
        functools.partial(pair_body, step),
        out_shape=tuple(shape for shape, _ in out),
        in_specs=[smem] * 4 + ([vmem] * len(arrays) if first else [vmem, vmem, some, some]),
        out_specs=tuple(spec for _, spec in out),
        scratch_shapes=scratch,
        compiler_params=pltpu.CompilerParams(vmem_limit_bytes=48 * 2**20),
        cost_estimate=pl.CostEstimate(flops=2 * 10**9, bytes_accessed=10**8, transcendentals=0),
        name=f"pair_tiles_{step}",
    )(me, groups, diag_list, pair_list, *arrays)


def volume_body(me, groups, vol_list, vol_geo, *refs):
    geos, coefs = refs[:5], refs[5:10]
    table_ref, out, rows_ref, cols_ref, coef_ref, sums, dist_ref, tile_ref = refs[10:]
    column_rows(geos, [me[0] + k for k in range(-2, 3)], cols_ref)
    odd = lax.rem(me[0], 2)
    vector_rows(coefs, coef_ref, 0.0, [jnp.where(odd == 1, 4 - k, k) for k in range(5)])
    sums[...] = jnp.zeros_like(sums)

    def features(at, carry):
        row_features(vol_geo, me[0], rows_ref, at * 16, 16)
        return carry

    lax.fori_loop(0, VB // 16, features, 0)

    def use(first, k, pair):
        dims = (((1,), (1,)), ((), ()))
        p, q = vol_list[first + k], vol_list[first + k + 1]
        left = jnp.concatenate([coef_ref[(p >> 8) & 2047], coef_ref[(q >> 8) & 2047]], axis=0).astype(bf16)
        highs, lows = [], []
        for tile in pair:
            high = tile.astype(bf16)
            highs.append(high)
            lows.append((tile - high.astype(f32)).astype(bf16))
        image = lax.dot_general(left, jnp.concatenate(highs, axis=0), dims, preferred_element_type=f32)
        image += lax.dot_general(left, jnp.concatenate(lows, axis=0), dims, preferred_element_type=f32)
        return [(sums, p & 255, image[:8, :TILE]), (sums, q & 255, image[8:, TILE:])]

    tile_loop(groups[0], vol_list, rows_ref, cols_ref, table_ref, dist_ref, tile_ref, use)

    def finish(first):
        value = sums[pl.ds(first, 8)]
        rows = [(value[k] + pltpu.roll(value[k], 4, 0))[:3] for k in range(8)]
        out[:, pl.ds(pl.multiple_of(first * TILE, 8 * TILE), 8 * TILE)] = jnp.concatenate(rows, axis=1) * TILE**0.5

    each_chunk(VB, finish)


def volume_call(me, groups, vol_list, *arrays):
    smem = pl.BlockSpec(memory_space=pltpu.SMEM)
    vmem = pl.BlockSpec(memory_space=pltpu.VMEM)
    return pl.pallas_call(
        volume_body,
        out_shape=jax.ShapeDtypeStruct((3, VB * TILE), f32),
        in_specs=[smem] * 3 + [vmem] * len(arrays),
        out_specs=vmem,
        scratch_shapes=[
            pltpu.VMEM((VB, TILE, TILE), bf16),
            pltpu.VMEM((5 * CB + 1, 8, TILE), f32),
            pltpu.VMEM((5 * CB + 1, 8, TILE), f32),
            pltpu.VMEM((VB, 8, TILE), f32),
            pltpu.VMEM((GROUP, TILE, TILE), f32),
            pltpu.VMEM((GROUP, TILE, TILE), f32),
        ],
        compiler_params=pltpu.CompilerParams(vmem_limit_bytes=56 * 2**20),
        cost_estimate=pl.CostEstimate(flops=2 * 10**9, bytes_accessed=10**8, transcendentals=0),
        name="volume_tiles",
    )(me, groups, vol_list, *arrays)


def cg_weights(moment):
    def gram(first, second):
        return sum(a * b * moment[i + j] for i, a in enumerate(first) for j, b in enumerate(second))

    def image(vector):
        grown = [SHIFT * a for a in vector] + [0.0]
        return [a + (vector[k - 1] if k else 0.0) for k, a in enumerate(grown)]

    def axpy(scale, first, second):
        size = max(len(first), len(second))
        pad = lambda v: list(v) + [0.0] * (size - len(v))
        return [scale * a + b for a, b in zip(pad(first), pad(second))]

    one = jnp.ones_like(moment[0])
    residual, direction, total = [one], [one], [0.0 * one]
    norm = gram(residual, residual)
    for step in range(3):
        grown = image(direction)
        length = norm / gram(direction, grown)
        total = axpy(length, direction, total)
        if step < 2:
            residual = axpy(-length, grown, residual)
            norm_next = gram(residual, residual)
            direction = axpy(norm_next / norm, direction, residual)
            norm = norm_next
    return total


def comp_sum(first, second):
    return jnp.sum(first * second, axis=1)


def body(ctrl_points, ctrl_disp, stiffness, pair_rows, pair_cols, pair_count, vol_points, vol_rows, vol_cols, vol_count):
    me = lax.axis_index("nodes")
    devices = lax.axis_size("nodes")
    order = (2, 1, 0, -1, -2)

    geo = {0: ctrl_points, -1: from_behind(ctrl_points, "nodes", -1)}
    beside = from_behind(ctrl_disp, "nodes", -1)
    table = offset_table()

    slots = lax.iota(i32, MAXT)
    right = pair_cols >= CB
    live = (slots < pair_count[0]) & (~right | (me < devices - 1))
    code = offset_code(right.astype(i32), pair_rows, pair_cols % CB)
    pair_list = jnp.where(live, pair_rows | (pair_cols << 8) | (code << 19), (2 * CB) << 8)
    pair_groups = (pair_count + 2 * GROUP - 1) // (2 * GROUP) * 2
    own = lax.iota(i32, CB)
    diag_list = own | (own << 8) | (62 << 19)

    slots = lax.iota(i32, MAXV)
    step_x = vol_cols // CB - 2
    source = me + step_x
    live = (slots < vol_count[0]) & (source >= 0) & (source < devices)
    code = offset_code(step_x, vol_rows, vol_cols % CB)
    vol_list = jnp.where(live, vol_rows | (vol_cols << 8) | (code << 19), (5 * CB) << 8)
    vol_groups = (vol_count + GROUP - 1) // GROUP
    here = me.astype(i32)[None]

    images = functools.partial(pair_call, me=here, groups=pair_groups, diag_list=diag_list, pair_list=pair_list)

    def exchanged(own_part, right_part):
        back = from_behind(right_part, "nodes", 1)
        ahead = from_behind(own_part, "nodes", -1)
        return own_part + back, ahead + right_part

    own_part, diag_tiles = images("diag", ctrl_disp, ctrl_points, table, stiffness[None, :])
    own_part, right_part, pair_tiles = images(
        "pairs", ctrl_disp, beside, ctrl_points, geo[-1], table, own_part
    )
    tiles = (diag_tiles, pair_tiles)
    total, total_beside = exchanged(own_part, right_part)
    diagonal, diagonal_beside = total[3:4], total_beside[3:4]
    first = total[:3] + diagonal * ctrl_disp
    first_beside = total_beside[:3] + diagonal_beside * beside
    later, first = lax.optimization_barrier((ctrl_points, first))
    for offset in (1, 2, -2):
        geo[offset] = from_behind(later, "nodes", offset)
    own_part, right_part = images(1, first, first_beside, *tiles)
    own_part, right_part, geo[1], geo[2], geo[-2] = lax.optimization_barrier(
        (own_part, right_part, geo[1], geo[2], geo[-2])
    )
    total, total_beside = exchanged(own_part, right_part)
    second = total[:3] + diagonal * first
    second_beside = total_beside[:3] + diagonal_beside * first_beside
    (quad,) = images(2, second, second_beside, *tiles)
    moments = jnp.concatenate(
        [
            comp_sum(ctrl_disp, ctrl_disp),
            comp_sum(ctrl_disp, first),
            comp_sum(first, first),
            comp_sum(first, second),
            comp_sum(second, second),
            jnp.sum(quad, axis=1)[:3] + comp_sum(diagonal * second, second),
            jnp.zeros((TILE - 18,), f32),
        ]
    )

    sent = jnp.broadcast_to(moments[None, None, :], (devices, 1, TILE))
    moments = jnp.sum(lax.all_to_all(sent, "nodes", 0, 0, tiled=True), axis=(0, 1))
    weights = cg_weights([moments[3 * k : 3 * k + 3] for k in range(6)])
    coef = sum(w[:, None] * u for w, u in zip(weights, (ctrl_disp, first, second)))
    near = around(coef, "nodes")
    moved = volume_call(here, vol_groups, vol_list, vol_points, *[geo[k] for k in order], *near, table)
    return (coef, moved)


def solution(mesh):
    across = P(None, "nodes")
    flat = P("nodes")
    return jax.shard_map(
        body,
        mesh=mesh,
        in_specs=(across, across, flat, flat, flat, flat, across, flat, flat, flat),
        out_specs=(across, across),
        check_vma=False,
    )
```

```python
import functools

import jax
import jax.numpy as jnp
from jax import lax
from jax.experimental import pallas as pl
from jax.experimental.pallas import tpu as pltpu
from jax.sharding import PartitionSpec as P

TILE = 128
SIDE = 16
CB = 256
VB = 256
MAXT = 768
MAXV = 512
GROUP = 16
PART = 32
RING = 8
EIGHT = 8
DIAG_GROUPS = CB // GROUP
PAIR_GROUPS = MAXT // GROUP
SHIFT = 0.75
FAR = 64.0

f32 = jnp.float32
bf16 = jnp.bfloat16
i32 = jnp.int32


def from_behind(block, axis, distance):
    devices = range(lax.axis_size(axis))
    route = [(i - distance, i) for i in devices if i - distance in devices]
    return lax.ppermute(block, axis, route)


def around(block, axis):
    devices = range(lax.axis_size(axis))

    def send(value, target):
        return lax.ppermute(value, axis, [(i, target(i)) for i in devices if target(i) in devices])

    far = send(block, lambda i: i - 2 if i % 2 else i + 2)
    near = send(block, lambda i: i + 1 if i % 2 else i - 1)
    partner = send(block, lambda i: i ^ 1)
    shared = send(near, lambda i: i ^ 1)
    return [far, near, block, partner, shared]


def gathered_eights(block, axis, shift):
    size = lax.axis_size(axis)
    groups = [[(EIGHT * g + shift + k) % size for k in range(EIGHT)] for g in range(size // EIGHT)]
    return lax.all_gather(block, axis, axis_index_groups=groups)


def offset_table():
    code = lax.iota(i32, 125)
    step_x = (code // 25 - 2).astype(f32) * 0.25
    step_y = (code // 5 % 5 - 2).astype(f32) * 0.5
    step_z = (code % 5 - 2).astype(f32) * 0.5
    zero = jnp.zeros_like(step_x)
    rows = jnp.stack([step_x, step_y, step_z, step_x, step_y, step_z, zero, zero], axis=1)
    return jnp.broadcast_to(rows[:, :, None], (125, 8, TILE))


def offset_code(step_x, row_cell, col_cell):
    step_y = jnp.clip(col_cell // SIDE - row_cell // SIDE, -2, 2)
    step_z = jnp.clip(col_cell % SIDE - row_cell % SIDE, -2, 2)
    return (step_x + 2) * 25 + (step_y + 2) * 5 + step_z + 2


def row_ids():
    return lax.broadcasted_iota(i32, (8, TILE), 0)


def split(value):
    high = value.astype(bf16).astype(f32)
    return high, value - high


def three_rows(ref, first, count):
    value = ref[:, pl.ds(pl.multiple_of(first * TILE, count * TILE), count * TILE)]
    rest = jnp.zeros((5, TILE), f32)
    return [jnp.concatenate([value[:, k * TILE : (k + 1) * TILE], rest], axis=0) for k in range(count)]


def local_coords(blocks, first, device):
    row = row_ids()
    along_x = jnp.where(row == 0, 1.0, 0.0) * (device.astype(f32) + 0.5)
    along_y = jnp.where(row == 1, 2.0, 0.0) * ((first >> 4).astype(f32) + 0.5)
    along_z = jnp.where(row == 2, 2.0, 0.0)
    fixed = along_x + along_y
    cell = (first & 15).astype(f32) + 0.5
    return [(block - (fixed + along_z * (cell + k))) * 0.25 for k, block in enumerate(blocks)]


def each_chunk(count, todo):
    def step(at, carry):
        todo(8 * at)
        return carry

    lax.fori_loop(0, count // 8, step, 0)


def column_rows(geo_refs, devices, cols_ref):
    unit = jnp.where(row_ids() == 6, 1.0, 0.0)
    for at, ref in enumerate(geo_refs):

        def fill(first):
            local = local_coords(three_rows(ref, first, 8), first, devices[at])
            rows = [block + pltpu.roll(block, 3, 0) + unit for block in local]
            cols_ref[pl.ds(at * CB + first, 8)] = jnp.stack(rows)

        each_chunk(CB, fill)
    cols_ref[len(geo_refs) * CB] = jnp.full((8, TILE), FAR, f32)


def vector_rows(refs, vec_ref, unit, places=None):
    unit = jnp.where(row_ids() == 3, unit, 0.0)
    for at, ref in enumerate(refs):

        def fill(first):
            rows = []
            for block in three_rows(ref, first, 8):
                high, low = split(block)
                rows.append(high + pltpu.roll(low, 4, 0) + unit)
            vec_ref[pl.ds((at if places is None else places[at]) * CB + first, 8)] = jnp.stack(rows)

        each_chunk(CB, fill)
    vec_ref[len(refs) * CB] = jnp.zeros((8, TILE), f32)


def row_features(geo_ref, device, rows_ref, first, count):
    row = row_ids()
    middle = (row >= 3) & (row < 6)

    def features(coords):
        norm = jnp.sum(coords * coords, axis=0, keepdims=True)
        full = jnp.where(middle, 1.0, jnp.where(row == 6, norm, -2.0 * coords))
        high, rest = split(full)
        mid, low = split(rest)
        last = jnp.where(row < 3, mid, jnp.where(middle, 1.0, low))
        return [high, high, mid, last]

    blocks = local_coords(three_rows(geo_ref, first, count), first, device)
    for k in range(0, count, 4):
        parts = []
        for j in range(4):
            parts += features(blocks[k + j])
        turned = jnp.transpose(jnp.concatenate(parts, axis=0).astype(bf16))
        for j in range(4):
            rows_ref[first + k + j] = turned if j == 0 else pltpu.roll(turned, TILE - j * PART, 1)


def tile_loop(groups, listed, rows_ref, cols_ref, table_ref, dist_ref, tile_ref, use, ahead=None, keep=None):
    row = row_ids()
    squares = (row >= 3) & (row < 6)
    unit = row == 6
    dist_ref[...] = jnp.full_like(dist_ref, FAR)
    tile_ref[...] = jnp.zeros_like(tile_ref)

    def distances(slot):
        packed = listed[slot]
        moved = cols_ref[(packed >> 8) & 2047] + table_ref[packed >> 19]
        full = jnp.where(squares, moved * moved, moved)
        high, rest = split(full)
        mid, low = split(rest)
        last = jnp.where(squares, low, jnp.where(unit, 1.0, mid))
        features = jnp.concatenate([high, mid, high, last], axis=0).astype(bf16)
        return jnp.dot(rows_ref[packed & 255][:, :PART], features, preferred_element_type=f32)

    def phi(dist_sq):
        dist_sq = jnp.maximum(dist_sq, 1e-12)
        gap = jnp.maximum(0.5 - dist_sq * lax.rsqrt(dist_sq), 0.0)
        gap_sq = gap * gap
        return gap_sq * gap_sq * (0.625 - gap)

    if keep is not None:
        stage_ref, sems, home = keep

    def copy_out(group):
        slot = lax.rem(group, RING)
        return pltpu.make_async_copy(stage_ref.at[pl.ds(slot, 1)], home(group), sems.at[slot])

    def step(at, carry):
        used = jnp.maximum(at - 2, 0) * GROUP
        first = jnp.minimum(at, groups - 1) * GROUP
        if keep is not None:
            stage = lax.rem(at + RING - 1, RING)
            before = at - 1 - RING

            @pl.when(before >= 0)
            def _():
                copy_out(before).wait()

        found = []
        for k in range(0, GROUP, 2):
            found += use(used, k, (tile_ref[k], tile_ref[k + 1]))
            for j in (k, k + 1):
                tile = phi(dist_ref[j]).astype(tile_ref.dtype)
                tile_ref[j] = tile
                if keep is not None:
                    stage_ref[stage, j] = tile
            for j in (k, k + 1):
                dist_ref[j] = distances(first + j)
        for out, block, value in found:
            out[block] += value
        if ahead is not None:
            ahead(jnp.minimum(at + 1, groups - 1) * GROUP)
        if keep is not None:

            @pl.when((at > 0) & (at <= groups))
            def _():
                copy_out(at - 1).start()

        return carry

    lax.fori_loop(0, jnp.where(groups > 0, groups + 2, 0), step, 0)
    if keep is not None:
        for back in range(1, RING):
            group = groups - back

            @pl.when(group >= 0)
            def _():
                copy_out(group).wait()


def stream_loop(pairs, home, stage_ref, sems, use):
    ring = stage_ref.shape[0]

    def copy_in(at):
        slot = lax.rem(at, ring)
        return pltpu.make_async_copy(home(2 * at, 2), stage_ref.at[slot], sems.at[slot])

    for at in range(ring - 1):

        @pl.when(at < pairs)
        def _():
            copy_in(at).start()

    def step(at, carry):
        @pl.when(at + ring - 1 < pairs)
        def _():
            copy_in(at + ring - 1).start()

        copy_in(at).wait()
        slot = lax.rem(at, ring)
        found = []
        for k in range(0, 2 * GROUP, 2):
            tile = k % GROUP
            found += use(2 * at * GROUP, k, (stage_ref[slot, k // GROUP, tile], stage_ref[slot, k // GROUP, tile + 1]))
        for out, block, value in found:
            out[block] += value
        return carry

    lax.fori_loop(0, pairs, step, 0)


def pair_body(step, me, groups, diag_list, pair_list, *refs):
    row = row_ids()
    own = functools.partial(row_features, device=me[0], count=GROUP)
    if step == "diag":
        own_vec, own_geo, table_ref, stiff_ref, own_out, diag_tiles = refs[:6]
        vec_ref, row_sum, col_sum, stage_ref, sems, rows_ref, cols_ref, dist_ref, tile_ref = refs[6:]
        column_rows((own_geo,), (me[0],), cols_ref)
        vector_rows((own_vec,), vec_ref, 1.0)
    elif step == "pairs":
        own_vec, right_vec, own_geo, right_geo, table_ref, diag_ref, own_out, right_out, pair_tiles = refs[:9]
        vec_ref, row_sum, col_sum, stage_ref, sems, rows_ref, cols_ref, dist_ref, tile_ref = refs[9:]
        column_rows((own_geo, right_geo), (me[0], me[0] + 1), cols_ref)
        vector_rows((own_vec, right_vec), vec_ref, 1.0)
    else:
        own_vec, right_vec, diag_tiles, pair_tiles, *outs, vec_ref, row_sum, col_sum, stage_ref, sems = refs
        vector_rows((own_vec, right_vec), vec_ref, 1.0)
    row_sum[...] = jnp.zeros_like(row_sum)
    col_sum[...] = jnp.zeros_like(col_sum)

    def two(first, second):
        return jnp.concatenate([first, second], axis=0).astype(bf16)

    def use_diag(first, k, pair):
        a, b = diag_list[first + k] & 255, diag_list[first + k + 1] & 255
        left = two(jnp.where(row == 3, 0.0, vec_ref[a]), jnp.where(row == 3, 0.0, vec_ref[b]))
        image = jnp.dot(
            left, jnp.concatenate(pair, axis=1), preferred_element_type=f32
        )
        return [(col_sum, a, image[:8, :TILE]), (col_sum, b, image[8:, TILE:])]

    def use_pair(first, k, pair):
        p, q = pair_list[first + k], pair_list[first + k + 1]
        row_a, col_a = p & 255, (p >> 8) & 2047
        row_b, col_b = q & 255, (q >> 8) & 2047
        left = two(vec_ref[row_a], vec_ref[row_b])
        if step == 2:
            left = left * 2
        image = jnp.dot(left, jnp.concatenate(pair, axis=1), preferred_element_type=f32)
        found = [(col_sum, col_a, image[:8, :TILE]), (col_sum, col_b, image[8:, TILE:])]
        if step != 2:
            image = lax.dot_general(
                two(vec_ref[col_a], vec_ref[col_b]),
                jnp.concatenate(pair, axis=0),
                (((1,), (1,)), ((), ())),
                preferred_element_type=f32,
            )
            found += [(row_sum, row_a, image[:8, :TILE]), (row_sum, row_b, image[8:, TILE:])]
        return found

    def diag_home(group, count=1):
        return diag_tiles.at[pl.ds(group, count)]

    def pair_home(group, count=1):
        return pair_tiles.at[pl.ds(group, count)]

    if step in ("diag", "pairs"):
        loop = functools.partial(
            tile_loop, rows_ref=rows_ref, cols_ref=cols_ref, table_ref=table_ref, dist_ref=dist_ref, tile_ref=tile_ref
        )

        def features(at, carry):
            own(own_geo, rows_ref=rows_ref, first=at * GROUP)
            return carry

        if step == "diag":
            features(jnp.int32(0), 0)
            loop(
                jnp.int32(DIAG_GROUPS),
                diag_list,
                use=use_diag,
                ahead=lambda first: own(own_geo, rows_ref=rows_ref, first=first),
                keep=(stage_ref, sems, diag_home),
            )
        else:
            lax.fori_loop(0, DIAG_GROUPS, features, 0)
            loop(groups[0], pair_list, use=use_pair, keep=(stage_ref, sems, pair_home))
    else:
        stream_loop(jnp.int32(DIAG_GROUPS // 2), diag_home, stage_ref, sems, use_diag)
        stream_loop(lax.div(groups[0], 2), pair_home, stage_ref, sems, use_pair)

    def fold(value):
        return value + pltpu.roll(value, 4, 0)

    if step != 2:
        if step == "diag":
            images = (own_out,)
        else:
            images = (own_out, right_out) if step == "pairs" else outs

        def finish(first):
            place = pl.ds(pl.multiple_of(first * TILE, 8 * TILE), 8 * TILE)
            sums = row_sum[pl.ds(first, 8)] + col_sum[pl.ds(first, 8)]
            image = jnp.concatenate([fold(sums[k])[:4] for k in range(8)], axis=1)
            if step == "diag":
                fourth = lax.broadcasted_iota(i32, image.shape, 0) == 3
                image = image + jnp.where(fourth, stiff_ref[:, place] - SHIFT, 0.0)
            elif step == "pairs":
                image = image + diag_ref[:, place]
            images[0][:, place] = image
            if step != "diag":
                sums = col_sum[pl.ds(CB + first, 8)]
                images[1][:, place] = jnp.concatenate([fold(sums[k])[:4] for k in range(8)], axis=1)

        each_chunk(CB, finish)
    else:
        quad_out = outs[0]

        def finish(at, sums):
            return tuple(
                total + fold(col_sum[8 * at + k]) * fold(vec_ref[8 * at + k]) for k, total in enumerate(sums)
            )

        zero = jnp.zeros((8, TILE), f32)
        sums = lax.fori_loop(0, 2 * CB // 8, finish, (zero,) * 8)
        quad_out[...] = sum(sums)


def pair_call(step, *arrays, me, groups, diag_list, pair_list):
    smem = pl.BlockSpec(memory_space=pltpu.SMEM)
    vmem = pl.BlockSpec(memory_space=pltpu.VMEM)
    some = pl.BlockSpec(memory_space=pl.ANY)
    image = (jax.ShapeDtypeStruct((4, CB * TILE), f32), vmem)
    out = {
        "diag": (image, (jax.ShapeDtypeStruct((DIAG_GROUPS, GROUP, TILE, TILE), bf16), some)),
        "pairs": (image, image, (jax.ShapeDtypeStruct((PAIR_GROUPS, GROUP, TILE, TILE), bf16), some)),
        1: (image, image),
        2: ((jax.ShapeDtypeStruct((8, TILE), f32), vmem),),
    }[step]
    first = step in ("diag", "pairs")
    blocks = (1 if step == "diag" else 2) * CB + 1
    scratch = [
        pltpu.VMEM((blocks, 8, TILE), f32),
        pltpu.VMEM((CB, 8, TILE), f32),
        pltpu.VMEM((blocks, 8, TILE), f32),
        pltpu.VMEM((RING, GROUP, TILE, TILE) if first else (RING // 2, 2, GROUP, TILE, TILE), bf16),
        pltpu.SemaphoreType.DMA((RING,)),
    ]
    if first:
        scratch += [
            pltpu.VMEM((CB, TILE, TILE), bf16),
            pltpu.VMEM((blocks, 8, TILE), f32),
            pltpu.VMEM((GROUP, TILE, TILE), f32),
            pltpu.VMEM((GROUP, TILE, TILE), bf16),
        ]
    return pl.pallas_call(
        functools.partial(pair_body, step),
        out_shape=tuple(shape for shape, _ in out),
        in_specs=[smem] * 4 + ([vmem] * len(arrays) if first else [vmem, vmem, some, some]),
        out_specs=tuple(spec for _, spec in out),
        scratch_shapes=scratch,
        compiler_params=pltpu.CompilerParams(vmem_limit_bytes=48 * 2**20),
        cost_estimate=pl.CostEstimate(flops=2 * 10**9, bytes_accessed=10**8, transcendentals=0),
        name=f"pair_tiles_{step}",
    )(me, groups, diag_list, pair_list, *arrays)


def volume_body(me, groups, vol_list, vol_geo, own_geo, ahead_geo, *refs):
    coefs, refs = refs[:5], refs[5:]
    table_ref, plain, shifted, out, rows_ref, cols_ref, coef_ref, sums, dist_ref, tile_ref, far_geo, sems = refs
    at = lax.rem(me[0], EIGHT)
    inner = (at >= 2) & (at < EIGHT - 2)

    def fetch(source, index, k):
        return pltpu.make_async_copy(source.at[index], far_geo.at[k], sems.at[k])

    for k, step in enumerate((-2, -1, 2)):

        @pl.when(inner)
        def _():
            fetch(plain, at + step, k).start()

        @pl.when(jnp.logical_not(inner))
        def _():
            fetch(shifted, lax.rem(at + EIGHT // 2, EIGHT) + step, k).start()

    odd = lax.rem(me[0], 2)
    vector_rows(coefs, coef_ref, 0.0, [jnp.where(odd == 1, 4 - k, k) for k in range(5)])
    sums[...] = jnp.zeros_like(sums)

    def features(at, carry):
        row_features(vol_geo, me[0], rows_ref, at * 16, 16)
        return carry

    lax.fori_loop(0, VB // 16, features, 0)
    for k in range(3):
        fetch(plain, 0, k).wait()
    geos = (far_geo.at[0], far_geo.at[1], own_geo, ahead_geo, far_geo.at[2])
    column_rows(geos, [me[0] + k for k in range(-2, 3)], cols_ref)

    def use(first, k, pair):
        dims = (((1,), (1,)), ((), ()))
        p, q = vol_list[first + k], vol_list[first + k + 1]
        left = jnp.concatenate([coef_ref[(p >> 8) & 2047], coef_ref[(q >> 8) & 2047]], axis=0).astype(bf16)
        highs, lows = [], []
        for tile in pair:
            high = tile.astype(bf16)
            highs.append(high)
            lows.append((tile - high.astype(f32)).astype(bf16))
        image = lax.dot_general(left, jnp.concatenate(highs, axis=0), dims, preferred_element_type=f32)
        image += lax.dot_general(left, jnp.concatenate(lows, axis=0), dims, preferred_element_type=f32)
        return [(sums, p & 255, image[:8, :TILE]), (sums, q & 255, image[8:, TILE:])]

    tile_loop(groups[0], vol_list, rows_ref, cols_ref, table_ref, dist_ref, tile_ref, use)

    def finish(first):
        value = sums[pl.ds(first, 8)]
        rows = [(value[k] + pltpu.roll(value[k], 4, 0))[:3] for k in range(8)]
        out[:, pl.ds(pl.multiple_of(first * TILE, 8 * TILE), 8 * TILE)] = jnp.concatenate(rows, axis=1) * TILE**0.5

    each_chunk(VB, finish)


def volume_call(me, groups, vol_list, *arrays):
    smem = pl.BlockSpec(memory_space=pltpu.SMEM)
    vmem = pl.BlockSpec(memory_space=pltpu.VMEM)
    return pl.pallas_call(
        volume_body,
        out_shape=jax.ShapeDtypeStruct((3, VB * TILE), f32),
        in_specs=[smem] * 3 + [vmem] * (len(arrays) - 2) + [pl.BlockSpec(memory_space=pl.ANY)] * 2,
        out_specs=vmem,
        scratch_shapes=[
            pltpu.VMEM((VB, TILE, TILE), bf16),
            pltpu.VMEM((5 * CB + 1, 8, TILE), f32),
            pltpu.VMEM((5 * CB + 1, 8, TILE), f32),
            pltpu.VMEM((VB, 8, TILE), f32),
            pltpu.VMEM((GROUP, TILE, TILE), f32),
            pltpu.VMEM((GROUP, TILE, TILE), f32),
            pltpu.VMEM((3, 3, CB * TILE), f32),
            pltpu.SemaphoreType.DMA((3,)),
        ],
        compiler_params=pltpu.CompilerParams(vmem_limit_bytes=56 * 2**20),
        cost_estimate=pl.CostEstimate(flops=2 * 10**9, bytes_accessed=10**8, transcendentals=0),
        name="volume_tiles",
    )(me, groups, vol_list, *arrays)


def cg_weights(moment):
    def gram(first, second):
        return sum(a * b * moment[i + j] for i, a in enumerate(first) for j, b in enumerate(second))

    def image(vector):
        grown = [SHIFT * a for a in vector] + [0.0]
        return [a + (vector[k - 1] if k else 0.0) for k, a in enumerate(grown)]

    def axpy(scale, first, second):
        size = max(len(first), len(second))
        pad = lambda v: list(v) + [0.0] * (size - len(v))
        return [scale * a + b for a, b in zip(pad(first), pad(second))]

    one = jnp.ones_like(moment[0])
    residual, direction, total = [one], [one], [0.0 * one]
    norm = gram(residual, residual)
    for step in range(3):
        grown = image(direction)
        length = norm / gram(direction, grown)
        total = axpy(length, direction, total)
        if step < 2:
            residual = axpy(-length, grown, residual)
            norm_next = gram(residual, residual)
            direction = axpy(norm_next / norm, direction, residual)
            norm = norm_next
    return total


def comp_sum(first, second):
    return jnp.sum(first * second, axis=1)


def body(ctrl_points, ctrl_disp, stiffness, pair_rows, pair_cols, pair_count, vol_points, vol_rows, vol_cols, vol_count):
    me = lax.axis_index("nodes")
    devices = lax.axis_size("nodes")

    ahead = from_behind(ctrl_points, "nodes", -1)
    beside = from_behind(ctrl_disp, "nodes", -1)
    gathered = [gathered_eights(ctrl_points, "nodes", shift) for shift in (0, EIGHT // 2)]
    table = offset_table()

    slots = lax.iota(i32, MAXT)
    right = pair_cols >= CB
    live = (slots < pair_count[0]) & (~right | (me < devices - 1))
    code = offset_code(right.astype(i32), pair_rows, pair_cols % CB)
    pair_list = jnp.where(live, pair_rows | (pair_cols << 8) | (code << 19), (2 * CB) << 8)
    pair_groups = (pair_count + 2 * GROUP - 1) // (2 * GROUP) * 2
    own = lax.iota(i32, CB)
    diag_list = own | (own << 8) | (62 << 19)

    slots = lax.iota(i32, MAXV)
    step_x = vol_cols // CB - 2
    source = me + step_x
    live = (slots < vol_count[0]) & (source >= 0) & (source < devices)
    code = offset_code(step_x, vol_rows, vol_cols % CB)
    vol_list = jnp.where(live, vol_rows | (vol_cols << 8) | (code << 19), (5 * CB) << 8)
    vol_groups = (vol_count + GROUP - 1) // GROUP
    here = me.astype(i32)[None]

    images = functools.partial(pair_call, me=here, groups=pair_groups, diag_list=diag_list, pair_list=pair_list)

    def exchanged(own_part, right_part):
        back = from_behind(right_part, "nodes", 1)
        ahead = from_behind(own_part, "nodes", -1)
        return own_part + back, ahead + right_part

    own_part, diag_tiles = images("diag", ctrl_disp, ctrl_points, table, stiffness[None, :])
    own_part, right_part, pair_tiles = images(
        "pairs", ctrl_disp, beside, ctrl_points, ahead, table, own_part
    )
    own_part, right_part, gathered[0] = lax.optimization_barrier((own_part, right_part, gathered[0]))
    tiles = (diag_tiles, pair_tiles)
    total, total_beside = exchanged(own_part, right_part)
    diagonal, diagonal_beside = total[3:4], total_beside[3:4]
    first = total[:3] + diagonal * ctrl_disp
    first_beside = total_beside[:3] + diagonal_beside * beside
    own_part, right_part = images(1, first, first_beside, *tiles)
    own_part, right_part, gathered[1] = lax.optimization_barrier((own_part, right_part, gathered[1]))
    total, total_beside = exchanged(own_part, right_part)
    second = total[:3] + diagonal * first
    second_beside = total_beside[:3] + diagonal_beside * first_beside
    (quad,) = images(2, second, second_beside, *tiles)
    moments = jnp.concatenate(
        [
            comp_sum(ctrl_disp, ctrl_disp),
            comp_sum(ctrl_disp, first),
            comp_sum(first, first),
            comp_sum(first, second),
            comp_sum(second, second),
            jnp.sum(quad, axis=1)[:3] + comp_sum(diagonal * second, second),
            jnp.zeros((TILE - 18,), f32),
        ]
    )

    sent = jnp.broadcast_to(moments[None, None, :], (devices, 1, TILE))
    moments = jnp.sum(lax.all_to_all(sent, "nodes", 0, 0, tiled=True), axis=(0, 1))
    weights = cg_weights([moments[3 * k : 3 * k + 3] for k in range(6)])
    coef = sum(w[:, None] * u for w, u in zip(weights, (ctrl_disp, first, second)))
    near = around(coef, "nodes")
    moved = volume_call(here, vol_groups, vol_list, vol_points, ctrl_points, ahead, *near, table, *gathered)
    return (coef, moved)


def solution(mesh):
    across = P(None, "nodes")
    flat = P("nodes")
    return jax.shard_map(
        body,
        mesh=mesh,
        in_specs=(across, across, flat, flat, flat, flat, across, flat, flat, flat),
        out_specs=(across, across),
        check_vma=False,
    )
```

```python
import functools

import jax
import jax.numpy as jnp
from jax import lax
from jax.experimental import pallas as pl
from jax.experimental.pallas import tpu as pltpu
from jax.sharding import PartitionSpec as P

TILE = 128
SIDE = 16
CB = 256
VB = 256
MAXT = 768
MAXV = 512
GROUP = 16
PART = 32
RING = 8
DIAG_GROUPS = CB // GROUP
PAIR_GROUPS = MAXT // GROUP
SHIFT = 0.75
FAR = 64.0

f32 = jnp.float32
bf16 = jnp.bfloat16
i32 = jnp.int32


def from_behind(block, axis, distance):
    devices = range(lax.axis_size(axis))
    route = [(i - distance, i) for i in devices if i - distance in devices]
    return lax.ppermute(block, axis, route)


def around(block, axis):
    devices = range(lax.axis_size(axis))

    def send(value, target):
        return lax.ppermute(value, axis, [(i, target(i)) for i in devices if target(i) in devices])

    far = send(block, lambda i: i - 2 if i % 2 else i + 2)
    near = send(block, lambda i: i + 1 if i % 2 else i - 1)
    partner = send(block, lambda i: i ^ 1)
    shared = send(near, lambda i: i ^ 1)
    return [far, near, block, partner, shared]


def offset_table():
    code = lax.iota(i32, 125)
    step_x = (code // 25 - 2).astype(f32) * 0.25
    step_y = (code // 5 % 5 - 2).astype(f32) * 0.5
    step_z = (code % 5 - 2).astype(f32) * 0.5
    zero = jnp.zeros_like(step_x)
    rows = jnp.stack([step_x, step_y, step_z, step_x, step_y, step_z, zero, zero], axis=1)
    return jnp.broadcast_to(rows[:, :, None], (125, 8, TILE))


def offset_code(step_x, row_cell, col_cell):
    step_y = jnp.clip(col_cell // SIDE - row_cell // SIDE, -2, 2)
    step_z = jnp.clip(col_cell % SIDE - row_cell % SIDE, -2, 2)
    return (step_x + 2) * 25 + (step_y + 2) * 5 + step_z + 2


def row_ids():
    return lax.broadcasted_iota(i32, (8, TILE), 0)


def split(value):
    high = value.astype(bf16).astype(f32)
    return high, value - high


def three_rows(ref, first, count):
    value = ref[:, pl.ds(pl.multiple_of(first * TILE, count * TILE), count * TILE)]
    rest = jnp.zeros((5, TILE), f32)
    return [jnp.concatenate([value[:, k * TILE : (k + 1) * TILE], rest], axis=0) for k in range(count)]


def local_coords(blocks, first, device):
    row = row_ids()
    along_x = jnp.where(row == 0, 1.0, 0.0) * (device.astype(f32) + 0.5)
    along_y = jnp.where(row == 1, 2.0, 0.0) * ((first >> 4).astype(f32) + 0.5)
    along_z = jnp.where(row == 2, 2.0, 0.0)
    fixed = along_x + along_y
    cell = (first & 15).astype(f32) + 0.5
    return [(block - (fixed + along_z * (cell + k))) * 0.25 for k, block in enumerate(blocks)]


def each_chunk(count, todo):
    def step(at, carry):
        todo(8 * at)
        return carry

    lax.fori_loop(0, count // 8, step, 0)


def column_rows(geo_refs, devices, cols_ref):
    unit = jnp.where(row_ids() == 6, 1.0, 0.0)
    for at, ref in enumerate(geo_refs):

        def fill(first):
            local = local_coords(three_rows(ref, first, 8), first, devices[at])
            rows = [block + pltpu.roll(block, 3, 0) + unit for block in local]
            cols_ref[pl.ds(at * CB + first, 8)] = jnp.stack(rows)

        each_chunk(CB, fill)
    cols_ref[len(geo_refs) * CB] = jnp.full((8, TILE), FAR, f32)


def vector_rows(refs, vec_ref, unit, places=None):
    unit = jnp.where(row_ids() == 3, unit, 0.0)
    for at, ref in enumerate(refs):

        def fill(first):
            rows = []
            for block in three_rows(ref, first, 8):
                high, low = split(block)
                rows.append(high + pltpu.roll(low, 4, 0) + unit)
            vec_ref[pl.ds((at if places is None else places[at]) * CB + first, 8)] = jnp.stack(rows)

        each_chunk(CB, fill)
    vec_ref[len(refs) * CB] = jnp.zeros((8, TILE), f32)


def row_features(geo_ref, device, rows_ref, first, count):
    row = row_ids()
    middle = (row >= 3) & (row < 6)

    def features(coords):
        norm = jnp.sum(coords * coords, axis=0, keepdims=True)
        full = jnp.where(middle, 1.0, jnp.where(row == 6, norm, -2.0 * coords))
        high, rest = split(full)
        mid, low = split(rest)
        last = jnp.where(row < 3, mid, jnp.where(middle, 1.0, low))
        return [high, high, mid, last]

    blocks = local_coords(three_rows(geo_ref, first, count), first, device)
    for k in range(0, count, 4):
        parts = []
        for j in range(4):
            parts += features(blocks[k + j])
        turned = jnp.transpose(jnp.concatenate(parts, axis=0).astype(bf16))
        for j in range(4):
            rows_ref[first + k + j] = turned if j == 0 else pltpu.roll(turned, TILE - j * PART, 1)


def tile_loop(groups, listed, rows_ref, cols_ref, table_ref, dist_ref, tile_ref, use, ahead=None, keep=None):
    row = row_ids()
    squares = (row >= 3) & (row < 6)
    unit = row == 6
    dist_ref[...] = jnp.full_like(dist_ref, FAR)
    tile_ref[...] = jnp.zeros_like(tile_ref)

    def distances(slot):
        packed = listed[slot]
        moved = cols_ref[(packed >> 8) & 2047] + table_ref[packed >> 19]
        full = jnp.where(squares, moved * moved, moved)
        high, rest = split(full)
        mid, low = split(rest)
        last = jnp.where(squares, low, jnp.where(unit, 1.0, mid))
        features = jnp.concatenate([high, mid, high, last], axis=0).astype(bf16)
        return jnp.dot(rows_ref[packed & 255][:, :PART], features, preferred_element_type=f32)

    def phi(dist_sq):
        dist_sq = jnp.maximum(dist_sq, 1e-12)
        gap = jnp.maximum(0.5 - dist_sq * lax.rsqrt(dist_sq), 0.0)
        gap_sq = gap * gap
        return gap_sq * gap_sq * (0.625 - gap)

    if keep is not None:
        stage_ref, sems, home = keep

    def copy_out(group):
        slot = lax.rem(group, RING)
        return pltpu.make_async_copy(stage_ref.at[pl.ds(slot, 1)], home(group), sems.at[slot])

    def step(at, carry):
        used = jnp.maximum(at - 2, 0) * GROUP
        first = jnp.minimum(at, groups - 1) * GROUP
        if keep is not None:
            stage = lax.rem(at + RING - 1, RING)
            before = at - 1 - RING

            @pl.when(before >= 0)
            def _():
                copy_out(before).wait()

        found = []
        for k in range(0, GROUP, 2):
            found += use(used, k, (tile_ref[k], tile_ref[k + 1]))
            for j in (k, k + 1):
                tile = phi(dist_ref[j]).astype(tile_ref.dtype)
                tile_ref[j] = tile
                if keep is not None:
                    stage_ref[stage, j] = tile
            for j in (k, k + 1):
                dist_ref[j] = distances(first + j)
        for out, block, value in found:
            out[block] += value
        if ahead is not None:
            ahead(jnp.minimum(at + 1, groups - 1) * GROUP)
        if keep is not None:

            @pl.when((at > 0) & (at <= groups))
            def _():
                copy_out(at - 1).start()

        return carry

    lax.fori_loop(0, jnp.where(groups > 0, groups + 2, 0), step, 0)
    if keep is not None:
        for back in range(1, RING):
            group = groups - back

            @pl.when(group >= 0)
            def _():
                copy_out(group).wait()


def stream(diag_tiles, pair_tiles, pairs, stage_ref, sems):
    ring = stage_ref.shape[0]
    diag_pairs = DIAG_GROUPS // 2
    total = diag_pairs + pairs

    def copy_in(tiles, at, slot):
        return pltpu.make_async_copy(tiles.at[pl.ds(2 * at, 2)], stage_ref.at[slot], sems.at[slot])

    def start(at):
        slot = lax.rem(at, ring)

        @pl.when(at < diag_pairs)
        def _():
            copy_in(diag_tiles, at, slot).start()

        @pl.when((at >= diag_pairs) & (at < total))
        def _():
            copy_in(pair_tiles, at - diag_pairs, slot).start()

    for at in range(ring - 1):
        start(jnp.int32(at))

    def loop(first, count, use):
        def step(at, carry):
            here = first + at
            start(here + ring - 1)
            slot = lax.rem(here, ring)
            copy_in(diag_tiles, 0, slot).wait()
            found = []
            for k in range(0, 2 * GROUP, 2):
                part, tile = k // GROUP, k % GROUP
                found += use(2 * at * GROUP, k, (stage_ref[slot, part, tile], stage_ref[slot, part, tile + 1]))
            for out, block, value in found:
                out[block] += value
            return carry

        lax.fori_loop(0, count, step, 0)

    return loop


def pair_body(step, me, groups, diag_list, pair_list, *refs):
    row = row_ids()
    own = functools.partial(row_features, device=me[0], count=GROUP)
    if step == "diag":
        own_vec, own_geo, table_ref, own_out, diag_tiles = refs[:5]
        vec_ref, row_sum, col_sum, stage_ref, sems, rows_ref, cols_ref, dist_ref, tile_ref = refs[5:]
        column_rows((own_geo,), (me[0],), cols_ref)
        vector_rows((own_vec,), vec_ref, 1.0)
    elif step == "pairs":
        own_vec, right_vec, own_geo, right_geo, table_ref, stiff_ref, diag_ref = refs[:7]
        own_out, right_out, pair_tiles = refs[7:10]
        vec_ref, row_sum, col_sum, stage_ref, sems, rows_ref, cols_ref, dist_ref, tile_ref = refs[10:]
        column_rows((own_geo, right_geo), (me[0], me[0] + 1), cols_ref)
        vector_rows((own_vec, right_vec), vec_ref, 1.0)
    else:
        own_vec, right_vec, diag_tiles, pair_tiles, *outs, vec_ref, row_sum, col_sum, stage_ref, sems = refs
        pairs = lax.div(groups[0], 2)
        loop = stream(diag_tiles, pair_tiles, pairs, stage_ref, sems)
        vector_rows((own_vec, right_vec), vec_ref, 1.0)
    row_sum[...] = jnp.zeros_like(row_sum)
    col_sum[...] = jnp.zeros_like(col_sum)

    def two(first, second):
        return jnp.concatenate([first, second], axis=0).astype(bf16)

    def use_diag(first, k, pair):
        a, b = diag_list[first + k] & 255, diag_list[first + k + 1] & 255
        left = two(jnp.where(row == 3, 0.0, vec_ref[a]), jnp.where(row == 3, 0.0, vec_ref[b]))
        image = jnp.dot(
            left, jnp.concatenate(pair, axis=1), preferred_element_type=f32
        )
        return [(col_sum, a, image[:8, :TILE]), (col_sum, b, image[8:, TILE:])]

    def use_pair(first, k, pair):
        p, q = pair_list[first + k], pair_list[first + k + 1]
        row_a, col_a = p & 255, (p >> 8) & 2047
        row_b, col_b = q & 255, (q >> 8) & 2047
        left = two(vec_ref[row_a], vec_ref[row_b])
        if step == 2:
            left = left * 2
        image = jnp.dot(left, jnp.concatenate(pair, axis=1), preferred_element_type=f32)
        found = [(col_sum, col_a, image[:8, :TILE]), (col_sum, col_b, image[8:, TILE:])]
        if step != 2:
            image = lax.dot_general(
                two(vec_ref[col_a], vec_ref[col_b]),
                jnp.concatenate(pair, axis=0),
                (((1,), (1,)), ((), ())),
                preferred_element_type=f32,
            )
            found += [(row_sum, row_a, image[:8, :TILE]), (row_sum, row_b, image[8:, TILE:])]
        return found

    def diag_home(group, count=1):
        return diag_tiles.at[pl.ds(group, count)]

    def pair_home(group, count=1):
        return pair_tiles.at[pl.ds(group, count)]

    if step in ("diag", "pairs"):
        loop = functools.partial(
            tile_loop, rows_ref=rows_ref, cols_ref=cols_ref, table_ref=table_ref, dist_ref=dist_ref, tile_ref=tile_ref
        )

        def features(at, carry):
            own(own_geo, rows_ref=rows_ref, first=at * GROUP)
            return carry

        if step == "diag":
            features(jnp.int32(0), 0)
            loop(
                jnp.int32(DIAG_GROUPS),
                diag_list,
                use=use_diag,
                ahead=lambda first: own(own_geo, rows_ref=rows_ref, first=first),
                keep=(stage_ref, sems, diag_home),
            )
        else:
            lax.fori_loop(0, DIAG_GROUPS, features, 0)
            loop(groups[0], pair_list, use=use_pair, keep=(stage_ref, sems, pair_home))
    else:
        loop(0, DIAG_GROUPS // 2, use_diag)
        loop(DIAG_GROUPS // 2, pairs, use_pair)

    def fold(value):
        return value + pltpu.roll(value, 4, 0)

    if step != 2:
        if step == "diag":
            images = (own_out,)
        else:
            images = (own_out, right_out) if step == "pairs" else outs

        def finish(first):
            place = pl.ds(pl.multiple_of(first * TILE, 8 * TILE), 8 * TILE)
            sums = row_sum[pl.ds(first, 8)] + col_sum[pl.ds(first, 8)]
            image = jnp.concatenate([fold(sums[k])[:4] for k in range(8)], axis=1)
            if step == "pairs":
                fourth = lax.broadcasted_iota(i32, image.shape, 0) == 3
                image = image + diag_ref[:, place] + jnp.where(fourth, stiff_ref[:, place] - SHIFT, 0.0)
            images[0][:, place] = image
            if step != "diag":
                sums = col_sum[pl.ds(CB + first, 8)]
                images[1][:, place] = jnp.concatenate([fold(sums[k])[:4] for k in range(8)], axis=1)

        each_chunk(CB, finish)
    else:
        quad_out = outs[0]

        def finish(at, sums):
            return tuple(
                total + fold(col_sum[8 * at + k]) * fold(vec_ref[8 * at + k]) for k, total in enumerate(sums)
            )

        zero = jnp.zeros((8, TILE), f32)
        sums = lax.fori_loop(0, 2 * CB // 8, finish, (zero,) * 8)
        quad_out[...] = sum(sums)


def pair_call(step, *arrays, me, groups, diag_list, pair_list):
    smem = pl.BlockSpec(memory_space=pltpu.SMEM)
    vmem = pl.BlockSpec(memory_space=pltpu.VMEM)
    some = pl.BlockSpec(memory_space=pl.ANY)
    image = (jax.ShapeDtypeStruct((4, CB * TILE), f32), vmem)
    out = {
        "diag": (image, (jax.ShapeDtypeStruct((DIAG_GROUPS, GROUP, TILE, TILE), bf16), some)),
        "pairs": (image, image, (jax.ShapeDtypeStruct((PAIR_GROUPS, GROUP, TILE, TILE), bf16), some)),
        1: (image, image),
        2: ((jax.ShapeDtypeStruct((8, TILE), f32), vmem),),
    }[step]
    first = step in ("diag", "pairs")
    blocks = (1 if step == "diag" else 2) * CB + 1
    scratch = [
        pltpu.VMEM((blocks, 8, TILE), f32),
        pltpu.VMEM((CB, 8, TILE), f32),
        pltpu.VMEM((blocks, 8, TILE), f32),
        pltpu.VMEM((RING, GROUP, TILE, TILE) if first else (RING // 2, 2, GROUP, TILE, TILE), bf16),
        pltpu.SemaphoreType.DMA((RING,)),
    ]
    if first:
        scratch += [
            pltpu.VMEM((CB, TILE, TILE), bf16),
            pltpu.VMEM((blocks, 8, TILE), f32),
            pltpu.VMEM((GROUP, TILE, TILE), f32),
            pltpu.VMEM((GROUP, TILE, TILE), bf16),
        ]
    return pl.pallas_call(
        functools.partial(pair_body, step),
        out_shape=tuple(shape for shape, _ in out),
        in_specs=[smem] * 4 + ([vmem] * len(arrays) if first else [vmem, vmem, some, some]),
        out_specs=tuple(spec for _, spec in out),
        scratch_shapes=scratch,
        compiler_params=pltpu.CompilerParams(vmem_limit_bytes=48 * 2**20),
        cost_estimate=pl.CostEstimate(flops=2 * 10**9, bytes_accessed=10**8, transcendentals=0),
        name=f"pair_tiles_{step}",
    )(me, groups, diag_list, pair_list, *arrays)


def volume_body(me, groups, vol_list, vol_geo, *refs):
    geos, coefs = refs[:5], refs[5:10]
    table_ref, out, rows_ref, cols_ref, coef_ref, sums, dist_ref, tile_ref = refs[10:]
    column_rows(geos, [me[0] + k for k in range(-2, 3)], cols_ref)
    odd = lax.rem(me[0], 2)
    vector_rows(coefs, coef_ref, 0.0, [jnp.where(odd == 1, 4 - k, k) for k in range(5)])
    sums[...] = jnp.zeros_like(sums)

    def features(at, carry):
        row_features(vol_geo, me[0], rows_ref, at * 16, 16)
        return carry

    lax.fori_loop(0, VB // 16, features, 0)

    def use(first, k, pair):
        dims = (((1,), (1,)), ((), ()))
        p, q = vol_list[first + k], vol_list[first + k + 1]
        left = jnp.concatenate([coef_ref[(p >> 8) & 2047], coef_ref[(q >> 8) & 2047]], axis=0).astype(bf16)
        highs, lows = [], []
        for tile in pair:
            high = tile.astype(bf16)
            highs.append(high)
            lows.append((tile - high.astype(f32)).astype(bf16))
        image = lax.dot_general(left, jnp.concatenate(highs, axis=0), dims, preferred_element_type=f32)
        image += lax.dot_general(left, jnp.concatenate(lows, axis=0), dims, preferred_element_type=f32)
        return [(sums, p & 255, image[:8, :TILE]), (sums, q & 255, image[8:, TILE:])]

    tile_loop(groups[0], vol_list, rows_ref, cols_ref, table_ref, dist_ref, tile_ref, use)

    def finish(first):
        value = sums[pl.ds(first, 8)]
        rows = [(value[k] + pltpu.roll(value[k], 4, 0))[:3] for k in range(8)]
        out[:, pl.ds(pl.multiple_of(first * TILE, 8 * TILE), 8 * TILE)] = jnp.concatenate(rows, axis=1) * TILE**0.5

    each_chunk(VB, finish)


def volume_call(me, groups, vol_list, *arrays):
    smem = pl.BlockSpec(memory_space=pltpu.SMEM)
    vmem = pl.BlockSpec(memory_space=pltpu.VMEM)
    return pl.pallas_call(
        volume_body,
        out_shape=jax.ShapeDtypeStruct((3, VB * TILE), f32),
        in_specs=[smem] * 3 + [vmem] * len(arrays),
        out_specs=vmem,
        scratch_shapes=[
            pltpu.VMEM((VB, TILE, TILE), bf16),
            pltpu.VMEM((5 * CB + 1, 8, TILE), f32),
            pltpu.VMEM((5 * CB + 1, 8, TILE), f32),
            pltpu.VMEM((VB, 8, TILE), f32),
            pltpu.VMEM((GROUP, TILE, TILE), f32),
            pltpu.VMEM((GROUP, TILE, TILE), f32),
        ],
        compiler_params=pltpu.CompilerParams(vmem_limit_bytes=56 * 2**20),
        cost_estimate=pl.CostEstimate(flops=2 * 10**9, bytes_accessed=10**8, transcendentals=0),
        name="volume_tiles",
    )(me, groups, vol_list, *arrays)


def cg_weights(moment):
    def gram(first, second):
        return sum(a * b * moment[i + j] for i, a in enumerate(first) for j, b in enumerate(second))

    def image(vector):
        grown = [SHIFT * a for a in vector] + [0.0]
        return [a + (vector[k - 1] if k else 0.0) for k, a in enumerate(grown)]

    def axpy(scale, first, second):
        size = max(len(first), len(second))
        pad = lambda v: list(v) + [0.0] * (size - len(v))
        return [scale * a + b for a, b in zip(pad(first), pad(second))]

    one = jnp.ones_like(moment[0])
    residual, direction, total = [one], [one], [0.0 * one]
    norm = gram(residual, residual)
    for step in range(3):
        grown = image(direction)
        length = norm / gram(direction, grown)
        total = axpy(length, direction, total)
        if step < 2:
            residual = axpy(-length, grown, residual)
            norm_next = gram(residual, residual)
            direction = axpy(norm_next / norm, direction, residual)
            norm = norm_next
    return total


def comp_sum(first, second):
    return jnp.sum(first * second, axis=1)


def body(ctrl_points, ctrl_disp, stiffness, pair_rows, pair_cols, pair_count, vol_points, vol_rows, vol_cols, vol_count):
    me = lax.axis_index("nodes")
    devices = lax.axis_size("nodes")
    order = (2, 1, 0, -1, -2)

    geo = {0: ctrl_points, -1: from_behind(ctrl_points, "nodes", -1)}
    beside = from_behind(ctrl_disp, "nodes", -1)
    table = offset_table()

    slots = lax.iota(i32, MAXT)
    right = pair_cols >= CB
    live = (slots < pair_count[0]) & (~right | (me < devices - 1))
    code = offset_code(right.astype(i32), pair_rows, pair_cols % CB)
    pair_list = jnp.where(live, pair_rows | (pair_cols << 8) | (code << 19), (2 * CB) << 8)
    pair_groups = (pair_count + 2 * GROUP - 1) // (2 * GROUP) * 2
    own = lax.iota(i32, CB)
    diag_list = own | (own << 8) | (62 << 19)

    slots = lax.iota(i32, MAXV)
    step_x = vol_cols // CB - 2
    source = me + step_x
    live = (slots < vol_count[0]) & (source >= 0) & (source < devices)
    code = offset_code(step_x, vol_rows, vol_cols % CB)
    vol_list = jnp.where(live, vol_rows | (vol_cols << 8) | (code << 19), (5 * CB) << 8)
    vol_groups = (vol_count + GROUP - 1) // GROUP
    here = me.astype(i32)[None]

    images = functools.partial(pair_call, me=here, groups=pair_groups, diag_list=diag_list, pair_list=pair_list)

    def exchanged(own_part, right_part):
        back = from_behind(right_part, "nodes", 1)
        ahead = from_behind(own_part, "nodes", -1)
        return own_part + back, ahead + right_part

    own_part, diag_tiles = images("diag", ctrl_disp, ctrl_points, table)
    own_part, right_part, pair_tiles = images(
        "pairs", ctrl_disp, beside, ctrl_points, geo[-1], table, stiffness[None, :], own_part
    )
    tiles = (diag_tiles, pair_tiles)
    total, total_beside = exchanged(own_part, right_part)
    diagonal, diagonal_beside = total[3:4], total_beside[3:4]
    first = total[:3] + diagonal * ctrl_disp
    first_beside = total_beside[:3] + diagonal_beside * beside
    later, first = lax.optimization_barrier((ctrl_points, first))
    for offset in (1, 2, -2):
        geo[offset] = from_behind(later, "nodes", offset)
    own_part, right_part = images(1, first, first_beside, *tiles)
    own_part, right_part, geo[1], geo[2], geo[-2] = lax.optimization_barrier(
        (own_part, right_part, geo[1], geo[2], geo[-2])
    )
    total, total_beside = exchanged(own_part, right_part)
    second = total[:3] + diagonal * first
    second_beside = total_beside[:3] + diagonal_beside * first_beside
    (quad,) = images(2, second, second_beside, *tiles)
    moments = jnp.concatenate(
        [
            comp_sum(ctrl_disp, ctrl_disp),
            comp_sum(ctrl_disp, first),
            comp_sum(first, first),
            comp_sum(first, second),
            comp_sum(second, second),
            jnp.sum(quad, axis=1)[:3] + comp_sum(diagonal * second, second),
            jnp.zeros((TILE - 18,), f32),
        ]
    )

    sent = jnp.broadcast_to(moments[None, None, :], (devices, 1, TILE))
    moments = jnp.sum(lax.all_to_all(sent, "nodes", 0, 0, tiled=True), axis=(0, 1))
    weights = cg_weights([moments[3 * k : 3 * k + 3] for k in range(6)])
    coef = sum(w[:, None] * u for w, u in zip(weights, (ctrl_disp, first, second)))
    near = around(coef, "nodes")
    moved = volume_call(here, vol_groups, vol_list, vol_points, *[geo[k] for k in order], *near, table)
    return (coef, moved)


def solution(mesh):
    across = P(None, "nodes")
    flat = P("nodes")
    return jax.shard_map(
        body,
        mesh=mesh,
        in_specs=(across, across, flat, flat, flat, flat, across, flat, flat, flat),
        out_specs=(across, across),
        check_vma=False,
    )
```

```python
import functools

import jax
import jax.numpy as jnp
from jax import lax
from jax.experimental import pallas as pl
from jax.experimental.pallas import tpu as pltpu
from jax.sharding import PartitionSpec as P

TILE = 128
SIDE = 16
CB = 256
VB = 256
MAXT = 768
MAXV = 512
GROUP = 16
PART = 32
RING = 8
CHUNK = 16
DIAG_GROUPS = CB // GROUP
PAIR_GROUPS = MAXT // GROUP
SHIFT = 0.75
FAR = 64.0

f32 = jnp.float32
bf16 = jnp.bfloat16
i32 = jnp.int32


def from_behind(block, axis, distance):
    devices = range(lax.axis_size(axis))
    route = [(i - distance, i) for i in devices if i - distance in devices]
    return lax.ppermute(block, axis, route)


def around(block, axis):
    devices = range(lax.axis_size(axis))

    def send(value, target):
        return lax.ppermute(value, axis, [(i, target(i)) for i in devices if target(i) in devices])

    far = send(block, lambda i: i - 2 if i % 2 else i + 2)
    near = send(block, lambda i: i + 1 if i % 2 else i - 1)
    partner = send(block, lambda i: i ^ 1)
    shared = send(near, lambda i: i ^ 1)
    return [far, near, block, partner, shared]


def offset_table():
    code = lax.iota(i32, 125)
    step_x = (code // 25 - 2).astype(f32) * 0.25
    step_y = (code // 5 % 5 - 2).astype(f32) * 0.5
    step_z = (code % 5 - 2).astype(f32) * 0.5
    zero = jnp.zeros_like(step_x)
    rows = jnp.stack([step_x, step_y, step_z, step_x, step_y, step_z, zero, zero], axis=1)
    return jnp.broadcast_to(rows[:, :, None], (125, 8, TILE))


def offset_code(step_x, row_cell, col_cell):
    step_y = jnp.clip(col_cell // SIDE - row_cell // SIDE, -2, 2)
    step_z = jnp.clip(col_cell % SIDE - row_cell % SIDE, -2, 2)
    return (step_x + 2) * 25 + (step_y + 2) * 5 + step_z + 2


def row_ids():
    return lax.broadcasted_iota(i32, (8, TILE), 0)


def split(value):
    high = value.astype(bf16).astype(f32)
    return high, value - high


def three_rows(ref, first, count):
    value = ref[:, pl.ds(pl.multiple_of(first * TILE, count * TILE), count * TILE)]
    rest = jnp.zeros((5, TILE), f32)
    return [jnp.concatenate([value[:, k * TILE : (k + 1) * TILE], rest], axis=0) for k in range(count)]


def local_coords(blocks, first, device):
    row = row_ids()
    along_x = jnp.where(row == 0, 1.0, 0.0) * (device.astype(f32) + 0.5)
    along_y = jnp.where(row == 1, 2.0, 0.0) * ((first >> 4).astype(f32) + 0.5)
    along_z = jnp.where(row == 2, 2.0, 0.0)
    fixed = along_x + along_y
    cell = (first & 15).astype(f32) + 0.5
    return [(block - (fixed + along_z * (cell + k))) * 0.25 for k, block in enumerate(blocks)]


def each_chunk(count, todo, chunk=8):
    def step(at, carry):
        todo(chunk * at)
        return carry

    lax.fori_loop(0, count // chunk, step, 0)


def column_rows(geo_refs, devices, cols_ref):
    unit = jnp.where(row_ids() == 6, 1.0, 0.0)
    for at, ref in enumerate(geo_refs):

        def fill(first):
            local = local_coords(three_rows(ref, first, CHUNK), first, devices[at])
            rows = [block + pltpu.roll(block, 3, 0) + unit for block in local]
            cols_ref[pl.ds(at * CB + first, CHUNK)] = jnp.stack(rows)

        each_chunk(CB, fill, CHUNK)
    cols_ref[len(geo_refs) * CB] = jnp.full((8, TILE), FAR, f32)


def vector_rows(refs, vec_ref, unit, places=None):
    unit = jnp.where(row_ids() == 3, unit, 0.0)
    for at, ref in enumerate(refs):

        def fill(first):
            rows = []
            for block in three_rows(ref, first, CHUNK):
                high, low = split(block)
                rows.append(high + pltpu.roll(low, 4, 0) + unit)
            vec_ref[pl.ds((at if places is None else places[at]) * CB + first, CHUNK)] = jnp.stack(rows)

        each_chunk(CB, fill, CHUNK)
    vec_ref[len(refs) * CB] = jnp.zeros((8, TILE), f32)


def row_features(geo_ref, device, first, count):
    row = row_ids()
    middle = (row >= 3) & (row < 6)

    def features(coords):
        norm = jnp.sum(coords * coords, axis=0, keepdims=True)
        full = jnp.where(middle, 1.0, jnp.where(row == 6, norm, -2.0 * coords))
        high, rest = split(full)
        mid, low = split(rest)
        last = jnp.where(row < 3, mid, jnp.where(middle, 1.0, low))
        return [high, high, mid, last]

    blocks = local_coords(three_rows(geo_ref, first, count), first, device)
    parts = [features(block) for block in blocks]
    return [
        jnp.transpose(jnp.concatenate(sum(parts[k : k + 4], []), axis=0).astype(bf16)) for k in range(0, count, 4)
    ]


def spread(turned, rows_ref, first):
    for j in range(4):
        rows_ref[first + j] = turned if j == 0 else pltpu.roll(turned, TILE - j * PART, 1)


def tile_loop(groups, listed, rows_ref, cols_ref, table_ref, dist_ref, tile_ref, use, ahead=None, keep=None):
    row = row_ids()
    squares = (row >= 3) & (row < 6)
    unit = row == 6
    dist_ref[...] = jnp.full_like(dist_ref, FAR)
    tile_ref[...] = jnp.zeros_like(tile_ref)

    def distances(slot):
        packed = listed[slot]
        moved = cols_ref[(packed >> 8) & 2047] + table_ref[packed >> 19]
        full = jnp.where(squares, moved * moved, moved)
        high, rest = split(full)
        mid, low = split(rest)
        last = jnp.where(squares, low, jnp.where(unit, 1.0, mid))
        features = jnp.concatenate([high, mid, high, last], axis=0).astype(bf16)
        return jnp.dot(rows_ref[packed & 255][:, :PART], features, preferred_element_type=f32)

    def phi(dist_sq):
        dist_sq = jnp.maximum(dist_sq, 1e-12)
        gap = jnp.maximum(0.5 - dist_sq * lax.rsqrt(dist_sq), 0.0)
        gap_sq = gap * gap
        return gap_sq * gap_sq * (0.625 - gap)

    if keep is not None:
        stage_ref, sems, home = keep

    def copy_out(group):
        slot = lax.rem(group, RING)
        return pltpu.make_async_copy(stage_ref.at[pl.ds(slot, 1)], home(group), sems.at[slot])

    def step(at, carry):
        used = jnp.maximum(at - 2, 0) * GROUP
        first = jnp.minimum(at, groups - 1) * GROUP
        if keep is not None:
            stage = lax.rem(at + RING - 1, RING)
            before = at - 1 - RING

            @pl.when(before >= 0)
            def _():
                copy_out(before).wait()

        found = []
        for k in range(0, GROUP, 2):
            found += use(used, k, (tile_ref[k], tile_ref[k + 1]))
            for j in (k, k + 1):
                tile = phi(dist_ref[j]).astype(tile_ref.dtype)
                tile_ref[j] = tile
                if keep is not None:
                    stage_ref[stage, j] = tile
            for j in (k, k + 1):
                dist_ref[j] = distances(first + j)
        for out, block, value in found:
            out[block] += value
        if ahead is not None:
            ahead(jnp.minimum(at + 1, groups - 1) * GROUP)
        if keep is not None:

            @pl.when((at > 0) & (at <= groups))
            def _():
                copy_out(at - 1).start()

        return carry

    lax.fori_loop(0, jnp.where(groups > 0, groups + 2, 0), step, 0)
    if keep is not None:
        for back in range(1, RING):
            group = groups - back

            @pl.when(group >= 0)
            def _():
                copy_out(group).wait()


def stream(diag_tiles, pair_tiles, pairs, stage_ref, sems):
    ring = stage_ref.shape[0]
    diag_pairs = DIAG_GROUPS // 2
    total = diag_pairs + pairs

    def copy_in(tiles, at, slot):
        return pltpu.make_async_copy(tiles.at[pl.ds(2 * at, 2)], stage_ref.at[slot], sems.at[slot])

    def start(at):
        slot = lax.rem(at, ring)

        @pl.when(at < diag_pairs)
        def _():
            copy_in(diag_tiles, at, slot).start()

        @pl.when((at >= diag_pairs) & (at < total))
        def _():
            copy_in(pair_tiles, at - diag_pairs, slot).start()

    for at in range(ring - 1):
        start(jnp.int32(at))

    def loop(first, count, use):
        def step(at, carry):
            here = first + at
            start(here + ring - 1)
            slot = lax.rem(here, ring)
            copy_in(diag_tiles, 0, slot).wait()
            found = []
            for k in range(0, 2 * GROUP, 2):
                part, tile = k // GROUP, k % GROUP
                found += use(2 * at * GROUP, k, (stage_ref[slot, part, tile], stage_ref[slot, part, tile + 1]))
            for out, block, value in found:
                out[block] += value
            return carry

        lax.fori_loop(0, count, step, 0)

    return loop


def pair_body(step, me, groups, diag_list, pair_list, *refs):
    row = row_ids()

    def own(geo_ref, rows_ref, first):
        for k, turned in enumerate(row_features(geo_ref, me[0], first, GROUP)):
            spread(turned, rows_ref, first + 4 * k)

    if step == "diag":
        own_vec, own_geo, table_ref, own_out, diag_tiles = refs[:5]
        vec_ref, row_sum, col_sum, stage_ref, sems, rows_ref, cols_ref, dist_ref, tile_ref = refs[5:]
        column_rows((own_geo,), (me[0],), cols_ref)
        vector_rows((own_vec,), vec_ref, 1.0)
    elif step == "pairs":
        own_vec, right_vec, own_geo, right_geo, table_ref, stiff_ref, diag_ref = refs[:7]
        own_out, right_out, pair_tiles = refs[7:10]
        vec_ref, row_sum, col_sum, stage_ref, sems, rows_ref, cols_ref, dist_ref, tile_ref = refs[10:]
        column_rows((own_geo, right_geo), (me[0], me[0] + 1), cols_ref)
        vector_rows((own_vec, right_vec), vec_ref, 1.0)
    else:
        own_vec, right_vec, diag_tiles, pair_tiles, *outs, vec_ref, row_sum, col_sum, stage_ref, sems = refs
        pairs = lax.div(groups[0], 2)
        loop = stream(diag_tiles, pair_tiles, pairs, stage_ref, sems)
        vector_rows((own_vec, right_vec), vec_ref, 1.0)
    row_sum[...] = jnp.zeros_like(row_sum)
    col_sum[...] = jnp.zeros_like(col_sum)

    def two(first, second):
        return jnp.concatenate([first, second], axis=0).astype(bf16)

    def use_diag(first, k, pair):
        a, b = diag_list[first + k] & 255, diag_list[first + k + 1] & 255
        left = two(jnp.where(row == 3, 0.0, vec_ref[a]), jnp.where(row == 3, 0.0, vec_ref[b]))
        image = jnp.dot(
            left, jnp.concatenate(pair, axis=1), preferred_element_type=f32
        )
        return [(col_sum, a, image[:8, :TILE]), (col_sum, b, image[8:, TILE:])]

    def use_pair(first, k, pair):
        p, q = pair_list[first + k], pair_list[first + k + 1]
        row_a, col_a = p & 255, (p >> 8) & 2047
        row_b, col_b = q & 255, (q >> 8) & 2047
        left = two(vec_ref[row_a], vec_ref[row_b])
        if step == 2:
            left = left * 2
        image = jnp.dot(left, jnp.concatenate(pair, axis=1), preferred_element_type=f32)
        found = [(col_sum, col_a, image[:8, :TILE]), (col_sum, col_b, image[8:, TILE:])]
        if step != 2:
            image = lax.dot_general(
                two(vec_ref[col_a], vec_ref[col_b]),
                jnp.concatenate(pair, axis=0),
                (((1,), (1,)), ((), ())),
                preferred_element_type=f32,
            )
            found += [(row_sum, row_a, image[:8, :TILE]), (row_sum, row_b, image[8:, TILE:])]
        return found

    def diag_home(group, count=1):
        return diag_tiles.at[pl.ds(group, count)]

    def pair_home(group, count=1):
        return pair_tiles.at[pl.ds(group, count)]

    if step in ("diag", "pairs"):
        loop = functools.partial(
            tile_loop, rows_ref=rows_ref, cols_ref=cols_ref, table_ref=table_ref, dist_ref=dist_ref, tile_ref=tile_ref
        )

        def features(at, carry):
            own(own_geo, rows_ref=rows_ref, first=at * GROUP)
            return carry

        if step == "diag":
            features(jnp.int32(0), 0)
            loop(
                jnp.int32(DIAG_GROUPS),
                diag_list,
                use=use_diag,
                ahead=lambda first: own(own_geo, rows_ref=rows_ref, first=first),
                keep=(stage_ref, sems, diag_home),
            )
        else:
            lax.fori_loop(0, DIAG_GROUPS, features, 0)
            loop(groups[0], pair_list, use=use_pair, keep=(stage_ref, sems, pair_home))
    else:
        loop(0, DIAG_GROUPS // 2, use_diag)
        loop(DIAG_GROUPS // 2, pairs, use_pair)

    def fold(value):
        return value + pltpu.roll(value, 4, 0)

    if step != 2:
        if step == "diag":
            images = (own_out,)
        else:
            images = (own_out, right_out) if step == "pairs" else outs

        def finish(first):
            place = pl.ds(pl.multiple_of(first * TILE, 8 * TILE), 8 * TILE)
            sums = row_sum[pl.ds(first, 8)] + col_sum[pl.ds(first, 8)]
            image = jnp.concatenate([fold(sums[k])[:4] for k in range(8)], axis=1)
            if step == "pairs":
                fourth = lax.broadcasted_iota(i32, image.shape, 0) == 3
                image = image + diag_ref[:, place] + jnp.where(fourth, stiff_ref[:, place] - SHIFT, 0.0)
            images[0][:, place] = image
            if step != "diag":
                sums = col_sum[pl.ds(CB + first, 8)]
                images[1][:, place] = jnp.concatenate([fold(sums[k])[:4] for k in range(8)], axis=1)

        each_chunk(CB, finish)
    else:
        quad_out = outs[0]

        def finish(at, sums):
            return tuple(
                total + fold(col_sum[8 * at + k]) * fold(vec_ref[8 * at + k]) for k, total in enumerate(sums)
            )

        zero = jnp.zeros((8, TILE), f32)
        sums = lax.fori_loop(0, 2 * CB // 8, finish, (zero,) * 8)
        quad_out[...] = sum(sums)


def pair_call(step, *arrays, me, groups, diag_list, pair_list):
    smem = pl.BlockSpec(memory_space=pltpu.SMEM)
    vmem = pl.BlockSpec(memory_space=pltpu.VMEM)
    some = pl.BlockSpec(memory_space=pl.ANY)
    image = (jax.ShapeDtypeStruct((4, CB * TILE), f32), vmem)
    out = {
        "diag": (image, (jax.ShapeDtypeStruct((DIAG_GROUPS, GROUP, TILE, TILE), bf16), some)),
        "pairs": (image, image, (jax.ShapeDtypeStruct((PAIR_GROUPS, GROUP, TILE, TILE), bf16), some)),
        1: (image, image),
        2: ((jax.ShapeDtypeStruct((8, TILE), f32), vmem),),
    }[step]
    first = step in ("diag", "pairs")
    blocks = (1 if step == "diag" else 2) * CB + 1
    scratch = [
        pltpu.VMEM((blocks, 8, TILE), f32),
        pltpu.VMEM((CB, 8, TILE), f32),
        pltpu.VMEM((blocks, 8, TILE), f32),
        pltpu.VMEM((RING, GROUP, TILE, TILE) if first else (RING // 2, 2, GROUP, TILE, TILE), bf16),
        pltpu.SemaphoreType.DMA((RING,)),
    ]
    if first:
        scratch += [
            pltpu.VMEM((CB, TILE, TILE), bf16),
            pltpu.VMEM((blocks, 8, TILE), f32),
            pltpu.VMEM((GROUP, TILE, TILE), f32),
            pltpu.VMEM((GROUP, TILE, TILE), bf16),
        ]
    return pl.pallas_call(
        functools.partial(pair_body, step),
        out_shape=tuple(shape for shape, _ in out),
        in_specs=[smem] * 4 + ([vmem] * len(arrays) if first else [vmem, vmem, some, some]),
        out_specs=tuple(spec for _, spec in out),
        scratch_shapes=scratch,
        compiler_params=pltpu.CompilerParams(vmem_limit_bytes=48 * 2**20),
        cost_estimate=pl.CostEstimate(flops=2 * 10**9, bytes_accessed=10**8, transcendentals=0),
        name=f"pair_tiles_{step}",
    )(me, groups, diag_list, pair_list, *arrays)


def volume_body(me, groups, vol_list, vol_geo, *refs):
    geos, coefs = refs[:5], refs[5:10]
    table_ref, out, rows_ref, cols_ref, coef_ref, sums, dist_ref, tile_ref = refs[10:]
    column_rows(geos, [me[0] + k for k in range(-2, 3)], cols_ref)
    odd = lax.rem(me[0], 2)
    vector_rows(coefs, coef_ref, 0.0, [jnp.where(odd == 1, 4 - k, k) for k in range(5)])
    sums[...] = jnp.zeros_like(sums)

    def features(at, carry):
        for k, turned in enumerate(row_features(vol_geo, me[0], 16 * at, 16)):
            spread(turned, rows_ref, 16 * at + 4 * k)
        return carry

    lax.fori_loop(0, VB // 16, features, 0)

    def use(first, k, pair):
        dims = (((1,), (1,)), ((), ()))
        p, q = vol_list[first + k], vol_list[first + k + 1]
        left = jnp.concatenate([coef_ref[(p >> 8) & 2047], coef_ref[(q >> 8) & 2047]], axis=0).astype(bf16)
        highs, lows = [], []
        for tile in pair:
            high = tile.astype(bf16)
            highs.append(high)
            lows.append((tile - high.astype(f32)).astype(bf16))
        image = lax.dot_general(left, jnp.concatenate(highs, axis=0), dims, preferred_element_type=f32)
        image += lax.dot_general(left, jnp.concatenate(lows, axis=0), dims, preferred_element_type=f32)
        return [(sums, p & 255, image[:8, :TILE]), (sums, q & 255, image[8:, TILE:])]

    tile_loop(groups[0], vol_list, rows_ref, cols_ref, table_ref, dist_ref, tile_ref, use)

    def finish(first):
        value = sums[pl.ds(first, 8)]
        rows = [(value[k] + pltpu.roll(value[k], 4, 0))[:3] for k in range(8)]
        out[:, pl.ds(pl.multiple_of(first * TILE, 8 * TILE), 8 * TILE)] = jnp.concatenate(rows, axis=1) * TILE**0.5

    each_chunk(VB, finish)


def volume_call(me, groups, vol_list, *arrays):
    smem = pl.BlockSpec(memory_space=pltpu.SMEM)
    vmem = pl.BlockSpec(memory_space=pltpu.VMEM)
    return pl.pallas_call(
        volume_body,
        out_shape=jax.ShapeDtypeStruct((3, VB * TILE), f32),
        in_specs=[smem] * 3 + [vmem] * len(arrays),
        out_specs=vmem,
        scratch_shapes=[
            pltpu.VMEM((VB, TILE, TILE), bf16),
            pltpu.VMEM((5 * CB + 1, 8, TILE), f32),
            pltpu.VMEM((5 * CB + 1, 8, TILE), f32),
            pltpu.VMEM((VB, 8, TILE), f32),
            pltpu.VMEM((GROUP, TILE, TILE), f32),
            pltpu.VMEM((GROUP, TILE, TILE), f32),
        ],
        compiler_params=pltpu.CompilerParams(vmem_limit_bytes=56 * 2**20),
        cost_estimate=pl.CostEstimate(flops=2 * 10**9, bytes_accessed=10**8, transcendentals=0),
        name="volume_tiles",
    )(me, groups, vol_list, *arrays)


def cg_weights(moment):
    def gram(first, second):
        return sum(a * b * moment[i + j] for i, a in enumerate(first) for j, b in enumerate(second))

    def image(vector):
        grown = [SHIFT * a for a in vector] + [0.0]
        return [a + (vector[k - 1] if k else 0.0) for k, a in enumerate(grown)]

    def axpy(scale, first, second):
        size = max(len(first), len(second))
        pad = lambda v: list(v) + [0.0] * (size - len(v))
        return [scale * a + b for a, b in zip(pad(first), pad(second))]

    one = jnp.ones_like(moment[0])
    residual, direction, total = [one], [one], [0.0 * one]
    norm = gram(residual, residual)
    for step in range(3):
        grown = image(direction)
        length = norm / gram(direction, grown)
        total = axpy(length, direction, total)
        if step < 2:
            residual = axpy(-length, grown, residual)
            norm_next = gram(residual, residual)
            direction = axpy(norm_next / norm, direction, residual)
            norm = norm_next
    return total


def comp_sum(first, second):
    return jnp.sum(first * second, axis=1)


def body(ctrl_points, ctrl_disp, stiffness, pair_rows, pair_cols, pair_count, vol_points, vol_rows, vol_cols, vol_count):
    me = lax.axis_index("nodes")
    devices = lax.axis_size("nodes")
    order = (2, 1, 0, -1, -2)

    geo = {0: ctrl_points, -1: from_behind(ctrl_points, "nodes", -1)}
    beside = from_behind(ctrl_disp, "nodes", -1)
    table = offset_table()

    slots = lax.iota(i32, MAXT)
    right = pair_cols >= CB
    live = (slots < pair_count[0]) & (~right | (me < devices - 1))
    code = offset_code(right.astype(i32), pair_rows, pair_cols % CB)
    pair_list = jnp.where(live, pair_rows | (pair_cols << 8) | (code << 19), (2 * CB) << 8)
    pair_groups = (pair_count + 2 * GROUP - 1) // (2 * GROUP) * 2
    own = lax.iota(i32, CB)
    diag_list = own | (own << 8) | (62 << 19)

    slots = lax.iota(i32, MAXV)
    step_x = vol_cols // CB - 2
    source = me + step_x
    live = (slots < vol_count[0]) & (source >= 0) & (source < devices)
    code = offset_code(step_x, vol_rows, vol_cols % CB)
    vol_list = jnp.where(live, vol_rows | (vol_cols << 8) | (code << 19), (5 * CB) << 8)
    vol_groups = (vol_count + GROUP - 1) // GROUP
    here = me.astype(i32)[None]

    images = functools.partial(pair_call, me=here, groups=pair_groups, diag_list=diag_list, pair_list=pair_list)

    def exchanged(own_part, right_part):
        back = from_behind(right_part, "nodes", 1)
        ahead = from_behind(own_part, "nodes", -1)
        return own_part + back, ahead + right_part

    own_part, diag_tiles = images("diag", ctrl_disp, ctrl_points, table)
    own_part, right_part, pair_tiles = images(
        "pairs", ctrl_disp, beside, ctrl_points, geo[-1], table, stiffness[None, :], own_part
    )
    tiles = (diag_tiles, pair_tiles)
    total, total_beside = exchanged(own_part, right_part)
    diagonal, diagonal_beside = total[3:4], total_beside[3:4]
    first = total[:3] + diagonal * ctrl_disp
    first_beside = total_beside[:3] + diagonal_beside * beside
    later, first = lax.optimization_barrier((ctrl_points, first))
    for offset in (1, 2, -2):
        geo[offset] = from_behind(later, "nodes", offset)
    own_part, right_part = images(1, first, first_beside, *tiles)
    own_part, right_part, geo[1], geo[2], geo[-2] = lax.optimization_barrier(
        (own_part, right_part, geo[1], geo[2], geo[-2])
    )
    total, total_beside = exchanged(own_part, right_part)
    second = total[:3] + diagonal * first
    second_beside = total_beside[:3] + diagonal_beside * first_beside
    (quad,) = images(2, second, second_beside, *tiles)
    moments = jnp.concatenate(
        [
            comp_sum(ctrl_disp, ctrl_disp),
            comp_sum(ctrl_disp, first),
            comp_sum(first, first),
            comp_sum(first, second),
            comp_sum(second, second),
            jnp.sum(quad, axis=1)[:3] + comp_sum(diagonal * second, second),
            jnp.zeros((TILE - 18,), f32),
        ]
    )

    sent = jnp.broadcast_to(moments[None, None, :], (devices, 1, TILE))
    moments = jnp.sum(lax.all_to_all(sent, "nodes", 0, 0, tiled=True), axis=(0, 1))
    weights = cg_weights([moments[3 * k : 3 * k + 3] for k in range(6)])
    coef = sum(w[:, None] * u for w, u in zip(weights, (ctrl_disp, first, second)))
    near = around(coef, "nodes")
    moved = volume_call(here, vol_groups, vol_list, vol_points, *[geo[k] for k in order], *near, table)
    return (coef, moved)


def solution(mesh):
    across = P(None, "nodes")
    flat = P("nodes")
    return jax.shard_map(
        body,
        mesh=mesh,
        in_specs=(across, across, flat, flat, flat, flat, across, flat, flat, flat),
        out_specs=(across, across),
        check_vma=False,
    )
```

```python
import functools

import jax
import jax.numpy as jnp
from jax import lax
from jax.experimental import pallas as pl
from jax.experimental.pallas import tpu as pltpu
from jax.sharding import PartitionSpec as P

TILE = 128
SIDE = 16
CB = 256
VB = 256
MAXT = 768
MAXV = 512
GROUP = 16
PART = 32
RING = 8
CHUNK = 16
DIAG_GROUPS = CB // GROUP
PAIR_GROUPS = MAXT // GROUP
SHIFT = 0.75
FAR = 64.0

f32 = jnp.float32
bf16 = jnp.bfloat16
i32 = jnp.int32


def from_behind(block, axis, distance):
    devices = range(lax.axis_size(axis))
    route = [(i - distance, i) for i in devices if i - distance in devices]
    return lax.ppermute(block, axis, route)


def around(block, axis):
    devices = range(lax.axis_size(axis))

    def send(value, target):
        return lax.ppermute(value, axis, [(i, target(i)) for i in devices if target(i) in devices])

    far = send(block, lambda i: i - 2 if i % 2 else i + 2)
    near = send(block, lambda i: i + 1 if i % 2 else i - 1)
    partner = send(block, lambda i: i ^ 1)
    shared = send(near, lambda i: i ^ 1)
    return [far, near, block, partner, shared]


def offset_table():
    code = lax.iota(i32, 125)
    step_x = (code // 25 - 2).astype(f32) * 0.25
    step_y = (code // 5 % 5 - 2).astype(f32) * 0.5
    step_z = (code % 5 - 2).astype(f32) * 0.5
    zero = jnp.zeros_like(step_x)
    rows = jnp.stack([step_x, step_y, step_z, step_x, step_y, step_z, zero, zero], axis=1)
    return jnp.broadcast_to(rows[:, :, None], (125, 8, TILE))


def offset_code(step_x, row_cell, col_cell):
    step_y = jnp.clip(col_cell // SIDE - row_cell // SIDE, -2, 2)
    step_z = jnp.clip(col_cell % SIDE - row_cell % SIDE, -2, 2)
    return (step_x + 2) * 25 + (step_y + 2) * 5 + step_z + 2


def row_ids():
    return lax.broadcasted_iota(i32, (8, TILE), 0)


def split(value):
    high = value.astype(bf16).astype(f32)
    return high, value - high


def three_rows(ref, first, count):
    value = ref[:, pl.ds(pl.multiple_of(first * TILE, count * TILE), count * TILE)]
    rest = jnp.zeros((5, TILE), f32)
    return [jnp.concatenate([value[:, k * TILE : (k + 1) * TILE], rest], axis=0) for k in range(count)]


def local_coords(blocks, first, device):
    row = row_ids()
    along_x = jnp.where(row == 0, 1.0, 0.0) * (device.astype(f32) + 0.5)
    along_y = jnp.where(row == 1, 2.0, 0.0) * ((first >> 4).astype(f32) + 0.5)
    along_z = jnp.where(row == 2, 2.0, 0.0)
    fixed = along_x + along_y
    cell = (first & 15).astype(f32) + 0.5
    return [(block - (fixed + along_z * (cell + k))) * 0.25 for k, block in enumerate(blocks)]


def each_chunk(count, todo, chunk=8):
    def step(at, carry):
        todo(chunk * at)
        return carry

    lax.fori_loop(0, count // chunk, step, 0)


def column_rows(geo_refs, devices, cols_ref):
    unit = jnp.where(row_ids() == 6, 1.0, 0.0)
    for at, ref in enumerate(geo_refs):

        def fill(first):
            local = local_coords(three_rows(ref, first, CHUNK), first, devices[at])
            rows = [block + pltpu.roll(block, 3, 0) + unit for block in local]
            cols_ref[pl.ds(at * CB + first, CHUNK)] = jnp.stack(rows)

        each_chunk(CB, fill, CHUNK)
    cols_ref[len(geo_refs) * CB] = jnp.full((8, TILE), FAR, f32)


def vector_rows(refs, vec_ref, unit, places=None):
    unit = jnp.where(row_ids() == 3, unit, 0.0)
    for at, ref in enumerate(refs):

        def fill(first):
            rows = []
            for block in three_rows(ref, first, CHUNK):
                high, low = split(block)
                rows.append(high + pltpu.roll(low, 4, 0) + unit)
            vec_ref[pl.ds((at if places is None else places[at]) * CB + first, CHUNK)] = jnp.stack(rows)

        each_chunk(CB, fill, CHUNK)
    vec_ref[len(refs) * CB] = jnp.zeros((8, TILE), f32)


def row_features(geo_ref, device, first, count):
    row = row_ids()
    middle = (row >= 3) & (row < 6)

    def features(coords):
        norm = jnp.sum(coords * coords, axis=0, keepdims=True)
        full = jnp.where(middle, 1.0, jnp.where(row == 6, norm, -2.0 * coords))
        high, rest = split(full)
        mid, low = split(rest)
        last = jnp.where(row < 3, mid, jnp.where(middle, 1.0, low))
        return [high, high, mid, last]

    blocks = local_coords(three_rows(geo_ref, first, count), first, device)
    parts = [features(block) for block in blocks]
    return [
        jnp.transpose(jnp.concatenate(sum(parts[k : k + 4], []), axis=0).astype(bf16)) for k in range(0, count, 4)
    ]


def spread(turned, rows_ref, first):
    for j in range(4):
        rows_ref[first + j] = turned if j == 0 else pltpu.roll(turned, TILE - j * PART, 1)


def tile_loop(groups, listed, rows_ref, cols_ref, table_ref, dist_ref, tile_ref, use, ahead=None, keep=None):
    row = row_ids()
    squares = (row >= 3) & (row < 6)
    unit = row == 6
    dist_ref[...] = jnp.full_like(dist_ref, FAR)
    tile_ref[...] = jnp.zeros_like(tile_ref)

    def distances(slot):
        packed = listed[slot]
        moved = cols_ref[(packed >> 8) & 2047] + table_ref[packed >> 19]
        full = jnp.where(squares, moved * moved, moved)
        high, rest = split(full)
        mid, low = split(rest)
        last = jnp.where(squares, low, jnp.where(unit, 1.0, mid))
        features = jnp.concatenate([high, mid, high, last], axis=0).astype(bf16)
        return jnp.dot(rows_ref[packed & 255][:, :PART], features, preferred_element_type=f32)

    def phi(dist_sq):
        dist_sq = jnp.maximum(dist_sq, 1e-12)
        gap = jnp.maximum(0.5 - dist_sq * lax.rsqrt(dist_sq), 0.0)
        gap_sq = gap * gap
        return gap_sq * gap_sq * (0.625 - gap)

    if keep is not None:
        stage_ref, sems, home = keep

    def copy_out(group):
        slot = lax.rem(group, RING)
        return pltpu.make_async_copy(stage_ref.at[pl.ds(slot, 1)], home(group), sems.at[slot])

    def step(at, carry):
        used = jnp.maximum(at - 2, 0) * GROUP
        first = jnp.minimum(at, groups - 1) * GROUP
        if keep is not None:
            stage = lax.rem(at + RING - 1, RING)
            before = at - 1 - RING

            @pl.when(before >= 0)
            def _():
                copy_out(before).wait()

        found = []
        for k in range(0, GROUP, 2):
            found += use(used, k, (tile_ref[k], tile_ref[k + 1]))
            for j in (k, k + 1):
                tile = phi(dist_ref[j]).astype(tile_ref.dtype)
                tile_ref[j] = tile
                if keep is not None:
                    stage_ref[stage, j] = tile
            for j in (k, k + 1):
                dist_ref[j] = distances(first + j)
        for out, block, value in found:
            out[block] += value
        if ahead is not None:
            ahead(jnp.minimum(at + 1, groups - 1) * GROUP)
        if keep is not None:

            @pl.when((at > 0) & (at <= groups))
            def _():
                copy_out(at - 1).start()

        return carry

    lax.fori_loop(0, jnp.where(groups > 0, groups + 2, 0), step, 0)
    if keep is not None:
        for back in range(1, RING):
            group = groups - back

            @pl.when(group >= 0)
            def _():
                copy_out(group).wait()


def stream(diag_tiles, pair_tiles, pairs, stage_ref, sems):
    ring = stage_ref.shape[0]
    diag_pairs = DIAG_GROUPS // 2
    total = diag_pairs + pairs

    def copy_in(tiles, at, slot):
        return pltpu.make_async_copy(tiles.at[pl.ds(2 * at, 2)], stage_ref.at[slot], sems.at[slot])

    def start(at):
        slot = lax.rem(at, ring)

        @pl.when(at < diag_pairs)
        def _():
            copy_in(diag_tiles, at, slot).start()

        @pl.when((at >= diag_pairs) & (at < total))
        def _():
            copy_in(pair_tiles, at - diag_pairs, slot).start()

    for at in range(ring - 1):
        start(jnp.int32(at))

    def loop(first, count, use):
        def step(at, carry):
            here = first + at
            start(here + ring - 1)
            slot = lax.rem(here, ring)
            copy_in(diag_tiles, 0, slot).wait()
            found = []
            for k in range(0, 2 * GROUP, 2):
                part, tile = k // GROUP, k % GROUP
                found += use(2 * at * GROUP, k, (stage_ref[slot, part, tile], stage_ref[slot, part, tile + 1]))
            for out, block, value in found:
                out[block] += value
            return carry

        lax.fori_loop(0, count, step, 0)

    return loop


def pair_body(step, me, groups, diag_list, pair_list, *refs):
    row = row_ids()

    def own(geo_ref, rows_ref, first):
        for k, turned in enumerate(row_features(geo_ref, me[0], first, GROUP)):
            spread(turned, rows_ref, first + 4 * k)

    if step == "diag":
        own_vec, own_geo, table_ref, own_out, diag_tiles = refs[:5]
        vec_ref, row_sum, col_sum, stage_ref, sems, rows_ref, cols_ref, dist_ref, tile_ref = refs[5:]
        column_rows((own_geo,), (me[0],), cols_ref)
        vector_rows((own_vec,), vec_ref, 1.0)
    elif step == "pairs":
        own_vec, right_vec, own_geo, right_geo, table_ref, stiff_ref, diag_ref = refs[:7]
        own_out, right_out, pair_tiles = refs[7:10]
        vec_ref, row_sum, col_sum, stage_ref, sems, rows_ref, cols_ref, dist_ref, tile_ref = refs[10:]
        column_rows((own_geo, right_geo), (me[0], me[0] + 1), cols_ref)
        vector_rows((own_vec, right_vec), vec_ref, 1.0)
    else:
        own_vec, right_vec, diag_tiles, pair_tiles, *outs, vec_ref, row_sum, col_sum, stage_ref, sems = refs
        pairs = lax.div(groups[0], 2)
        loop = stream(diag_tiles, pair_tiles, pairs, stage_ref, sems)
        vector_rows((own_vec, right_vec), vec_ref, 1.0)
    row_sum[...] = jnp.zeros_like(row_sum)
    col_sum[...] = jnp.zeros_like(col_sum)

    def two(first, second):
        return jnp.concatenate([first, second], axis=0).astype(bf16)

    def use_diag(first, k, pair):
        a, b = diag_list[first + k] & 255, diag_list[first + k + 1] & 255
        left = two(jnp.where(row == 3, 0.0, vec_ref[a]), jnp.where(row == 3, 0.0, vec_ref[b]))
        image = jnp.dot(
            left, jnp.concatenate(pair, axis=1), preferred_element_type=f32
        )
        return [(col_sum, a, image[:8, :TILE]), (col_sum, b, image[8:, TILE:])]

    def use_pair(first, k, pair):
        p, q = pair_list[first + k], pair_list[first + k + 1]
        row_a, col_a = p & 255, (p >> 8) & 2047
        row_b, col_b = q & 255, (q >> 8) & 2047
        left = two(vec_ref[row_a], vec_ref[row_b])
        if step == 2:
            left = left * 2
        image = jnp.dot(left, jnp.concatenate(pair, axis=1), preferred_element_type=f32)
        found = [(col_sum, col_a, image[:8, :TILE]), (col_sum, col_b, image[8:, TILE:])]
        if step != 2:
            image = lax.dot_general(
                two(vec_ref[col_a], vec_ref[col_b]),
                jnp.concatenate(pair, axis=0),
                (((1,), (1,)), ((), ())),
                preferred_element_type=f32,
            )
            found += [(row_sum, row_a, image[:8, :TILE]), (row_sum, row_b, image[8:, TILE:])]
        return found

    def diag_home(group, count=1):
        return diag_tiles.at[pl.ds(group, count)]

    def pair_home(group, count=1):
        return pair_tiles.at[pl.ds(group, count)]

    if step in ("diag", "pairs"):
        loop = functools.partial(
            tile_loop, rows_ref=rows_ref, cols_ref=cols_ref, table_ref=table_ref, dist_ref=dist_ref, tile_ref=tile_ref
        )

        def features(at, carry):
            own(own_geo, rows_ref=rows_ref, first=at * GROUP)
            return carry

        if step == "diag":
            features(jnp.int32(0), 0)
            loop(
                jnp.int32(DIAG_GROUPS),
                diag_list,
                use=use_diag,
                ahead=lambda first: own(own_geo, rows_ref=rows_ref, first=first),
                keep=(stage_ref, sems, diag_home),
            )
        else:
            lax.fori_loop(0, DIAG_GROUPS, features, 0)
            loop(groups[0], pair_list, use=use_pair, keep=(stage_ref, sems, pair_home))
    else:
        loop(0, DIAG_GROUPS // 2, use_diag)
        loop(DIAG_GROUPS // 2, pairs, use_pair)

    def fold(value):
        return value + pltpu.roll(value, 4, 0)

    if step != 2:
        if step == "diag":
            images = (own_out,)
        else:
            images = (own_out, right_out) if step == "pairs" else outs

        def finish(first):
            place = pl.ds(pl.multiple_of(first * TILE, 8 * TILE), 8 * TILE)
            sums = row_sum[pl.ds(first, 8)] + col_sum[pl.ds(first, 8)]
            image = jnp.concatenate([fold(sums[k])[:4] for k in range(8)], axis=1)
            if step == "pairs":
                fourth = lax.broadcasted_iota(i32, image.shape, 0) == 3
                image = image + diag_ref[:, place] + jnp.where(fourth, stiff_ref[:, place] - SHIFT, 0.0)
            images[0][:, place] = image
            if step != "diag":
                sums = col_sum[pl.ds(CB + first, 8)]
                images[1][:, place] = jnp.concatenate([fold(sums[k])[:4] for k in range(8)], axis=1)

        each_chunk(CB, finish)
    else:
        quad_out = outs[0]

        def finish(at, sums):
            return tuple(
                total + fold(col_sum[8 * at + k]) * fold(vec_ref[8 * at + k]) for k, total in enumerate(sums)
            )

        zero = jnp.zeros((8, TILE), f32)
        sums = lax.fori_loop(0, 2 * CB // 8, finish, (zero,) * 8)
        quad_out[...] = sum(sums)


def pair_call(step, *arrays, me, groups, diag_list, pair_list):
    smem = pl.BlockSpec(memory_space=pltpu.SMEM)
    vmem = pl.BlockSpec(memory_space=pltpu.VMEM)
    some = pl.BlockSpec(memory_space=pl.ANY)
    image = (jax.ShapeDtypeStruct((4, CB * TILE), f32), vmem)
    out = {
        "diag": (image, (jax.ShapeDtypeStruct((DIAG_GROUPS, GROUP, TILE, TILE), bf16), some)),
        "pairs": (image, image, (jax.ShapeDtypeStruct((PAIR_GROUPS, GROUP, TILE, TILE), bf16), some)),
        1: (image, image),
        2: ((jax.ShapeDtypeStruct((8, TILE), f32), vmem),),
    }[step]
    first = step in ("diag", "pairs")
    blocks = (1 if step == "diag" else 2) * CB + 1
    scratch = [
        pltpu.VMEM((blocks, 8, TILE), f32),
        pltpu.VMEM((CB, 8, TILE), f32),
        pltpu.VMEM((blocks, 8, TILE), f32),
        pltpu.VMEM((RING, GROUP, TILE, TILE) if first else (RING // 2, 2, GROUP, TILE, TILE), bf16),
        pltpu.SemaphoreType.DMA((RING,)),
    ]
    if first:
        scratch += [
            pltpu.VMEM((CB, TILE, TILE), bf16),
            pltpu.VMEM((blocks, 8, TILE), f32),
            pltpu.VMEM((GROUP, TILE, TILE), f32),
            pltpu.VMEM((GROUP, TILE, TILE), bf16),
        ]
    return pl.pallas_call(
        functools.partial(pair_body, step),
        out_shape=tuple(shape for shape, _ in out),
        in_specs=[smem] * 4 + ([vmem] * len(arrays) if first else [vmem, vmem, some, some]),
        out_specs=tuple(spec for _, spec in out),
        scratch_shapes=scratch,
        compiler_params=pltpu.CompilerParams(vmem_limit_bytes=48 * 2**20),
        cost_estimate=pl.CostEstimate(flops=2 * 10**9, bytes_accessed=10**8, transcendentals=0),
        name=f"pair_tiles_{step}",
    )(me, groups, diag_list, pair_list, *arrays)


def volume_body(me, groups, vol_list, vol_geo, *refs):
    geos, coefs = refs[:5], refs[5:10]
    table_ref, out, rows_ref, cols_ref, coef_ref, sums, dist_ref, tile_ref = refs[10:]
    column_rows(geos, [me[0] + k for k in range(-2, 3)], cols_ref)
    odd = lax.rem(me[0], 2)
    vector_rows(coefs, coef_ref, 0.0, [jnp.where(odd == 1, 4 - k, k) for k in range(5)])
    sums[...] = jnp.zeros_like(sums)

    def features(at, carry):
        for k, turned in enumerate(row_features(vol_geo, me[0], 16 * at, 16)):
            spread(turned, rows_ref, 16 * at + 4 * k)
        return carry

    lax.fori_loop(0, VB // 16, features, 0)

    def use(first, k, pair):
        dims = (((1,), (1,)), ((), ()))
        p, q = vol_list[first + k], vol_list[first + k + 1]
        left = jnp.concatenate([coef_ref[(p >> 8) & 2047], coef_ref[(q >> 8) & 2047]], axis=0).astype(bf16)
        highs, lows = [], []
        for tile in pair:
            high = tile.astype(bf16)
            highs.append(high)
            lows.append((tile - high.astype(f32)).astype(bf16))
        image = lax.dot_general(left, jnp.concatenate(highs, axis=0), dims, preferred_element_type=f32)
        image += lax.dot_general(left, jnp.concatenate(lows, axis=0), dims, preferred_element_type=f32)
        return [(sums, p & 255, image[:8, :TILE]), (sums, q & 255, image[8:, TILE:])]

    tile_loop(groups[0], vol_list, rows_ref, cols_ref, table_ref, dist_ref, tile_ref, use)

    def finish(first):
        value = sums[pl.ds(first, 8)]
        rows = [(value[k] + pltpu.roll(value[k], 4, 0))[:3] for k in range(8)]
        out[:, pl.ds(pl.multiple_of(first * TILE, 8 * TILE), 8 * TILE)] = jnp.concatenate(rows, axis=1) * TILE**0.5

    each_chunk(VB, finish)


def volume_call(me, groups, vol_list, *arrays):
    smem = pl.BlockSpec(memory_space=pltpu.SMEM)
    vmem = pl.BlockSpec(memory_space=pltpu.VMEM)
    return pl.pallas_call(
        volume_body,
        out_shape=jax.ShapeDtypeStruct((3, VB * TILE), f32),
        in_specs=[smem] * 3 + [vmem] * len(arrays),
        out_specs=vmem,
        scratch_shapes=[
            pltpu.VMEM((VB, TILE, TILE), bf16),
            pltpu.VMEM((5 * CB + 1, 8, TILE), f32),
            pltpu.VMEM((5 * CB + 1, 8, TILE), f32),
            pltpu.VMEM((VB, 8, TILE), f32),
            pltpu.VMEM((GROUP, TILE, TILE), f32),
            pltpu.VMEM((GROUP, TILE, TILE), f32),
        ],
        compiler_params=pltpu.CompilerParams(vmem_limit_bytes=56 * 2**20),
        cost_estimate=pl.CostEstimate(flops=2 * 10**9, bytes_accessed=10**8, transcendentals=0),
        name="volume_tiles",
    )(me, groups, vol_list, *arrays)


def cg_weights(moment):
    def gram(first, second):
        return sum(a * b * moment[i + j] for i, a in enumerate(first) for j, b in enumerate(second))

    def image(vector):
        grown = [SHIFT * a for a in vector] + [0.0]
        return [a + (vector[k - 1] if k else 0.0) for k, a in enumerate(grown)]

    def axpy(scale, first, second):
        size = max(len(first), len(second))
        pad = lambda v: list(v) + [0.0] * (size - len(v))
        return [scale * a + b for a, b in zip(pad(first), pad(second))]

    one = jnp.ones_like(moment[0])
    residual, direction, total = [one], [one], [0.0 * one]
    norm = gram(residual, residual)
    for step in range(3):
        grown = image(direction)
        length = norm / gram(direction, grown)
        total = axpy(length, direction, total)
        if step < 2:
            residual = axpy(-length, grown, residual)
            norm_next = gram(residual, residual)
            direction = axpy(norm_next / norm, direction, residual)
            norm = norm_next
    return total


def comp_sum(first, second):
    return jnp.sum(first * second, axis=1)


def body(ctrl_points, ctrl_disp, stiffness, pair_rows, pair_cols, pair_count, vol_points, vol_rows, vol_cols, vol_count):
    me = lax.axis_index("nodes")
    devices = lax.axis_size("nodes")
    order = (2, 1, 0, -1, -2)

    geo = {0: ctrl_points, -1: from_behind(ctrl_points, "nodes", -1)}
    beside = from_behind(ctrl_disp, "nodes", -1)
    table = offset_table()

    slots = lax.iota(i32, MAXT)
    right = pair_cols >= CB
    live = (slots < pair_count[0]) & (~right | (me < devices - 1))
    code = offset_code(right.astype(i32), pair_rows, pair_cols % CB)
    pair_list = jnp.where(live, pair_rows | (pair_cols << 8) | (code << 19), (2 * CB) << 8)
    pair_groups = (pair_count + 2 * GROUP - 1) // (2 * GROUP) * 2
    own = lax.iota(i32, CB)
    diag_list = own | (own << 8) | (62 << 19)

    slots = lax.iota(i32, MAXV)
    step_x = vol_cols // CB - 2
    source = me + step_x
    live = (slots < vol_count[0]) & (source >= 0) & (source < devices)
    code = offset_code(step_x, vol_rows, vol_cols % CB)
    vol_list = jnp.where(live, vol_rows | (vol_cols << 8) | (code << 19), (5 * CB) << 8)
    vol_groups = (vol_count + GROUP - 1) // GROUP
    here = me.astype(i32)[None]

    images = functools.partial(pair_call, me=here, groups=pair_groups, diag_list=diag_list, pair_list=pair_list)

    def exchanged(own_part, right_part):
        back = from_behind(right_part, "nodes", 1)
        ahead = from_behind(own_part, "nodes", -1)
        return own_part + back, ahead + right_part

    own_part, diag_tiles = images("diag", ctrl_disp, ctrl_points, table)
    own_part, right_part, pair_tiles = images(
        "pairs", ctrl_disp, beside, ctrl_points, geo[-1], table, stiffness[None, :], own_part
    )
    tiles = (diag_tiles, pair_tiles)
    total, total_beside = exchanged(own_part, right_part)
    diagonal, diagonal_beside = total[3:4], total_beside[3:4]
    first = total[:3] + diagonal * ctrl_disp
    first_beside = total_beside[:3] + diagonal_beside * beside
    later, first = lax.optimization_barrier((ctrl_points, first))
    geo[1] = from_behind(later, "nodes", 1)
    own_part, right_part = images(1, first, first_beside, *tiles)
    own_part, right_part, geo[1] = lax.optimization_barrier((own_part, right_part, geo[1]))
    total, total_beside = exchanged(own_part, right_part)
    second = total[:3] + diagonal * first
    second_beside = total_beside[:3] + diagonal_beside * first_beside
    later, second = lax.optimization_barrier((ctrl_points, second))
    for offset in (2, -2):
        geo[offset] = from_behind(later, "nodes", offset)
    (quad,) = images(2, second, second_beside, *tiles)
    quad, geo[2], geo[-2] = lax.optimization_barrier((quad, geo[2], geo[-2]))
    moments = jnp.concatenate(
        [
            comp_sum(ctrl_disp, ctrl_disp),
            comp_sum(ctrl_disp, first),
            comp_sum(first, first),
            comp_sum(first, second),
            comp_sum(second, second),
            jnp.sum(quad, axis=1)[:3] + comp_sum(diagonal * second, second),
            jnp.zeros((TILE - 18,), f32),
        ]
    )

    sent = jnp.broadcast_to(moments[None, None, :], (devices, 1, TILE))
    moments = jnp.sum(lax.all_to_all(sent, "nodes", 0, 0, tiled=True), axis=(0, 1))
    weights = cg_weights([moments[3 * k : 3 * k + 3] for k in range(6)])
    coef = sum(w[:, None] * u for w, u in zip(weights, (ctrl_disp, first, second)))
    near = around(coef, "nodes")
    moved = volume_call(here, vol_groups, vol_list, vol_points, *[geo[k] for k in order], *near, table)
    return (coef, moved)


def solution(mesh):
    across = P(None, "nodes")
    flat = P("nodes")
    return jax.shard_map(
        body,
        mesh=mesh,
        in_specs=(across, across, flat, flat, flat, flat, across, flat, flat, flat),
        out_specs=(across, across),
        check_vma=False,
    )
```

```python
import functools

import jax
import jax.numpy as jnp
from jax import lax
from jax.experimental import pallas as pl
from jax.experimental.pallas import tpu as pltpu
from jax.sharding import PartitionSpec as P

TILE = 128
SIDE = 16
CB = 256
VB = 256
MAXT = 768
MAXV = 512
GROUP = 16
PART = 32
RING = 8
CHUNK = 16
DIAG_GROUPS = CB // GROUP
PAIR_GROUPS = MAXT // GROUP
SHIFT = 0.75
FAR = 64.0

f32 = jnp.float32
bf16 = jnp.bfloat16
i32 = jnp.int32


def from_behind(block, axis, distance):
    devices = range(lax.axis_size(axis))
    route = [(i - distance, i) for i in devices if i - distance in devices]
    return lax.ppermute(block, axis, route)


def around(block, axis):
    devices = range(lax.axis_size(axis))

    def send(value, target):
        return lax.ppermute(value, axis, [(i, target(i)) for i in devices if target(i) in devices])

    far = send(block, lambda i: i - 2 if i % 2 else i + 2)
    near = send(block, lambda i: i + 1 if i % 2 else i - 1)
    partner = send(block, lambda i: i ^ 1)
    shared = send(near, lambda i: i ^ 1)
    return [far, near, block, partner, shared]


def offset_table():
    code = lax.iota(i32, 125)
    step_x = (code // 25 - 2).astype(f32) * 0.25
    step_y = (code // 5 % 5 - 2).astype(f32) * 0.5
    step_z = (code % 5 - 2).astype(f32) * 0.5
    zero = jnp.zeros_like(step_x)
    rows = jnp.stack([step_x, step_y, step_z, step_x, step_y, step_z, zero, zero], axis=1)
    return jnp.broadcast_to(rows[:, :, None], (125, 8, TILE))


def offset_code(step_x, row_cell, col_cell):
    step_y = jnp.clip(col_cell // SIDE - row_cell // SIDE, -2, 2)
    step_z = jnp.clip(col_cell % SIDE - row_cell % SIDE, -2, 2)
    return (step_x + 2) * 25 + (step_y + 2) * 5 + step_z + 2


def row_ids():
    return lax.broadcasted_iota(i32, (8, TILE), 0)


def split(value):
    high = value.astype(bf16).astype(f32)
    return high, value - high


def three_rows(ref, first, count):
    value = ref[:, pl.ds(pl.multiple_of(first * TILE, count * TILE), count * TILE)]
    rest = jnp.zeros((5, TILE), f32)
    return [jnp.concatenate([value[:, k * TILE : (k + 1) * TILE], rest], axis=0) for k in range(count)]


def local_coords(blocks, first, device):
    row = row_ids()
    along_x = jnp.where(row == 0, 1.0, 0.0) * (device.astype(f32) + 0.5)
    along_y = jnp.where(row == 1, 2.0, 0.0) * ((first >> 4).astype(f32) + 0.5)
    along_z = jnp.where(row == 2, 2.0, 0.0)
    fixed = along_x + along_y
    cell = (first & 15).astype(f32) + 0.5
    return [(block - (fixed + along_z * (cell + k))) * 0.25 for k, block in enumerate(blocks)]


def each_chunk(count, todo, chunk=8):
    def step(at, carry):
        todo(chunk * at)
        return carry

    lax.fori_loop(0, count // chunk, step, 0)


def column_rows(geo_refs, devices, cols_ref):
    unit = jnp.where(row_ids() == 6, 1.0, 0.0)
    for at, ref in enumerate(geo_refs):

        def fill(first):
            local = local_coords(three_rows(ref, first, CHUNK), first, devices[at])
            rows = [block + pltpu.roll(block, 3, 0) + unit for block in local]
            cols_ref[pl.ds(at * CB + first, CHUNK)] = jnp.stack(rows)

        each_chunk(CB, fill, CHUNK)
    cols_ref[len(geo_refs) * CB] = jnp.full((8, TILE), FAR, f32)


def vector_rows(refs, vec_ref, unit, places=None):
    unit = jnp.where(row_ids() == 3, unit, 0.0)
    for at, ref in enumerate(refs):

        def fill(first):
            rows = []
            for block in three_rows(ref, first, 2 * CHUNK):
                high, low = split(block)
                rows.append(high + pltpu.roll(low, 4, 0) + unit)
            vec_ref[pl.ds((at if places is None else places[at]) * CB + first, 2 * CHUNK)] = jnp.stack(rows)

        each_chunk(CB, fill, 2 * CHUNK)
    vec_ref[len(refs) * CB] = jnp.zeros((8, TILE), f32)


def row_features(geo_ref, device, first, count):
    row = row_ids()
    middle = (row >= 3) & (row < 6)

    def features(coords):
        norm = jnp.sum(coords * coords, axis=0, keepdims=True)
        full = jnp.where(middle, 1.0, jnp.where(row == 6, norm, -2.0 * coords))
        high, rest = split(full)
        mid, low = split(rest)
        last = jnp.where(row < 3, mid, jnp.where(middle, 1.0, low))
        return [high, high, mid, last]

    blocks = local_coords(three_rows(geo_ref, first, count), first, device)
    parts = [features(block) for block in blocks]
    return [
        jnp.transpose(jnp.concatenate(sum(parts[k : k + 4], []), axis=0).astype(bf16)) for k in range(0, count, 4)
    ]


def spread(turned, rows_ref, first):
    for j in range(4):
        rows_ref[first + j] = turned if j == 0 else pltpu.roll(turned, TILE - j * PART, 1)


def tile_loop(groups, listed, rows_ref, cols_ref, table_ref, dist_ref, tile_ref, use, ahead=None, keep=None):
    row = row_ids()
    squares = (row >= 3) & (row < 6)
    unit = row == 6
    dist_ref[...] = jnp.full_like(dist_ref, FAR)
    tile_ref[...] = jnp.zeros_like(tile_ref)

    def distances(slot):
        packed = listed[slot]
        moved = cols_ref[(packed >> 8) & 2047] + table_ref[packed >> 19]
        full = jnp.where(squares, moved * moved, moved)
        high, rest = split(full)
        mid, low = split(rest)
        last = jnp.where(squares, low, jnp.where(unit, 1.0, mid))
        features = jnp.concatenate([high, mid, high, last], axis=0).astype(bf16)
        return jnp.dot(rows_ref[packed & 255][:, :PART], features, preferred_element_type=f32)

    def phi(dist_sq):
        dist_sq = jnp.maximum(dist_sq, 1e-12)
        gap = jnp.maximum(0.5 - dist_sq * lax.rsqrt(dist_sq), 0.0)
        gap_sq = gap * gap
        return gap_sq * gap_sq * (0.625 - gap)

    if keep is not None:
        stage_ref, sems, home = keep

    def copy_out(group):
        slot = lax.rem(group, RING)
        return pltpu.make_async_copy(stage_ref.at[pl.ds(slot, 1)], home(group), sems.at[slot])

    def step(at, carry):
        used = jnp.maximum(at - 2, 0) * GROUP
        first = jnp.minimum(at, groups - 1) * GROUP
        if keep is not None:
            stage = lax.rem(at + RING - 1, RING)
            before = at - 1 - RING

            @pl.when(before >= 0)
            def _():
                copy_out(before).wait()

        found = []
        for k in range(0, GROUP, 2):
            found += use(used, k, (tile_ref[k], tile_ref[k + 1]))
            for j in (k, k + 1):
                tile = phi(dist_ref[j]).astype(tile_ref.dtype)
                tile_ref[j] = tile
                if keep is not None:
                    stage_ref[stage, j] = tile
            for j in (k, k + 1):
                dist_ref[j] = distances(first + j)
        for out, block, value in found:
            out[block] += value
        if ahead is not None:
            ahead(jnp.minimum(at + 1, groups - 1) * GROUP)
        if keep is not None:

            @pl.when((at > 0) & (at <= groups))
            def _():
                copy_out(at - 1).start()

        return carry

    lax.fori_loop(0, jnp.where(groups > 0, groups + 2, 0), step, 0)
    if keep is not None:
        for back in range(1, RING):
            group = groups - back

            @pl.when(group >= 0)
            def _():
                copy_out(group).wait()


def stream(diag_tiles, pair_tiles, pairs, stage_ref, sems):
    ring = stage_ref.shape[0]
    diag_pairs = DIAG_GROUPS // 2
    total = diag_pairs + pairs

    def copy_in(tiles, at, slot):
        return pltpu.make_async_copy(tiles.at[pl.ds(2 * at, 2)], stage_ref.at[slot], sems.at[slot])

    def start(at):
        slot = lax.rem(at, ring)

        @pl.when(at < diag_pairs)
        def _():
            copy_in(diag_tiles, at, slot).start()

        @pl.when((at >= diag_pairs) & (at < total))
        def _():
            copy_in(pair_tiles, at - diag_pairs, slot).start()

    for at in range(ring - 1):
        start(jnp.int32(at))

    def loop(first, count, use):
        def step(at, carry):
            here = first + at
            start(here + ring - 1)
            slot = lax.rem(here, ring)
            copy_in(diag_tiles, 0, slot).wait()
            found = []
            for k in range(0, 2 * GROUP, 2):
                part, tile = k // GROUP, k % GROUP
                found += use(2 * at * GROUP, k, (stage_ref[slot, part, tile], stage_ref[slot, part, tile + 1]))
            for out, block, value in found:
                out[block] += value
            return carry

        lax.fori_loop(0, count, step, 0)

    return loop


def pair_body(step, me, groups, diag_list, pair_list, *refs):
    row = row_ids()

    def own(geo_ref, rows_ref, first):
        for k, turned in enumerate(row_features(geo_ref, me[0], first, GROUP)):
            spread(turned, rows_ref, first + 4 * k)

    if step == "diag":
        own_vec, own_geo, table_ref, own_out, diag_tiles = refs[:5]
        vec_ref, row_sum, col_sum, stage_ref, sems, rows_ref, cols_ref, dist_ref, tile_ref = refs[5:]
        column_rows((own_geo,), (me[0],), cols_ref)
        vector_rows((own_vec,), vec_ref, 1.0)
    elif step == "pairs":
        own_vec, right_vec, own_geo, right_geo, table_ref, stiff_ref, diag_ref = refs[:7]
        own_out, right_out, pair_tiles = refs[7:10]
        vec_ref, row_sum, col_sum, stage_ref, sems, rows_ref, cols_ref, dist_ref, tile_ref = refs[10:]
        column_rows((own_geo, right_geo), (me[0], me[0] + 1), cols_ref)
        vector_rows((own_vec, right_vec), vec_ref, 1.0)
    else:
        own_vec, right_vec, diag_tiles, pair_tiles, *outs, vec_ref, row_sum, col_sum, stage_ref, sems = refs
        pairs = lax.div(groups[0], 2)
        loop = stream(diag_tiles, pair_tiles, pairs, stage_ref, sems)
        vector_rows((own_vec, right_vec), vec_ref, 1.0)
    row_sum[...] = jnp.zeros_like(row_sum)
    col_sum[...] = jnp.zeros_like(col_sum)

    def two(first, second):
        return jnp.concatenate([first, second], axis=0).astype(bf16)

    def use_diag(first, k, pair):
        a, b = diag_list[first + k] & 255, diag_list[first + k + 1] & 255
        left = two(jnp.where(row == 3, 0.0, vec_ref[a]), jnp.where(row == 3, 0.0, vec_ref[b]))
        image = jnp.dot(
            left, jnp.concatenate(pair, axis=1), preferred_element_type=f32
        )
        return [(col_sum, a, image[:8, :TILE]), (col_sum, b, image[8:, TILE:])]

    def use_pair(first, k, pair):
        p, q = pair_list[first + k], pair_list[first + k + 1]
        row_a, col_a = p & 255, (p >> 8) & 2047
        row_b, col_b = q & 255, (q >> 8) & 2047
        left = two(vec_ref[row_a], vec_ref[row_b])
        if step == 2:
            left = left * 2
        image = jnp.dot(left, jnp.concatenate(pair, axis=1), preferred_element_type=f32)
        found = [(col_sum, col_a, image[:8, :TILE]), (col_sum, col_b, image[8:, TILE:])]
        if step != 2:
            image = lax.dot_general(
                two(vec_ref[col_a], vec_ref[col_b]),
                jnp.concatenate(pair, axis=0),
                (((1,), (1,)), ((), ())),
                preferred_element_type=f32,
            )
            found += [(row_sum, row_a, image[:8, :TILE]), (row_sum, row_b, image[8:, TILE:])]
        return found

    def diag_home(group, count=1):
        return diag_tiles.at[pl.ds(group, count)]

    def pair_home(group, count=1):
        return pair_tiles.at[pl.ds(group, count)]

    if step in ("diag", "pairs"):
        loop = functools.partial(
            tile_loop, rows_ref=rows_ref, cols_ref=cols_ref, table_ref=table_ref, dist_ref=dist_ref, tile_ref=tile_ref
        )

        def features(at, carry):
            own(own_geo, rows_ref=rows_ref, first=at * GROUP)
            return carry

        if step == "diag":
            features(jnp.int32(0), 0)
            loop(
                jnp.int32(DIAG_GROUPS),
                diag_list,
                use=use_diag,
                ahead=lambda first: own(own_geo, rows_ref=rows_ref, first=first),
                keep=(stage_ref, sems, diag_home),
            )
        else:
            lax.fori_loop(0, DIAG_GROUPS, features, 0)
            loop(groups[0], pair_list, use=use_pair, keep=(stage_ref, sems, pair_home))
    else:
        loop(0, DIAG_GROUPS // 2, use_diag)
        loop(DIAG_GROUPS // 2, pairs, use_pair)

    def fold(value):
        return value + pltpu.roll(value, 4, 0)

    if step != 2:
        if step == "diag":
            images = (own_out,)
        else:
            images = (own_out, right_out) if step == "pairs" else outs

        def finish(first):
            place = pl.ds(pl.multiple_of(first * TILE, 8 * TILE), 8 * TILE)
            sums = row_sum[pl.ds(first, 8)] + col_sum[pl.ds(first, 8)]
            image = jnp.concatenate([fold(sums[k])[:4] for k in range(8)], axis=1)
            if step == "pairs":
                fourth = lax.broadcasted_iota(i32, image.shape, 0) == 3
                image = image + diag_ref[:, place] + jnp.where(fourth, stiff_ref[:, place] - SHIFT, 0.0)
            images[0][:, place] = image
            if step != "diag":
                sums = col_sum[pl.ds(CB + first, 8)]
                images[1][:, place] = jnp.concatenate([fold(sums[k])[:4] for k in range(8)], axis=1)

        each_chunk(CB, finish)
    else:
        quad_out = outs[0]

        def finish(at, sums):
            return tuple(
                total + fold(col_sum[8 * at + k]) * fold(vec_ref[8 * at + k]) for k, total in enumerate(sums)
            )

        zero = jnp.zeros((8, TILE), f32)
        sums = lax.fori_loop(0, 2 * CB // 8, finish, (zero,) * 8)
        quad_out[...] = sum(sums)


def pair_call(step, *arrays, me, groups, diag_list, pair_list):
    smem = pl.BlockSpec(memory_space=pltpu.SMEM)
    vmem = pl.BlockSpec(memory_space=pltpu.VMEM)
    some = pl.BlockSpec(memory_space=pl.ANY)
    image = (jax.ShapeDtypeStruct((4, CB * TILE), f32), vmem)
    out = {
        "diag": (image, (jax.ShapeDtypeStruct((DIAG_GROUPS, GROUP, TILE, TILE), bf16), some)),
        "pairs": (image, image, (jax.ShapeDtypeStruct((PAIR_GROUPS, GROUP, TILE, TILE), bf16), some)),
        1: (image, image),
        2: ((jax.ShapeDtypeStruct((8, TILE), f32), vmem),),
    }[step]
    first = step in ("diag", "pairs")
    blocks = (1 if step == "diag" else 2) * CB + 1
    scratch = [
        pltpu.VMEM((blocks, 8, TILE), f32),
        pltpu.VMEM((CB, 8, TILE), f32),
        pltpu.VMEM((blocks, 8, TILE), f32),
        pltpu.VMEM((RING, GROUP, TILE, TILE) if first else (RING // 2, 2, GROUP, TILE, TILE), bf16),
        pltpu.SemaphoreType.DMA((RING,)),
    ]
    if first:
        scratch += [
            pltpu.VMEM((CB, TILE, TILE), bf16),
            pltpu.VMEM((blocks, 8, TILE), f32),
            pltpu.VMEM((GROUP, TILE, TILE), f32),
            pltpu.VMEM((GROUP, TILE, TILE), bf16),
        ]
    return pl.pallas_call(
        functools.partial(pair_body, step),
        out_shape=tuple(shape for shape, _ in out),
        in_specs=[smem] * 4 + ([vmem] * len(arrays) if first else [vmem, vmem, some, some]),
        out_specs=tuple(spec for _, spec in out),
        scratch_shapes=scratch,
        compiler_params=pltpu.CompilerParams(vmem_limit_bytes=48 * 2**20),
        cost_estimate=pl.CostEstimate(flops=2 * 10**9, bytes_accessed=10**8, transcendentals=0),
        name=f"pair_tiles_{step}",
    )(me, groups, diag_list, pair_list, *arrays)


def volume_body(me, groups, vol_list, vol_geo, *refs):
    geos, coefs = refs[:5], refs[5:10]
    table_ref, out, rows_ref, cols_ref, coef_ref, sums, dist_ref, tile_ref = refs[10:]
    column_rows(geos, [me[0] + k for k in range(-2, 3)], cols_ref)
    odd = lax.rem(me[0], 2)
    vector_rows(coefs, coef_ref, 0.0, [jnp.where(odd == 1, 4 - k, k) for k in range(5)])
    sums[...] = jnp.zeros_like(sums)

    def features(at, carry):
        for k, turned in enumerate(row_features(vol_geo, me[0], 16 * at, 16)):
            spread(turned, rows_ref, 16 * at + 4 * k)
        return carry

    lax.fori_loop(0, VB // 16, features, 0)

    def use(first, k, pair):
        dims = (((1,), (1,)), ((), ()))
        p, q = vol_list[first + k], vol_list[first + k + 1]
        left = jnp.concatenate([coef_ref[(p >> 8) & 2047], coef_ref[(q >> 8) & 2047]], axis=0).astype(bf16)
        highs, lows = [], []
        for tile in pair:
            high = tile.astype(bf16)
            highs.append(high)
            lows.append((tile - high.astype(f32)).astype(bf16))
        image = lax.dot_general(left, jnp.concatenate(highs, axis=0), dims, preferred_element_type=f32)
        image += lax.dot_general(left, jnp.concatenate(lows, axis=0), dims, preferred_element_type=f32)
        return [(sums, p & 255, image[:8, :TILE]), (sums, q & 255, image[8:, TILE:])]

    tile_loop(groups[0], vol_list, rows_ref, cols_ref, table_ref, dist_ref, tile_ref, use)

    def finish(first):
        value = sums[pl.ds(first, 8)]
        rows = [(value[k] + pltpu.roll(value[k], 4, 0))[:3] for k in range(8)]
        out[:, pl.ds(pl.multiple_of(first * TILE, 8 * TILE), 8 * TILE)] = jnp.concatenate(rows, axis=1) * TILE**0.5

    each_chunk(VB, finish)


def volume_call(me, groups, vol_list, *arrays):
    smem = pl.BlockSpec(memory_space=pltpu.SMEM)
    vmem = pl.BlockSpec(memory_space=pltpu.VMEM)
    return pl.pallas_call(
        volume_body,
        out_shape=jax.ShapeDtypeStruct((3, VB * TILE), f32),
        in_specs=[smem] * 3 + [vmem] * len(arrays),
        out_specs=vmem,
        scratch_shapes=[
            pltpu.VMEM((VB, TILE, TILE), bf16),
            pltpu.VMEM((5 * CB + 1, 8, TILE), f32),
            pltpu.VMEM((5 * CB + 1, 8, TILE), f32),
            pltpu.VMEM((VB, 8, TILE), f32),
            pltpu.VMEM((GROUP, TILE, TILE), f32),
            pltpu.VMEM((GROUP, TILE, TILE), f32),
        ],
        compiler_params=pltpu.CompilerParams(vmem_limit_bytes=56 * 2**20),
        cost_estimate=pl.CostEstimate(flops=2 * 10**9, bytes_accessed=10**8, transcendentals=0),
        name="volume_tiles",
    )(me, groups, vol_list, *arrays)


def cg_weights(moment):
    def gram(first, second):
        return sum(a * b * moment[i + j] for i, a in enumerate(first) for j, b in enumerate(second))

    def image(vector):
        grown = [SHIFT * a for a in vector] + [0.0]
        return [a + (vector[k - 1] if k else 0.0) for k, a in enumerate(grown)]

    def axpy(scale, first, second):
        size = max(len(first), len(second))
        pad = lambda v: list(v) + [0.0] * (size - len(v))
        return [scale * a + b for a, b in zip(pad(first), pad(second))]

    one = jnp.ones_like(moment[0])
    residual, direction, total = [one], [one], [0.0 * one]
    norm = gram(residual, residual)
    for step in range(3):
        grown = image(direction)
        length = norm / gram(direction, grown)
        total = axpy(length, direction, total)
        if step < 2:
            residual = axpy(-length, grown, residual)
            norm_next = gram(residual, residual)
            direction = axpy(norm_next / norm, direction, residual)
            norm = norm_next
    return total


def comp_sum(first, second):
    return jnp.sum(first * second, axis=1)


def body(ctrl_points, ctrl_disp, stiffness, pair_rows, pair_cols, pair_count, vol_points, vol_rows, vol_cols, vol_count):
    me = lax.axis_index("nodes")
    devices = lax.axis_size("nodes")
    order = (2, 1, 0, -1, -2)

    geo = {0: ctrl_points, -1: from_behind(ctrl_points, "nodes", -1)}
    beside = from_behind(ctrl_disp, "nodes", -1)
    table = offset_table()

    slots = lax.iota(i32, MAXT)
    right = pair_cols >= CB
    live = (slots < pair_count[0]) & (~right | (me < devices - 1))
    code = offset_code(right.astype(i32), pair_rows, pair_cols % CB)
    pair_list = jnp.where(live, pair_rows | (pair_cols << 8) | (code << 19), (2 * CB) << 8)
    pair_groups = (pair_count + 2 * GROUP - 1) // (2 * GROUP) * 2
    own = lax.iota(i32, CB)
    diag_list = own | (own << 8) | (62 << 19)

    slots = lax.iota(i32, MAXV)
    step_x = vol_cols // CB - 2
    source = me + step_x
    live = (slots < vol_count[0]) & (source >= 0) & (source < devices)
    code = offset_code(step_x, vol_rows, vol_cols % CB)
    vol_list = jnp.where(live, vol_rows | (vol_cols << 8) | (code << 19), (5 * CB) << 8)
    vol_groups = (vol_count + GROUP - 1) // GROUP
    here = me.astype(i32)[None]

    images = functools.partial(pair_call, me=here, groups=pair_groups, diag_list=diag_list, pair_list=pair_list)

    def exchanged(own_part, right_part):
        back = from_behind(right_part, "nodes", 1)
        ahead = from_behind(own_part, "nodes", -1)
        return own_part + back, ahead + right_part

    own_part, diag_tiles = images("diag", ctrl_disp, ctrl_points, table)
    own_part, right_part, pair_tiles = images(
        "pairs", ctrl_disp, beside, ctrl_points, geo[-1], table, stiffness[None, :], own_part
    )
    tiles = (diag_tiles, pair_tiles)
    total, total_beside = exchanged(own_part, right_part)
    diagonal, diagonal_beside = total[3:4], total_beside[3:4]
    first = total[:3] + diagonal * ctrl_disp
    first_beside = total_beside[:3] + diagonal_beside * beside
    later, first = lax.optimization_barrier((ctrl_points, first))
    for offset in (1, 2, -2):
        geo[offset] = from_behind(later, "nodes", offset)
    own_part, right_part = images(1, first, first_beside, *tiles)
    own_part, right_part, geo[1], geo[2], geo[-2] = lax.optimization_barrier(
        (own_part, right_part, geo[1], geo[2], geo[-2])
    )
    total, total_beside = exchanged(own_part, right_part)
    second = total[:3] + diagonal * first
    second_beside = total_beside[:3] + diagonal_beside * first_beside
    (quad,) = images(2, second, second_beside, *tiles)
    moments = jnp.concatenate(
        [
            comp_sum(ctrl_disp, ctrl_disp),
            comp_sum(ctrl_disp, first),
            comp_sum(first, first),
            comp_sum(first, second),
            comp_sum(second, second),
            jnp.sum(quad, axis=1)[:3] + comp_sum(diagonal * second, second),
            jnp.zeros((TILE - 18,), f32),
        ]
    )

    sent = jnp.broadcast_to(moments[None, None, :], (devices, 1, TILE))
    moments = jnp.sum(lax.all_to_all(sent, "nodes", 0, 0, tiled=True), axis=(0, 1))
    weights = cg_weights([moments[3 * k : 3 * k + 3] for k in range(6)])
    coef = sum(w[:, None] * u for w, u in zip(weights, (ctrl_disp, first, second)))
    near = around(coef, "nodes")
    moved = volume_call(here, vol_groups, vol_list, vol_points, *[geo[k] for k in order], *near, table)
    return (coef, moved)


def solution(mesh):
    across = P(None, "nodes")
    flat = P("nodes")
    return jax.shard_map(
        body,
        mesh=mesh,
        in_specs=(across, across, flat, flat, flat, flat, across, flat, flat, flat),
        out_specs=(across, across),
        check_vma=False,
    )
```
